128 devices in a mesh: row: 8 (over x, y_hi), col: 16 (over y_lo, z, core).
Axes of the slice: x: 4, y: 4 (y_hi: 2, y_lo: 2; y = y_hi * 2 + y_lo), z: 4, core: 2. Of those that a mesh axis runs over, the one named last changes fastest.
Arguments:
- pair_map: bfloat16 [64, 2048, 2048], P(None, 'row', 'col'), may hold values from -6 to 6
- features: bfloat16 [2048, 256], P(('row', 'col')), may hold values from -6 to 6
- left_weight: bfloat16 [256, 32], replicated, may hold values from -0.375 to 0.375
- right_weight: bfloat16 [256, 32], replicated, may hold values from -0.375 to 0.375
- outer_weight: bfloat16 [32, 32, 64], replicated, may hold values from -0.1875 to 0.1875
- conv_weight: bfloat16 [3, 3, 64, 64], replicated, may hold values from -0.25 to 0.25
- conv_bias: float32 [64], replicated, may hold values from -4 to 4
- cotangent: bfloat16 [64, 2048, 2048], P(None, 'row', 'col'), may hold values from -6 to 6
Outputs:
- pair_out: bfloat16 [64, 2048, 2048], P(None, 'row', 'col')
- pair_grad: bfloat16 [64, 2048, 2048], P(None, 'row', 'col')
- weight_grad: float32 [3, 3, 64, 64], replicated
- feature_grad: float32 [2048, 256], P(('row', 'col'))
The draws below stay inside these ranges and needn't reach their ends.
All inputs are finite; a program needn't handle non-finite values.
Results may differ from the reference program's by a relative error of at most 0.0059.
Values may be sent and summed in bfloat16 or wider, within the bound.
A program may use at most 320 MiB of HBM per device.

```python
import math
import jax
import jax.numpy as jnp
from jax import lax

C = 64
FEAT = 256
OUTER = 32
L = 2048


def steps_of(own_key, shape, split, least, largest):
    loudness = 1.0
    for axis_at, blocks in split:
        draws = jax.random.uniform(jax.random.fold_in(jax.random.fold_in(own_key, 6), axis_at), (blocks,), jnp.float32, least / len(split), largest / len(split))
        loudness = loudness * jnp.repeat(jnp.exp(draws), shape[axis_at] // blocks).reshape((-1,) + (1,) * (len(shape) - 1 - axis_at))
    return loudness


def gaussian(stream_key, extent, width, most, cuts=(), dtype=jnp.bfloat16):
    values = width * jax.random.normal(stream_key, extent, jnp.float32)
    if cuts:
        values = values * steps_of(stream_key, extent, cuts, -0.22, 0.18)
    return jnp.clip(values, -most, most).astype(dtype)


def setup_inputs(seed: int = 0) -> dict:
    splits = jax.random.split(jax.random.key(seed), 9)
    pair_map = gaussian(splits[0], (C, L, L), 1.0, 6.0, ((1, 8), (2, 16)))
    features = gaussian(splits[1], (L, FEAT), 1.0, 6.0, ((0, 128),))
    left_weight = gaussian(splits[2], (FEAT, OUTER), FEAT ** -0.5, 0.375)
    right_weight = gaussian(splits[3], (FEAT, OUTER), FEAT ** -0.5, 0.375)
    outer_weight = gaussian(splits[4], (OUTER, OUTER, C), (OUTER * OUTER) ** -0.5, 0.1875)
    conv_weight = gaussian(splits[5], (3, 3, C, C), (9 * C) ** -0.5, 0.25)
    conv_bias = gaussian(splits[6], (C,), 1.0, 4.0, (), jnp.float32)
    cotangent = gaussian(splits[7], (C, L, L), 1.0, 6.0, ((1, 8), (2, 16)))
    return dict(pair_map=pair_map, features=features, left_weight=left_weight, right_weight=right_weight, outer_weight=outer_weight, conv_weight=conv_weight, conv_bias=conv_bias, cotangent=cotangent)


REACH = 4

def tap_product(weight_tap, window):
    channel_count, height, breadth = window.shape
    flattened = window.reshape(channel_count, height * breadth)
    result = jnp.dot(weight_tap, flattened, preferred_element_type=jnp.float32)
    return result.reshape(weight_tap.shape[0], height, breadth)

def tap_outer(grad_flat, window):
    flattened = window.reshape(window.shape[0], -1)
    return lax.dot_general(grad_flat, flattened, (((1,), (1,)), ((), ())), preferred_element_type=jnp.float32)

def reference(pair_map, features, left_weight, right_weight, outer_weight, conv_weight, conv_bias, cotangent):
    highest = lax.Precision.HIGHEST
    channels, residues, _ = pair_map.shape
    left_rows = jnp.dot(features, left_weight, preferred_element_type=jnp.float32).astype(jnp.bfloat16)
    right_rows = jnp.dot(features, right_weight, preferred_element_type=jnp.float32).astype(jnp.bfloat16)
    mixing = jnp.einsum('pqc,jq->pcj', outer_weight.astype(jnp.float32), right_rows.astype(jnp.float32), precision=highest).astype(jnp.bfloat16)
    update = jnp.einsum('ip,pcj->cij', left_rows.astype(jnp.float32), mixing.astype(jnp.float32), precision=highest)
    hidden = lax.optimization_barrier((pair_map.astype(jnp.float32) + update).astype(jnp.bfloat16))
    hidden_wide = hidden.astype(jnp.float32)
    activated = jax.nn.elu(hidden_wide).astype(jnp.bfloat16)
    padding = ((0, 0), (REACH, REACH), (REACH, REACH))
    act_padded = jnp.pad(activated, padding)
    cot_padded = jnp.pad(cotangent, padding)
    cot_flat = cotangent.reshape(channels, -1)
    conv_total = jnp.zeros((channels, residues, residues), jnp.float32)
    input_grad = jnp.zeros((channels, residues, residues), jnp.float32)
    tap_rows = []
    for row_tap in range(3):
        row_grads = []
        for col_tap in range(3):
            window = act_padded[:, REACH * row_tap:REACH * row_tap + residues, REACH * col_tap:REACH * col_tap + residues]
            conv_total = conv_total + tap_product(conv_weight[row_tap, col_tap], window)
            row_grads.append(tap_outer(cot_flat, window))
            back_window = cot_padded[:, REACH * (2 - row_tap):REACH * (2 - row_tap) + residues, REACH * (2 - col_tap):REACH * (2 - col_tap) + residues]
            input_grad = input_grad + tap_product(conv_weight[row_tap, col_tap].T, back_window)
        tap_rows.append(jnp.stack(row_grads))
    pair_out = (hidden_wide + conv_bias[:, None, None] + conv_total).astype(jnp.bfloat16)
    slope = jnp.where(hidden_wide > 0, 1.0, jnp.exp(jnp.minimum(hidden_wide, 0.0)))
    pair_grad = (cotangent.astype(jnp.float32) + input_grad * slope).astype(jnp.bfloat16)
    weight_grad = jnp.stack(tap_rows) / residues
    grad_wide = pair_grad.astype(jnp.float32)
    left_grad = jnp.einsum('cij,pcj->ip', grad_wide, mixing.astype(jnp.float32), precision=highest)
    mixing_grad = jnp.einsum('ip,cij->pcj', left_rows.astype(jnp.float32), grad_wide, precision=highest)
    right_grad = jnp.einsum('pqc,pcj->jq', outer_weight.astype(jnp.float32), mixing_grad, precision=highest)
    feature_grad = (jnp.dot(left_grad, left_weight.T.astype(jnp.float32), precision=highest, preferred_element_type=jnp.float32) + jnp.dot(right_grad, right_weight.T.astype(jnp.float32), precision=highest, preferred_element_type=jnp.float32)) / math.sqrt(residues)
    return (pair_out, pair_grad, weight_grad, feature_grad)
```

```python
import functools
import math

import jax
import jax.numpy as jnp
import numpy as np
from jax import lax
from jax.experimental import pallas as pl
from jax.experimental.pallas import tpu as pltpu
from jax.sharding import PartitionSpec as P

MESH = pl.DeviceIdType.MESH
BF = jnp.bfloat16
F32 = jnp.float32
NT = (((1,), (1,)), ((), ()))
PACK = 32


def edge_selector():
    tile = np.zeros((PACK // 2, 2, PACK, 4, 2, 128), np.float32)
    for t in range(PACK // 2):
        for r in range(2):
            for q in range(4):
                tile[t, 0, 2 * t + r, q, r, q] = 1
                tile[t, 1, 2 * t + r, q, r, 124 + q] = 1
    return tile.reshape(PACK // 2 * 256, 256)


def dot(a, b, dims=None):
    if dims is None:
        return jnp.dot(a, b, preferred_element_type=F32)
    return lax.dot_general(a, b, dims, preferred_element_type=F32)


def kernel(
    nr, nc, ch, ti, outer, comm, residues,
    cot_hbm, pm_hbm, sel_hbm, bias, feat, lw, rw, ow, cw,
    po_hbm, pg_hbm, wg_out, fg_out,
    cot_n, hid_n, wide, gt, cot_t, act_t, hx, hb, sel,
    pack_acc, packs, land_row, land_col,
    lr, left_in, right_in, left, left_t, mixf, mix, wf, wb, ow_q, mgf,
    wg_acc, wgs, land_a, land_b, fin, lg_acc, lg_out, rg_out, land_l, land_r,
    in_sem, out_sem, f_send, f_recv, h_send, h_recv, w_send, w_recv, g_send, g_recv,
):
    row = lax.axis_index("row")
    col = lax.axis_index("col")
    kg = ti // PACK
    ng = ti // 4
    pitch = ti + 8
    own = lr.shape[0]
    flat = row * nc + col
    goal = flat // nr
    slot = lax.rem(flat, nr)
    up, down = lax.rem(row + nr - 1, nr), lax.rem(row + 1, nr)
    west, east = lax.rem(col + nc - 1, nc), lax.rem(col + 1, nc)
    cstep = 8
    nchunk = ch // cstep

    cot_in = [
        pltpu.make_async_copy(
            cot_hbm.at[pl.ds(k * cstep, cstep)], cot_n.at[pl.ds(k * cstep, cstep)], in_sem.at[k]
        )
        for k in range(nchunk)
    ]
    pm_in = pltpu.make_async_copy(pm_hbm, hid_n, in_sem.at[nchunk])
    sel_in = pltpu.make_async_copy(sel_hbm, sel, in_sem.at[nchunk + 1])
    for copy in cot_in:
        copy.start()
    sel_in.start()
    pm_in.start()

    def source(k):
        f = col * nr + k
        return f // nc, lax.rem(f, nc)

    if comm:
        barrier = pltpu.get_barrier_semaphore()

        def greet(r, c):
            pl.semaphore_signal(barrier, inc=1, device_id=(r, c), device_id_type=MESH)

        def greet_unless_me(r, c):
            @pl.when(jnp.logical_or(r != row, c != col))
            def _():
                greet(r, c)

        for d in range(1, nc):
            greet(row, lax.rem(col + d, nc))
        for d in range(1, nr):
            greet(lax.rem(row + d, nr), col)
        for r in (up, down):
            for c in (west, east):
                greet(r, c)
        for k in range(nr):
            greet_unless_me(k, goal)
            greet_unless_me(*source(k))
        total_greets = (nc - 1) + (nr - 1) + 4 + 2 * nr - jnp.where(goal == col, 2, 0)

    lr[...] = jnp.concatenate(
        [dot(feat[...], lw[...]), dot(feat[...], rw[...]), jnp.zeros((own, 128 - 2 * outer), F32)],
        axis=1,
    ).astype(BF)

    def remote(src, dst, ssem, rsem, dev):
        return pltpu.make_async_remote_copy(
            src_ref=src, dst_ref=dst, send_sem=ssem, recv_sem=rsem, device_id=dev, device_id_type=MESH
        )

    left_in[col] = lr[...]
    left_moves, right_moves = [], []
    if comm:
        pl.semaphore_wait(barrier, total_greets)
        for d in range(1, nc):
            move = remote(
                lr, left_in.at[col], f_send.at[d], f_recv.at[d], (row, lax.rem(col + d, nc))
            )
            move.start()
            left_moves.append(move)
        for k in range(nr):
            me = jnp.logical_and(row == k, goal == col)
            far = remote(
                lr, right_in.at[slot], f_send.at[nc + k], f_recv.at[nc + slot], (k, goal)
            )
            near = pltpu.make_async_copy(lr, right_in.at[slot], f_recv.at[nc + slot])

            @pl.when(me)
            def _():
                near.start()

            @pl.when(jnp.logical_not(me))
            def _():
                far.start()

            right_moves.append((me, far))

    for a in range(3):
        wf[a * ch : (a + 1) * ch, :] = jnp.concatenate([cw[3 * a + b] for b in range(3)], axis=1)
        wb[a * ch : (a + 1) * ch, :] = jnp.concatenate(
            [cw[3 * a + b].astype(F32).T for b in range(3)], axis=1
        ).astype(BF)
    ow_q[...] = jnp.concatenate([ow[p] for p in range(outer)], axis=1)

    for k in range(nchunk):
        cot_in[k].wait()

        @pl.loop(0, cstep)
        def _(c):
            at = pl.multiple_of((k * cstep + c) * pitch, 8)
            wide[pl.ds(at, ti), :] = cot_n[k * cstep + c].astype(F32)

    def to_rows(dst, first):
        @pl.loop(0, ti, unroll=8)
        def _(i):
            dst[first + i] = wide[pl.ds(i, ch, stride=pitch), :].astype(BF)

    to_rows(cot_t, 4)
    sel_in.wait()

    def pack_edges(src, first, which):
        pack_acc[...] = jnp.zeros_like(pack_acc)

        @pl.loop(0, PACK // 2)
        def _(t):
            rows = jnp.concatenate(
                [
                    jnp.concatenate(
                        [src[first + PACK * k + 2 * t], src[first + PACK * k + 2 * t + 1]], axis=1
                    )
                    for k in range(kg)
                ],
                axis=0,
            )
            tile = sel[pl.ds(pl.multiple_of(t * 256, 256), 256), :]
            pack_acc[...] += dot(rows, tile, NT)

        for side in range(2):
            packs[which, side] = (
                pack_acc[:, 128 * side : 128 * (side + 1)].astype(BF).reshape(kg, ch, 128)
            )

    def halo_moves(src, first, which):
        low, high = packs.at[which, 0], packs.at[which, 1]
        from_west, from_east = land_col.at[which, 0], land_col.at[which, 1]
        plan = [
            (src.at[pl.ds(first, 4)], land_row.at[which, 1], (up, col)),
            (src.at[pl.ds(first + ti - 4, 4)], land_row.at[which, 0], (down, col)),
            (low, from_east.at[pl.ds(1, kg)], (row, west)),
            (high, from_west.at[pl.ds(1, kg)], (row, east)),
            (low.at[0], from_east.at[kg + 1], (up, west)),
            (high.at[0], from_west.at[kg + 1], (up, east)),
            (low.at[kg - 1], from_east.at[0], (down, west)),
            (high.at[kg - 1], from_west.at[0], (down, east)),
        ]
        return [
            remote(s, d, h_send.at[which, m], h_recv.at[which, m], dev)
            for m, (s, d, dev) in enumerate(plan)
        ]

    pack_edges(cot_t, 4, 0)
    cot_moves = halo_moves(cot_t, 4, 0)
    if comm:
        for move in cot_moves:
            move.start()

    if comm:
        for d in range(1, nc):
            left_moves[d - 1].wait_recv()
        for k in range(nr):
            pltpu.make_async_copy(lr, right_in.at[k], f_recv.at[nc + k]).wait()
    left[...] = left_in[...].reshape(nc * own, 128)[:, :outer]
    left_t[...] = left[...].astype(F32).T.astype(BF)
    right = right_in[...].reshape(nr * own, 128)[:, outer : 2 * outer]
    step = 512
    for s in range(outer * ch // step):
        w = ow_q[:, s * step : (s + 1) * step].astype(F32).T.astype(BF)
        mixf[s * step : (s + 1) * step, :] = dot(w, right, NT).astype(BF).astype(F32)

    @pl.loop(0, ch, unroll=4)
    def _(c):
        mix[c] = mixf[pl.ds(c, outer, stride=ch), :].astype(BF)

    pm_in.wait()

    @pl.loop(0, ch, step=2)
    def _(c):
        both = jnp.concatenate([mix[c], mix[c + 1]], axis=1)
        update = dot(left[...], both)
        for k in range(2):
            hidden = (hid_n[c + k].astype(F32) + update[:, 128 * k : 128 * (k + 1)]).astype(BF)
            hid_n[c + k] = hidden
            h = hidden.astype(F32)
            at = pl.multiple_of((c + k) * pitch, 8)
            wide[pl.ds(at, ti), :] = jnp.where(h > 0, h, jnp.exp(jnp.minimum(h, 0.0)) - 1.0)

    to_rows(act_t, 8)
    for s in (0, 4, ti + 8, ti + 12):
        act_t[s : s + 4] = jnp.zeros((4, ch, 128), BF)
    pack_edges(act_t, 8, 1)
    act_moves = halo_moves(act_t, 8, 1)
    if comm:
        for move in act_moves:
            move.start()

    has_up, has_down, has_west, has_east = row > 0, row < nr - 1, col > 0, col < nc - 1

    def keep(ok, x):
        return jnp.where(ok, x, jnp.zeros_like(x))

    def unpack_edges(dst, first, which):
        dst[first : first + 4] = keep(has_up, land_row[which, 0])
        dst[first + ti + 4 : first + ti + 8] = keep(has_down, land_row[which, 1])
        for side, ok in ((0, has_west), (1, has_east)):
            lanes = slice(128 * side, 128 * (side + 1))
            hb[:ch, lanes] = keep(jnp.logical_and(ok, has_up), land_col[which, side, 0])
            for k in range(1, kg + 1):
                hb[k * ch : (k + 1) * ch, lanes] = keep(ok, land_col[which, side, k])
            hb[(kg + 1) * ch :, lanes] = keep(
                jnp.logical_and(ok, has_down), land_col[which, side, kg + 1]
            )

        @pl.loop(0, PACK // 2)
        def _(t):
            tile = sel[pl.ds(pl.multiple_of(t * 256, 256), 256), :]
            out = dot(hb[...], tile).astype(BF)
            for k in range(kg + 2):
                for r in range(2):
                    hx[PACK * k + 2 * t + r] = out[k * ch : (k + 1) * ch, 128 * r : 128 * (r + 1)]

    lane = lax.broadcasted_iota(jnp.int32, (ch, 128), 1)

    def stack(src, first, g, turned):
        rows = []
        for r in range(4):
            x = src[first + 4 * g + r]
            edge = hx[PACK - 4 + 4 * g + r]
            before = jnp.where(lane < 4, edge, pltpu.roll(x, 4, 1))
            after = jnp.where(lane >= 124, edge, pltpu.roll(x, 124, 1))
            rows.append(jnp.concatenate([after, x, before] if turned else [before, x, after], axis=0))
        return jnp.concatenate(rows, axis=1)

    def spread(part, g, order):
        for r in range(4):
            lanes = slice(128 * r, 128 * (r + 1))
            for k, a in enumerate(order):
                at = pl.ds(pl.multiple_of((4 * (g + k) + r) * ch, ch), ch)
                term = part[a * ch : (a + 1) * ch, lanes]
                if k < 2:
                    gt[at, :] += term
                else:
                    gt[at, :] = term

    if comm:
        for move in cot_moves:
            move.wait_recv()
    unpack_edges(cot_t, 0, 0)
    gt[: 8 * ch] = jnp.zeros((8 * ch, 128), F32)
    wg_acc[...] = jnp.zeros_like(wg_acc)

    @pl.loop(0, ng + 2)
    def _(g):
        terms = stack(cot_t, 0, g, True)
        spread(dot(wb[...], terms), g, (0, 1, 2))
        acts = jnp.concatenate(
            [
                jnp.concatenate([act_t[4 * (g + a) + r] for r in range(4)], axis=1)
                for a in range(3)
            ],
            axis=0,
        )
        wg_acc[...] += dot(terms, acts, NT)

    part = 2 * 3 * ch // nc
    wgs[: 3 * ch] = wg_acc[:, :128]
    wgs[3 * ch :] = jnp.concatenate([wg_acc[:, 128:], jnp.zeros((3 * ch, 256 - 3 * ch), F32)], axis=1)
    land_a[col] = wgs[pl.ds(pl.multiple_of(col * part, 8), part)]
    a_moves, b_moves, c_moves, l_moves, r_moves = [], [], [], [], []
    if comm:
        for d in range(1, nc):
            other = lax.rem(col + d, nc)
            move = remote(
                wgs.at[pl.ds(pl.multiple_of(other * part, 8), part)],
                land_a.at[col], w_send.at[d], w_recv.at[d], (row, other),
            )
            move.start()
            a_moves.append(move)

    lg_acc[...] = jnp.zeros_like(lg_acc)
    pg_out = [
        pltpu.make_async_copy(
            cot_n.at[pl.ds(k * cstep, cstep)], pg_hbm.at[pl.ds(k * cstep, cstep)], out_sem.at[k]
        )
        for k in range(nchunk)
    ]
    for k in range(nchunk):

        @pl.loop(k * cstep, (k + 1) * cstep, step=2)
        def _(c):
            grads = []
            for m in range(2):
                h = hid_n[c + m].astype(F32)
                slope = jnp.where(h > 0, 1.0, jnp.exp(jnp.minimum(h, 0.0)))
                g = gt[pl.ds(8 * ch + c + m, ti, stride=ch), :]
                pg = (cot_n[c + m].astype(F32) + g * slope).astype(BF)
                cot_n[c + m] = pg
                grads.append(pg)
            grads = jnp.concatenate(grads, axis=1)
            both = jnp.concatenate([mix[c], mix[c + 1]], axis=1)
            lg_acc[...] += dot(grads, both, NT)
            mg = dot(left_t[...], grads)
            for m in range(2):
                mgf[pl.ds(c + m, outer, stride=ch), :] = mg[:, 128 * m : 128 * (m + 1)]

        pg_out[k].start()

    mg = mgf[...]
    mg_hi = mg.astype(BF)
    mg_lo = (mg - mg_hi.astype(F32)).astype(BF)
    rg = (dot(ow_q[...], mg_hi) + dot(ow_q[...], mg_lo)).T
    rg_out[...] = rg.reshape(nr, own, outer)
    lg_out[...] = lg_acc[...].reshape(nc, own, outer)
    land_l[col] = lg_out[col]
    if comm:
        for d in range(1, nc):
            other = lax.rem(col + d, nc)
            move = remote(lg_out.at[other], land_l.at[col], g_send.at[d], g_recv.at[d], (row, other))
            move.start()
            l_moves.append(move)
        for k in range(nr):
            r, c = source(k)
            me = jnp.logical_and(r == row, c == col)
            far = remote(
                rg_out.at[k], land_r.at[row], g_send.at[nc + k], g_recv.at[nc + row], (r, c)
            )
            near = pltpu.make_async_copy(rg_out.at[k], land_r.at[row], g_recv.at[nc + row])

            @pl.when(me)
            def _():
                near.start()

            @pl.when(jnp.logical_not(me))
            def _():
                far.start()

            r_moves.append((me, far))
        for move in a_moves:
            move.wait_recv()
    total = land_a[0]
    for k in range(1, nc):
        total = total + land_a[k]
    land_b[row] = total
    if comm:
        for d in range(1, nr):
            move = remote(
                land_b.at[row], land_b.at[row], w_send.at[nc + d], w_recv.at[nc + d],
                (lax.rem(row + d, nr), col),
            )
            move.start()
            b_moves.append(move)
        for move in act_moves:
            move.wait_recv()
    unpack_edges(act_t, 4, 1)
    gt[: 8 * ch] = jnp.zeros((8 * ch, 128), F32)

    def forward(g):
        spread(dot(wf[...], stack(act_t, 4, g, False)), g, (2, 1, 0))

    forward(0)
    forward(1)
    po_out = [
        pltpu.make_async_copy(
            hid_n.at[:, pl.ds(PACK * k, PACK)], po_hbm.at[:, pl.ds(PACK * k, PACK)],
            out_sem.at[nchunk + k],
        )
        for k in range(kg)
    ]
    for k in range(kg):

        @pl.loop(8 * k + 2, 8 * k + 10)
        def _(g):
            forward(g)

        @pl.loop(0, ch, unroll=4)
        def _(c):
            conv = gt[pl.ds((8 + PACK * k) * ch + c, PACK, stride=ch), :]
            h = hid_n[c, pl.ds(PACK * k, PACK), :].astype(F32)
            hid_n[c, pl.ds(PACK * k, PACK), :] = (h + bias[c] + conv).astype(BF)

        po_out[k].start()
        if k == kg // 2 - 1:
            if comm:
                for move in b_moves:
                    move.wait_recv()
            total = land_b[0]
            for m in range(1, nr):
                total = total + land_b[m]
            fin[col] = total * (1.0 / residues)
            if comm:
                for d in range(1, nc):
                    move = remote(
                        fin.at[col], fin.at[col], w_send.at[nc + nr + d], w_recv.at[nc + nr + d],
                        (row, lax.rem(col + d, nc)),
                    )
                    move.start()
                    c_moves.append(move)

    if comm:
        for move in l_moves:
            move.wait_recv()
        for k in range(nr):
            pltpu.make_async_copy(rg_out.at[k], land_r.at[k], g_recv.at[nc + k]).wait()
    lg = land_l[0]
    for k in range(1, nc):
        lg = lg + land_l[k]
    rg = land_r[0]
    for k in range(1, nr):
        rg = rg + land_r[k]

    def exact(x, w):
        total = jnp.zeros((own, w.shape[0]), F32)
        for _ in range(3):
            head = x.astype(BF)
            total = total + dot(head, w, NT)
            x = x - head.astype(F32)
        return total

    fg_out[...] = (exact(lg, lw[...]) + exact(rg, rw[...])) * (1.0 / math.sqrt(residues))

    if comm:
        for move in c_moves:
            move.wait_recv()
    whole = fin[...].reshape(6 * ch, 128)
    for a in range(3):
        for b in range(3):
            base = 3 * ch * (a // 2) + b * ch
            at = ch * (a % 2)
            wg_out[3 * a + b] = whole[base : base + ch, at : at + ch]

    for copy in pg_out + po_out:
        copy.wait()
    if comm:
        for move in left_moves + cot_moves + act_moves + a_moves + b_moves + c_moves + l_moves:
            move.wait_send()
        for me, far in right_moves + r_moves:

            @pl.when(jnp.logical_not(me))
            def _():
                far.wait_send()


def call(nr, nc, residues, comm, pair_map, features, lw, rw, ow, cw, bias, cot):
    ch, ti, tj = pair_map.shape
    own, feat = features.shape
    outer = lw.shape[1]
    kg = ti // PACK
    part = 6 * ch // nc
    any_spec = pl.BlockSpec(memory_space=pl.ANY)
    vmem = pl.BlockSpec(memory_space=pltpu.VMEM)
    smem = pl.BlockSpec(memory_space=pltpu.SMEM)
    V = pltpu.VMEM
    dma = pltpu.SemaphoreType.DMA
    scratch = [
        V((ch, ti, tj), BF),
        V((ch, ti, tj), BF),
        V((ch * (ti + 8), 128), F32),
        V(((ti + 20) * ch, 128), F32),
        V((ti + 8, ch, 128), BF),
        V((ti + 16, ch, 128), BF),
        V(((kg + 2) * PACK, ch, 128), BF),
        V(((kg + 2) * ch, 256), BF),
        V((PACK // 2 * 256, 256), BF),
        V((kg * ch, 256), F32),
        V((2, 2, kg, ch, 128), BF),
        V((2, 2, 4, ch, 128), BF),
        V((2, 2, kg + 2, ch, 128), BF),
        V((own, 128), BF),
        V((nc, own, 128), BF),
        V((nr, own, 128), BF),
        V((ti, outer), BF),
        V((outer, ti), BF),
        V((outer * ch, 128), F32),
        V((ch, outer, 128), BF),
        V((3 * ch, 3 * ch), BF),
        V((3 * ch, 3 * ch), BF),
        V((outer, outer * ch), BF),
        V((outer * ch, 128), F32),
        V((3 * ch, 3 * ch), F32),
        V((6 * ch, 128), F32),
        V((nc, part, 128), F32),
        V((nr, part, 128), F32),
        V((nc, part, 128), F32),
        V((ti, outer), F32),
        V((nc, own, outer), F32),
        V((nr, own, outer), F32),
        V((nc, own, outer), F32),
        V((nr, own, outer), F32),
        dma((ch // 8 + 2,)),
        dma((ch // 8 + kg,)),
        dma((nc + nr,)),
        dma((nc + nr,)),
        dma((2, 8)),
        dma((2, 8)),
        dma((2 * nc + nr,)),
        dma((2 * nc + nr,)),
        dma((nc + nr,)),
        dma((nc + nr,)),
    ]
    macs = ti * tj * (27 * ch * ch + 3 * outer * ch)
    sel = jnp.asarray(edge_selector(), BF)
    out = pl.pallas_call(
        functools.partial(kernel, nr, nc, ch, ti, outer, comm, residues),
        out_shape=[
            jax.ShapeDtypeStruct((ch, ti, tj), BF),
            jax.ShapeDtypeStruct((ch, ti, tj), BF),
            jax.ShapeDtypeStruct((9, ch, ch), F32),
            jax.ShapeDtypeStruct((own, feat), F32),
        ],
        in_specs=[any_spec, any_spec, any_spec, smem] + [vmem] * 5,
        out_specs=[any_spec, any_spec, vmem, vmem],
        scratch_shapes=scratch,
        compiler_params=pltpu.CompilerParams(
            collective_id=0 if comm else None,
            has_side_effects=True,
            vmem_limit_bytes=60 * 1024 * 1024,
        ),
        cost_estimate=pl.CostEstimate(
            flops=2 * macs, bytes_accessed=8 * ch * ti * tj, transcendentals=2 * ch * ti * tj
        ),
    )(cot, pair_map, sel, bias, features, lw, rw, ow, cw.reshape(9, ch, ch))
    return out[0], out[1], out[2].reshape(3, 3, ch, ch), out[3]


def solution(mesh):
    nr, nc = mesh.shape["row"], mesh.shape["col"]

    def shards(pair_map, features, lw, rw, ow, cw, bias, cot):
        return call(
            nr, nc, pair_map.shape[1] * nr, True, pair_map, features, lw, rw, ow, cw, bias, cot
        )

    in_specs = (
        P(None, "row", "col"),
        P(("row", "col"), None),
        P(),
        P(),
        P(),
        P(),
        P(),
        P(None, "row", "col"),
    )
    out_specs = (P(None, "row", "col"), P(None, "row", "col"), P(), P(("row", "col"), None))
    return jax.shard_map(shards, mesh=mesh, in_specs=in_specs, out_specs=out_specs, check_vma=False)
```

```python
import functools
import math

import jax
import jax.numpy as jnp
from jax import lax
from jax.experimental import pallas as pl
from jax.experimental.pallas import tpu as pltpu
from jax.sharding import PartitionSpec as P

MESH = pl.DeviceIdType.MESH
BF = jnp.bfloat16
F32 = jnp.float32
NT = (((1,), (1,)), ((), ()))
PACK = 16
BLOCK = 32


def dot(a, b, dims=None):
    if dims is None:
        return jnp.dot(a, b, preferred_element_type=F32)
    return lax.dot_general(a, b, dims, preferred_element_type=F32)


def kernel(
    nr, nc, ch, ti, outer, comm, residues,
    cot_hbm, pm_hbm, bias, feat, lw, rw, ow, cw,
    po_hbm, pg_hbm, wg_out, fg_out,
    cot_n, hid_n, slope_n, wide, gt, cot_t, act_t, hx, even, odd, upd_even, upd_odd, packs, land_row, land_col,
    lr, left_in, right_in, left, left_t, mixf, mix, wf, wb, ow_q, mgf,
    wg_acc, wgs, land_a, land_b, fin, lg_acc, lg_out, rg_out, land_l, land_r,
    in_sem, out_sem, f_send, f_recv, h_send, h_recv, w_send, w_recv, g_send, g_recv,
):
    row = lax.axis_index("row")
    col = lax.axis_index("col")
    kg = ti // PACK
    ng = ti // 4
    pitch = ti + 8
    wch = ch + 8
    own = lr.shape[0]
    flat = row * nc + col
    goal = flat // nr
    slot = lax.rem(flat, nr)
    up, down = lax.rem(row + nr - 1, nr), lax.rem(row + 1, nr)
    west, east = lax.rem(col + nc - 1, nc), lax.rem(col + 1, nc)
    cstep = 8
    nchunk = ch // cstep

    cot_in = [
        pltpu.make_async_copy(
            cot_hbm.at[pl.ds(k * cstep, cstep)], cot_n.at[pl.ds(k * cstep, cstep)], in_sem.at[k]
        )
        for k in range(nchunk)
    ]
    pm_in = pltpu.make_async_copy(pm_hbm, hid_n, in_sem.at[nchunk])
    for copy in cot_in:
        copy.start()
    pm_in.start()

    def source(k):
        f = col * nr + k
        return f // nc, lax.rem(f, nc)

    if comm:
        barrier = pltpu.get_barrier_semaphore()

        def greet(r, c):
            pl.semaphore_signal(barrier, inc=1, device_id=(r, c), device_id_type=MESH)

        def greet_unless_me(r, c):
            @pl.when(jnp.logical_or(r != row, c != col))
            def _():
                greet(r, c)

        for d in range(1, nc):
            greet(row, lax.rem(col + d, nc))
        for d in range(1, nr):
            greet(lax.rem(row + d, nr), col)
        for r in (up, down):
            for c in (west, east):
                greet(r, c)
        for k in range(nr):
            greet_unless_me(k, goal)
            greet_unless_me(*source(k))
        total_greets = (nc - 1) + (nr - 1) + 4 + 2 * nr - jnp.where(goal == col, 2, 0)

    lr[...] = jnp.concatenate(
        [dot(feat[...], lw[...], NT), dot(feat[...], rw[...], NT), jnp.zeros((own, 128 - 2 * outer), F32)],
        axis=1,
    ).astype(BF)

    def remote(src, dst, ssem, rsem, dev):
        return pltpu.make_async_remote_copy(
            src_ref=src, dst_ref=dst, send_sem=ssem, recv_sem=rsem, device_id=dev, device_id_type=MESH
        )

    for a in range(3):
        wf[a * ch : (a + 1) * ch, :] = jnp.concatenate([cw[3 * a + b] for b in range(3)], axis=1)
        wb[a * ch : (a + 1) * ch, :] = jnp.concatenate(
            [cw[3 * a + b].astype(F32).T for b in range(3)], axis=1
        ).astype(BF)
    ow_q[...] = jnp.concatenate([ow[p] for p in range(outer)], axis=1)

    def p_widen():
        for k in range(nchunk):
            cot_in[k].wait()

            @pl.loop(0, cstep, unroll=2)
            def _(c):
                at = pl.multiple_of((k * cstep + c) * pitch, 8)
                wide[pl.ds(at, ti), :] = cot_n[k * cstep + c].astype(F32)

    p_widen()

    left_in[col] = lr[...]
    left_moves, right_moves = [], []
    if comm:
        pl.semaphore_wait(barrier, total_greets)
        for d in range(1, nc):
            move = remote(
                lr, left_in.at[col], f_send.at[d], f_recv.at[d], (row, lax.rem(col + d, nc))
            )
            move.start()
            left_moves.append(move)
        for k in range(nr):
            me = jnp.logical_and(row == k, goal == col)
            far = remote(
                lr, right_in.at[slot], f_send.at[nc + k], f_recv.at[nc + slot], (k, goal)
            )
            near = pltpu.make_async_copy(lr, right_in.at[slot], f_recv.at[nc + slot])

            @pl.when(me)
            def _():
                near.start()

            @pl.when(jnp.logical_not(me))
            def _():
                far.start()

            right_moves.append((me, far))

    lane = lax.broadcasted_iota(jnp.int32, (ch, 128), 1)
    window = lax.rem(lane + 4, 128) // 8

    def to_rows(dst, first, which):
        @pl.loop(0, kg, unroll=2)
        def _(k):
            packed = None
            for m in range(PACK):
                row_at = PACK * k + m
                x = wide[pl.ds(row_at, ch, stride=pitch), :].astype(BF)
                dst[first + row_at] = x
                packed = x if m == 0 else jnp.where(window == m, pltpu.roll(x, 8 * m, 1), packed)
            packs[which, k] = packed

    def halo_moves(src, first, which):
        edges = packs.at[which]
        from_west, from_east = land_col.at[which, 0], land_col.at[which, 1]
        plan = [
            (src.at[pl.ds(first, 4)], land_row.at[which, 1], (up, col)),
            (src.at[pl.ds(first + ti - 4, 4)], land_row.at[which, 0], (down, col)),
            (edges, from_east.at[pl.ds(1, kg)], (row, west)),
            (edges, from_west.at[pl.ds(1, kg)], (row, east)),
            (edges.at[0], from_east.at[kg + 1], (up, west)),
            (edges.at[0], from_west.at[kg + 1], (up, east)),
            (edges.at[kg - 1], from_east.at[0], (down, west)),
            (edges.at[kg - 1], from_west.at[0], (down, east)),
        ]
        return [
            remote(s, d, h_send.at[which, m], h_recv.at[which, m], dev)
            for m, (s, d, dev) in enumerate(plan)
        ]

    to_rows(cot_t, 4, 0)
    cot_moves = halo_moves(cot_t, 4, 0)
    if comm:
        for move in cot_moves:
            move.start()

    if comm:
        for d in range(1, nc):
            left_moves[d - 1].wait_recv()
        for k in range(nr):
            pltpu.make_async_copy(lr, right_in.at[k], f_recv.at[nc + k]).wait()
    left[...] = left_in[...].reshape(nc * own, 128)[:, :outer]
    left_t[...] = left[...].astype(F32).T.astype(BF)
    right = right_in[...].reshape(nr * own, 128)[:, outer : 2 * outer]
    step = 512
    for s in range(outer * ch // step):
        w = ow_q[:, s * step : (s + 1) * step].astype(F32).T.astype(BF)
        rows = dot(w, right, NT).astype(BF).astype(F32)
        for m in range(step // ch):
            at = (s * (step // ch) + m) * wch
            mixf[at : at + ch, :] = rows[m * ch : (m + 1) * ch]

    @pl.loop(0, ch, unroll=4)
    def _(c):
        mix[c] = mixf[pl.ds(c, outer, stride=wch), :].astype(BF)

    pm_in.wait()

    def p_hidden():
        def update(c):
            return dot(left[...], jnp.concatenate([mix[c], mix[c + 1]], axis=1))

        def finish(c, change):
            for k in range(2):
                hidden = (hid_n[c + k].astype(F32) + change[:, 128 * k : 128 * (k + 1)]).astype(BF)
                hid_n[c + k] = hidden
                h = hidden.astype(F32)
                e = jnp.exp(jnp.minimum(h, 0.0))
                slope_n[c + k] = e.astype(BF)
                at = pl.multiple_of((c + k) * pitch, 8)
                wide[pl.ds(at, ti), :] = jnp.where(h > 0, h, e - 1.0)

        upd_even[...] = update(0)

        @pl.loop(0, ch, step=4)
        def _(c):
            upd_odd[...] = update(c + 2)
            finish(c, upd_even[...])
            upd_even[...] = update(jnp.minimum(c + 4, ch - 2))
            finish(c + 2, upd_odd[...])

    p_hidden()

    to_rows(act_t, 8, 1)
    for s in (0, 4, ti + 8, ti + 12):
        act_t[s : s + 4] = jnp.zeros((4, ch, 128), BF)
    act_moves = halo_moves(act_t, 8, 1)
    if comm:
        for move in act_moves:
            move.start()

    has_up, has_down, has_west, has_east = row > 0, row < nr - 1, col > 0, col < nc - 1

    def keep(ok, x):
        return jnp.where(ok, x, jnp.zeros_like(x))

    def unpack_edges(dst, first, which):
        dst[first : first + 4] = keep(has_up, land_row[which, 0])
        dst[first + ti + 4 : first + ti + 8] = keep(has_down, land_row[which, 1])

        def place(k, ok):
            from_west = keep(jnp.logical_and(ok, has_west), land_col[which, 0, k])
            from_east = keep(jnp.logical_and(ok, has_east), land_col[which, 1, k])
            hx[k] = jnp.where(
                lax.rem(lane, 8) < 4, pltpu.roll(from_west, 4, 1), pltpu.roll(from_east, 124, 1)
            )

        place(0, has_up)
        place(kg + 1, has_down)

        @pl.loop(1, kg + 1, unroll=4)
        def _(k):
            place(k, True)

    def fill(dst, src, first, n, q, turned):
        for r in range(8):
            x = src[first + 16 * n + q + r]
            at = q + r + PACK - 4
            edge = pltpu.roll(hx[n + at // PACK], (PACK - at % PACK) % PACK * 8, 1)
            before = jnp.where(lane < 4, edge, pltpu.roll(x, 4, 1))
            after = jnp.where(lane >= 124, edge, pltpu.roll(x, 124, 1))
            lanes = slice(128 * r, 128 * (r + 1))
            dst[:ch, lanes] = after if turned else before
            dst[ch : 2 * ch, lanes] = x
            dst[2 * ch :, lanes] = before if turned else after

    def halves(x):
        return [x[:, :512], x[:, 512:]]

    def spread(parts, g, order):
        for s in range(len(parts) + 2):
            terms = [
                parts[s - k][a * ch : (a + 1) * ch]
                for k, a in enumerate(order)
                if 0 <= s - k < len(parts)
            ]
            total = terms[0]
            for term in terms[1:]:
                total = total + term
            for r in range(4):
                at = pl.ds(pl.multiple_of((4 * (g + s) + r) * wch, 8), ch)
                term = total[:, 128 * r : 128 * (r + 1)]
                gt[at, :] = gt[at, :] + term if s < 2 else term

    if comm:
        for move in cot_moves:
            move.wait_recv()
    unpack_edges(cot_t, 0, 0)
    gt[: 8 * wch] = jnp.zeros((8 * wch, 128), F32)
    wg_acc[...] = jnp.zeros_like(wg_acc)

    def p_back():
        fill(even, cot_t, 0, 0, 0, True)

        def acts(first):
            return jnp.concatenate(
                [
                    jnp.concatenate([act_t[first + 4 * a + r] for r in range(8)], axis=1)
                    for a in range(3)
                ],
                axis=0,
            )

        @pl.loop(0, ti // 16)
        def _(n):
            parts = halves(dot(wb[...], even[...]))
            grad = dot(even[...], acts(16 * n), NT)
            fill(odd, cot_t, 0, n, 8, True)
            parts += halves(dot(wb[...], odd[...]))
            grad = grad + dot(odd[...], acts(16 * n + 8), NT)
            fill(even, cot_t, 0, n, 16, True)
            spread(parts, 4 * n, (0, 1, 2))
            wg_acc[...] += grad

        spread(halves(dot(wb[...], even[...])), ng, (0, 1, 2))
        wg_acc[...] += dot(even[...], acts(ti), NT)

    p_back()

    part = 2 * 3 * ch // nc
    wgs[: 3 * ch] = wg_acc[:, :128]
    wgs[3 * ch :] = jnp.concatenate([wg_acc[:, 128:], jnp.zeros((3 * ch, 256 - 3 * ch), F32)], axis=1)
    land_a[col] = wgs[pl.ds(pl.multiple_of(col * part, 8), part)]
    a_moves, b_moves, c_moves, l_moves, r_moves = [], [], [], [], []
    if comm:
        for d in range(1, nc):
            other = lax.rem(col + d, nc)
            move = remote(
                wgs.at[pl.ds(pl.multiple_of(other * part, 8), part)],
                land_a.at[col], w_send.at[d], w_recv.at[d], (row, other),
            )
            move.start()
            a_moves.append(move)

    pg_out = [
        pltpu.make_async_copy(
            cot_n.at[pl.ds(k * cstep, cstep)], pg_hbm.at[pl.ds(k * cstep, cstep)], out_sem.at[k]
        )
        for k in range(nchunk)
    ]
    lg_acc[...] = jnp.zeros_like(lg_acc)

    def p_grad(k):
        @pl.loop(k * cstep, (k + 1) * cstep, step=4)
        def _(c):
            grads = []
            for m in range(4):
                g = gt[pl.ds(8 * wch + c + m, ti, stride=wch), :]
                pg = (cot_n[c + m].astype(F32) + g * slope_n[c + m].astype(F32)).astype(BF)
                cot_n[c + m] = pg
                grads.append(pg)
            grads = jnp.concatenate(grads, axis=1)
            mixes = jnp.concatenate([mix[c + m] for m in range(4)], axis=1)
            lg_acc[...] += dot(mixes, grads, NT)
            mg = dot(left_t[...], grads)
            for m in range(4):
                mgf[pl.ds(c + m, outer, stride=wch), :] = mg[:, 128 * m : 128 * (m + 1)]

    for k in range(nchunk):
        p_grad(k)
        pg_out[k].start()

    mg = jnp.concatenate([mgf[p * wch : p * wch + ch, :] for p in range(outer)], axis=0)
    mg_hi = mg.astype(BF)
    mg_lo = (mg - mg_hi.astype(F32)).astype(BF)
    rg = (dot(ow_q[...], mg_hi) + dot(ow_q[...], mg_lo)).T
    rg_out[...] = rg.reshape(nr, own, outer)
    lg_out[...] = lg_acc[...].T.reshape(nc, own, outer)
    land_l[col] = lg_out[col]
    if comm:
        for d in range(1, nc):
            other = lax.rem(col + d, nc)
            move = remote(lg_out.at[other], land_l.at[col], g_send.at[d], g_recv.at[d], (row, other))
            move.start()
            l_moves.append(move)
        for k in range(nr):
            r, c = source(k)
            me = jnp.logical_and(r == row, c == col)
            far = remote(
                rg_out.at[k], land_r.at[row], g_send.at[nc + k], g_recv.at[nc + row], (r, c)
            )
            near = pltpu.make_async_copy(rg_out.at[k], land_r.at[row], g_recv.at[nc + row])

            @pl.when(me)
            def _():
                near.start()

            @pl.when(jnp.logical_not(me))
            def _():
                far.start()

            r_moves.append((me, far))
        for move in a_moves:
            move.wait_recv()
    total = land_a[0]
    for k in range(1, nc):
        total = total + land_a[k]
    land_b[row] = total
    if comm:
        for d in range(1, nr):
            move = remote(
                land_b.at[row], land_b.at[row], w_send.at[nc + d], w_recv.at[nc + d],
                (lax.rem(row + d, nr), col),
            )
            move.start()
            b_moves.append(move)
        for move in act_moves:
            move.wait_recv()
    unpack_edges(act_t, 4, 1)
    gt[: 8 * wch] = jnp.zeros((8 * wch, 128), F32)

    nblock = ti // BLOCK
    po_out = [
        pltpu.make_async_copy(
            hid_n.at[:, pl.ds(BLOCK * k, BLOCK)], po_hbm.at[:, pl.ds(BLOCK * k, BLOCK)],
            out_sem.at[nchunk + k],
        )
        for k in range(nblock)
    ]

    fill(even, act_t, 4, 0, 0, False)

    def p_forward(first, last):
        @pl.loop(first, last)
        def _(n):
            parts = halves(dot(wf[...], even[...]))
            fill(odd, act_t, 4, n, 8, False)
            parts += halves(dot(wf[...], odd[...]))
            fill(even, act_t, 4, n, 16, False)
            spread(parts, 4 * n, (2, 1, 0))

    def p_finish(k):
        @pl.loop(0, ch, unroll=16)
        def _(c):
            conv = gt[pl.ds((8 + BLOCK * k) * wch + c, BLOCK, stride=wch), :]
            h = hid_n[c, pl.ds(BLOCK * k, BLOCK), :].astype(F32)
            hid_n[c, pl.ds(BLOCK * k, BLOCK), :] = (h + bias[c] + conv).astype(BF)

    for k in range(nblock):
        p_forward(2 * k + 1 if k else 0, min(2 * k + 3, ti // 16))
        if k == nblock - 1:
            spread(halves(dot(wf[...], even[...])), ng, (2, 1, 0))
        p_finish(k)
        po_out[k].start()
        if k == nblock // 2 - 1:
            if comm:
                for move in b_moves:
                    move.wait_recv()
            total = land_b[0]
            for m in range(1, nr):
                total = total + land_b[m]
            fin[col] = total * (1.0 / residues)
            if comm:
                for d in range(1, nc):
                    move = remote(
                        fin.at[col], fin.at[col], w_send.at[nc + nr + d], w_recv.at[nc + nr + d],
                        (row, lax.rem(col + d, nc)),
                    )
                    move.start()
                    c_moves.append(move)

    if comm:
        for move in l_moves:
            move.wait_recv()
        for k in range(nr):
            pltpu.make_async_copy(rg_out.at[k], land_r.at[k], g_recv.at[nc + k]).wait()
    lg = land_l[0]
    for k in range(1, nc):
        lg = lg + land_l[k]
    rg = land_r[0]
    for k in range(1, nr):
        rg = rg + land_r[k]

    def exact(x, w):
        total = jnp.zeros((own, w.shape[1]), F32)
        for _ in range(3):
            head = x.astype(BF)
            total = total + dot(head, w)
            x = x - head.astype(F32)
        return total

    fg_out[...] = (exact(lg, lw[...]) + exact(rg, rw[...])) * (1.0 / math.sqrt(residues))

    if comm:
        for move in c_moves:
            move.wait_recv()
    whole = fin[...].reshape(6 * ch, 128)
    for a in range(3):
        for b in range(3):
            base = 3 * ch * (a // 2) + b * ch
            at = ch * (a % 2)
            wg_out[3 * a + b] = whole[base : base + ch, at : at + ch]

    for copy in pg_out + po_out:
        copy.wait()
    if comm:
        for move in left_moves + cot_moves + act_moves + a_moves + b_moves + c_moves + l_moves:
            move.wait_send()
        for me, far in right_moves + r_moves:

            @pl.when(jnp.logical_not(me))
            def _():
                far.wait_send()


def call(nr, nc, residues, comm, pair_map, features, lw, rw, ow, cw, bias, cot):
    ch, ti, tj = pair_map.shape
    own, feat = features.shape
    outer = lw.shape[1]
    kg = ti // PACK
    part = 6 * ch // nc
    any_spec = pl.BlockSpec(memory_space=pl.ANY)
    vmem = pl.BlockSpec(memory_space=pltpu.VMEM)
    smem = pl.BlockSpec(memory_space=pltpu.SMEM)
    V = pltpu.VMEM
    dma = pltpu.SemaphoreType.DMA
    scratch = [
        V((ch, ti, tj), BF),
        V((ch, ti, tj), BF),
        V((ch, ti, tj), BF),
        V((ch * (ti + 8), 128), F32),
        V(((ti + 20) * (ch + 8), 128), F32),
        V((ti + 8, ch, 128), BF),
        V((ti + 16, ch, 128), BF),
        V((kg + 2, ch, 128), BF),
        V((3 * ch, 1024), BF),
        V((3 * ch, 1024), BF),
        V((ti, 256), F32),
        V((ti, 256), F32),
        V((2, kg, ch, 128), BF),
        V((2, 2, 4, ch, 128), BF),
        V((2, 2, kg + 2, ch, 128), BF),
        V((own, 128), BF),
        V((nc, own, 128), BF),
        V((nr, own, 128), BF),
        V((ti, outer), BF),
        V((outer, ti), BF),
        V((outer * (ch + 8), 128), F32),
        V((ch, outer, 128), BF),
        V((3 * ch, 3 * ch), BF),
        V((3 * ch, 3 * ch), BF),
        V((outer, outer * ch), BF),
        V((outer * (ch + 8), 128), F32),
        V((3 * ch, 3 * ch), F32),
        V((6 * ch, 128), F32),
        V((nc, part, 128), F32),
        V((nr, part, 128), F32),
        V((nc, part, 128), F32),
        V((outer, ti), F32),
        V((nc, own, outer), F32),
        V((nr, own, outer), F32),
        V((nc, own, outer), F32),
        V((nr, own, outer), F32),
        dma((ch // 8 + 1,)),
        dma((ch // 8 + ti // BLOCK,)),
        dma((nc + nr,)),
        dma((nc + nr,)),
        dma((2, 8)),
        dma((2, 8)),
        dma((2 * nc + nr,)),
        dma((2 * nc + nr,)),
        dma((nc + nr,)),
        dma((nc + nr,)),
    ]
    macs = ti * tj * (27 * ch * ch + 3 * outer * ch)
    out = pl.pallas_call(
        functools.partial(kernel, nr, nc, ch, ti, outer, comm, residues),
        out_shape=[
            jax.ShapeDtypeStruct((ch, ti, tj), BF),
            jax.ShapeDtypeStruct((ch, ti, tj), BF),
            jax.ShapeDtypeStruct((9, ch, ch), F32),
            jax.ShapeDtypeStruct((own, feat), F32),
        ],
        in_specs=[any_spec, any_spec, smem] + [vmem] * 5,
        out_specs=[any_spec, any_spec, vmem, vmem],
        scratch_shapes=scratch,
        compiler_params=pltpu.CompilerParams(
            collective_id=0 if comm else None,
            has_side_effects=True,
            vmem_limit_bytes=60 * 1024 * 1024,
        ),
        cost_estimate=pl.CostEstimate(
            flops=2 * macs, bytes_accessed=8 * ch * ti * tj, transcendentals=2 * ch * ti * tj
        ),
    )(cot, pair_map, bias, features, lw.T, rw.T, ow, cw.reshape(9, ch, ch))
    return out[0], out[1], out[2].reshape(3, 3, ch, ch), out[3]


def solution(mesh):
    nr, nc = mesh.shape["row"], mesh.shape["col"]

    def shards(pair_map, features, lw, rw, ow, cw, bias, cot):
        return call(
            nr, nc, pair_map.shape[1] * nr, True, pair_map, features, lw, rw, ow, cw, bias, cot
        )

    in_specs = (
        P(None, "row", "col"),
        P(("row", "col"), None),
        P(),
        P(),
        P(),
        P(),
        P(),
        P(None, "row", "col"),
    )
    out_specs = (P(None, "row", "col"), P(None, "row", "col"), P(), P(("row", "col"), None))
    return jax.shard_map(shards, mesh=mesh, in_specs=in_specs, out_specs=out_specs, check_vma=False)
```

```python
import functools
import math

import jax
import jax.numpy as jnp
from jax import lax
from jax.experimental import pallas as pl
from jax.experimental.pallas import tpu as pltpu
from jax.sharding import PartitionSpec as P

MESH = pl.DeviceIdType.MESH
BF = jnp.bfloat16
F32 = jnp.float32
NT = (((1,), (1,)), ((), ()))
PACK = 16
BLOCK = 32
STEP = 4


def dot(a, b, dims=None):
    if dims is None:
        return jnp.dot(a, b, preferred_element_type=F32)
    return lax.dot_general(a, b, dims, preferred_element_type=F32)


def kernel(
    nr, nc, ch, ti, outer, comm, residues,
    cot_hbm, pm_hbm, feat, lw, rw, ow, cw,
    hid_n, cot_n, gt, wg_out, fg_out,
    slope_n, wide, cot_t, act_t, hx, even, odd, upd_even, upd_odd, packs, land_row, land_col,
    lr, left_in, right_in, left, left_t, mixf, mix, wf, wb, ow_q, mgf,
    wg_acc, wgs, land_a, land_b, fin, lg_acc, lg_out, rg_out, land_l, land_r,
    in_sem, f_send, f_recv, h_send, h_recv, w_send, w_recv, g_send, g_recv,
):
    row = lax.axis_index("row")
    col = lax.axis_index("col")
    kg = ti // PACK
    ng = ti // 4
    pitch = ti + 8
    wch = ch + 8
    own = lr.shape[0]
    flat = row * nc + col
    goal = flat // nr
    slot = lax.rem(flat, nr)
    up, down = lax.rem(row + nr - 1, nr), lax.rem(row + 1, nr)
    west, east = lax.rem(col + nc - 1, nc), lax.rem(col + 1, nc)
    cstep = 8
    nchunk = ch // cstep

    cot_in = [
        pltpu.make_async_copy(
            cot_hbm.at[pl.ds(k * cstep, cstep)], cot_n.at[pl.ds(k * cstep, cstep)], in_sem.at[k]
        )
        for k in range(nchunk)
    ]
    pm_in = pltpu.make_async_copy(pm_hbm, hid_n, in_sem.at[nchunk])
    for copy in cot_in:
        copy.start()
    pm_in.start()

    def source(k):
        f = col * nr + k
        return f // nc, lax.rem(f, nc)

    if comm:
        barrier = pltpu.get_barrier_semaphore()

        def greet(r, c):
            pl.semaphore_signal(barrier, inc=1, device_id=(r, c), device_id_type=MESH)

        def greet_unless_me(r, c):
            @pl.when(jnp.logical_or(r != row, c != col))
            def _():
                greet(r, c)

        for d in range(1, nc):
            greet(row, lax.rem(col + d, nc))
        for d in range(1, nr):
            greet(lax.rem(row + d, nr), col)
        for r in (up, down):
            for c in (west, east):
                greet(r, c)
        for k in range(nr):
            greet_unless_me(k, goal)
            greet_unless_me(*source(k))
        total_greets = (nc - 1) + (nr - 1) + 4 + 2 * nr - jnp.where(goal == col, 2, 0)

    lr[...] = jnp.concatenate(
        [dot(feat[...], lw[...], NT), dot(feat[...], rw[...], NT), jnp.zeros((own, 128 - 2 * outer), F32)],
        axis=1,
    ).astype(BF)

    def remote(src, dst, ssem, rsem, dev):
        return pltpu.make_async_remote_copy(
            src_ref=src, dst_ref=dst, send_sem=ssem, recv_sem=rsem, device_id=dev, device_id_type=MESH
        )

    for a in range(3):
        wf[a * ch : (a + 1) * ch, :] = jnp.concatenate([cw[3 * a + b] for b in range(3)], axis=1)
        wb[a * ch : (a + 1) * ch, :] = jnp.concatenate(
            [cw[3 * a + b].astype(F32).T for b in range(3)], axis=1
        ).astype(BF)
    ow_q[...] = jnp.concatenate([ow[p] for p in range(outer)], axis=1)

    def p_widen():
        for k in range(nchunk):
            cot_in[k].wait()

            @pl.loop(0, cstep, unroll=2)
            def _(c):
                at = pl.multiple_of((k * cstep + c) * pitch, 8)
                wide[pl.ds(at, ti), :] = cot_n[k * cstep + c].astype(F32)

    p_widen()

    left_in[col] = lr[...]
    left_moves, right_moves = [], []
    if comm:
        pl.semaphore_wait(barrier, total_greets)
        for d in range(1, nc):
            move = remote(
                lr, left_in.at[col], f_send.at[d], f_recv.at[d], (row, lax.rem(col + d, nc))
            )
            move.start()
            left_moves.append(move)
        for k in range(nr):
            me = jnp.logical_and(row == k, goal == col)
            far = remote(
                lr, right_in.at[slot], f_send.at[nc + k], f_recv.at[nc + slot], (k, goal)
            )
            near = pltpu.make_async_copy(lr, right_in.at[slot], f_recv.at[nc + slot])

            @pl.when(me)
            def _():
                near.start()

            @pl.when(jnp.logical_not(me))
            def _():
                far.start()

            right_moves.append((me, far))

    lane = lax.broadcasted_iota(jnp.int32, (ch, 128), 1)
    window = lax.rem(lane + 4, 128) // 8

    def to_rows(dst, first, which):
        @pl.loop(0, kg, unroll=2)
        def _(k):
            packed = None
            for m in range(PACK):
                row_at = PACK * k + m
                x = wide[pl.ds(row_at, ch, stride=pitch), :].astype(BF)
                dst[first + row_at] = x
                packed = x if m == 0 else jnp.where(window == m, pltpu.roll(x, 8 * m, 1), packed)
            packs[which, k] = packed

    def halo_moves(src, first, which):
        edges = packs.at[which]
        from_west, from_east = land_col.at[which, 0], land_col.at[which, 1]
        plan = [
            (src.at[pl.ds(first, 4)], land_row.at[which, 1], (up, col)),
            (src.at[pl.ds(first + ti - 4, 4)], land_row.at[which, 0], (down, col)),
            (edges, from_east.at[pl.ds(1, kg)], (row, west)),
            (edges, from_west.at[pl.ds(1, kg)], (row, east)),
            (edges.at[0], from_east.at[kg + 1], (up, west)),
            (edges.at[0], from_west.at[kg + 1], (up, east)),
            (edges.at[kg - 1], from_east.at[0], (down, west)),
            (edges.at[kg - 1], from_west.at[0], (down, east)),
        ]
        return [
            remote(s, d, h_send.at[which, m], h_recv.at[which, m], dev)
            for m, (s, d, dev) in enumerate(plan)
        ]

    to_rows(cot_t, 4, 0)
    cot_moves = halo_moves(cot_t, 4, 0)
    if comm:
        for move in cot_moves:
            move.start()

    if comm:
        for d in range(1, nc):
            left_moves[d - 1].wait_recv()
        for k in range(nr):
            pltpu.make_async_copy(lr, right_in.at[k], f_recv.at[nc + k]).wait()
    left[...] = left_in[...].reshape(nc * own, 128)[:, :outer]
    left_t[...] = left[...].astype(F32).T.astype(BF)
    right = right_in[...].reshape(nr * own, 128)[:, outer : 2 * outer]
    step = 512
    for s in range(outer * ch // step):
        w = ow_q[:, s * step : (s + 1) * step].astype(F32).T.astype(BF)
        rows = dot(w, right, NT).astype(BF).astype(F32)
        for m in range(step // ch):
            at = (s * (step // ch) + m) * wch
            mixf[at : at + ch, :] = rows[m * ch : (m + 1) * ch]

    @pl.loop(0, ch, unroll=4)
    def _(c):
        mix[c] = mixf[pl.ds(c, outer, stride=wch), :].astype(BF)

    pm_in.wait()

    def p_hidden():
        def update(c):
            return dot(left[...], jnp.concatenate([mix[c], mix[c + 1]], axis=1))

        def finish(c, change):
            for k in range(2):
                hidden = (hid_n[c + k].astype(F32) + change[:, 128 * k : 128 * (k + 1)]).astype(BF)
                hid_n[c + k] = hidden
                h = hidden.astype(F32)
                e = jnp.minimum(jnp.exp(h), 1.0)
                slope_n[c + k] = e.astype(BF)
                at = pl.multiple_of((c + k) * pitch, 8)
                wide[pl.ds(at, ti), :] = jnp.maximum(h, e - 1.0)

        upd_even[...] = update(0)

        @pl.loop(0, ch, step=4)
        def _(c):
            upd_odd[...] = update(c + 2)
            finish(c, upd_even[...])
            upd_even[...] = update(jnp.minimum(c + 4, ch - 2))
            finish(c + 2, upd_odd[...])

    p_hidden()

    to_rows(act_t, 8, 1)
    for s in (0, 4, ti + 8, ti + 12):
        act_t[s : s + 4] = jnp.zeros((4, ch, 128), BF)
    act_moves = halo_moves(act_t, 8, 1)
    if comm:
        for move in act_moves:
            move.start()

    has_up, has_down, has_west, has_east = row > 0, row < nr - 1, col > 0, col < nc - 1

    def keep(ok, x):
        return jnp.where(ok, x, jnp.zeros_like(x))

    def unpack_edges(dst, first, which):
        dst[first : first + 4] = keep(has_up, land_row[which, 0])
        dst[first + ti + 4 : first + ti + 8] = keep(has_down, land_row[which, 1])

        def place(k, ok):
            from_west = keep(jnp.logical_and(ok, has_west), land_col[which, 0, k])
            from_east = keep(jnp.logical_and(ok, has_east), land_col[which, 1, k])
            hx[k] = jnp.where(
                lax.rem(lane, 8) < 4, pltpu.roll(from_west, 4, 1), pltpu.roll(from_east, 124, 1)
            )

        place(0, has_up)
        place(kg + 1, has_down)

        @pl.loop(1, kg + 1, unroll=4)
        def _(k):
            place(k, True)

    def fill(dst, src, first, n, q, turned):
        for r in range(8):
            x = src[first + 16 * n + q + r]
            at = q + r + PACK - 4
            edge = pltpu.roll(hx[n + at // PACK], (PACK - at % PACK) % PACK * 8, 1)
            before = jnp.where(lane < 4, edge, pltpu.roll(x, 4, 1))
            after = jnp.where(lane >= 124, edge, pltpu.roll(x, 124, 1))
            lanes = slice(128 * r, 128 * (r + 1))
            dst[:ch, lanes] = after if turned else before
            dst[ch : 2 * ch, lanes] = x
            dst[2 * ch :, lanes] = before if turned else after

    def halves(x):
        return [x[:, :512], x[:, 512:]]

    def spread(parts, g, order):
        for s in range(len(parts) + 2):
            terms = [
                parts[s - k][a * ch : (a + 1) * ch]
                for k, a in enumerate(order)
                if 0 <= s - k < len(parts)
            ]
            total = terms[0]
            for term in terms[1:]:
                total = total + term
            for r in range(4):
                at = pl.ds(pl.multiple_of((4 * (g + s) + r) * wch, 8), ch)
                term = total[:, 128 * r : 128 * (r + 1)]
                gt[at, :] = gt[at, :] + term if s < 2 else term

    if comm:
        for move in cot_moves:
            move.wait_recv()
    unpack_edges(cot_t, 0, 0)
    gt[: 8 * wch] = jnp.zeros((8 * wch, 128), F32)
    wg_acc[...] = jnp.zeros_like(wg_acc)

    def p_back():
        fill(even, cot_t, 0, 0, 0, True)

        def acts(first):
            return jnp.concatenate(
                [
                    jnp.concatenate([act_t[first + 4 * a + r] for r in range(8)], axis=1)
                    for a in range(3)
                ],
                axis=0,
            )

        @pl.loop(0, ti // 16, step=STEP)
        def _(n):
            parts, grad = [], 0
            for m in range(STEP):
                parts += halves(dot(wb[...], even[...]))
                grad = grad + dot(even[...], acts(16 * (n + m)), NT)
                fill(odd, cot_t, 0, n + m, 8, True)
                parts += halves(dot(wb[...], odd[...]))
                grad = grad + dot(odd[...], acts(16 * (n + m) + 8), NT)
                fill(even, cot_t, 0, n + m, 16, True)
            spread(parts, 4 * n, (0, 1, 2))
            wg_acc[...] += grad

        spread(halves(dot(wb[...], even[...])), ng, (0, 1, 2))
        wg_acc[...] += dot(even[...], acts(ti), NT)

    p_back()

    part = 2 * 3 * ch // nc
    wgs[: 3 * ch] = wg_acc[:, :128]
    wgs[3 * ch :] = jnp.concatenate([wg_acc[:, 128:], jnp.zeros((3 * ch, 256 - 3 * ch), F32)], axis=1)
    land_a[col] = wgs[pl.ds(pl.multiple_of(col * part, 8), part)]
    a_moves, b_moves, c_moves, l_moves, r_moves = [], [], [], [], []
    if comm:
        for d in range(1, nc):
            other = lax.rem(col + d, nc)
            move = remote(
                wgs.at[pl.ds(pl.multiple_of(other * part, 8), part)],
                land_a.at[col], w_send.at[d], w_recv.at[d], (row, other),
            )
            move.start()
            a_moves.append(move)

    lg_acc[...] = jnp.zeros_like(lg_acc)

    def p_grad():
        @pl.loop(0, ch, step=8)
        def _(c):
            lg = 0
            for half in (c, c + 4):
                grads = []
                for m in range(4):
                    g = gt[pl.ds(8 * wch + half + m, ti, stride=wch), :]
                    pg = (cot_n[half + m].astype(F32) + g * slope_n[half + m].astype(F32)).astype(BF)
                    cot_n[half + m] = pg
                    grads.append(pg)
                grads = jnp.concatenate(grads, axis=1)
                mixes = jnp.concatenate([mix[half + m] for m in range(4)], axis=1)
                lg = lg + dot(mixes, grads, NT)
                mg = dot(left_t[...], grads)
                for m in range(4):
                    mgf[pl.ds(half + m, outer, stride=wch), :] = mg[:, 128 * m : 128 * (m + 1)]
            lg_acc[...] += lg

    p_grad()

    mg = jnp.concatenate([mgf[p * wch : p * wch + ch, :] for p in range(outer)], axis=0)
    mg_hi = mg.astype(BF)
    mg_lo = (mg - mg_hi.astype(F32)).astype(BF)
    rg = (dot(ow_q[...], mg_hi) + dot(ow_q[...], mg_lo)).T
    rg_out[...] = rg.reshape(nr, own, outer)
    lg_out[...] = lg_acc[...].T.reshape(nc, own, outer)
    land_l[col] = lg_out[col]
    if comm:
        for d in range(1, nc):
            other = lax.rem(col + d, nc)
            move = remote(lg_out.at[other], land_l.at[col], g_send.at[d], g_recv.at[d], (row, other))
            move.start()
            l_moves.append(move)
        for k in range(nr):
            r, c = source(k)
            me = jnp.logical_and(r == row, c == col)
            far = remote(
                rg_out.at[k], land_r.at[row], g_send.at[nc + k], g_recv.at[nc + row], (r, c)
            )
            near = pltpu.make_async_copy(rg_out.at[k], land_r.at[row], g_recv.at[nc + row])

            @pl.when(me)
            def _():
                near.start()

            @pl.when(jnp.logical_not(me))
            def _():
                far.start()

            r_moves.append((me, far))
        for move in a_moves:
            move.wait_recv()
    total = land_a[0]
    for k in range(1, nc):
        total = total + land_a[k]
    land_b[row] = total
    if comm:
        for d in range(1, nr):
            move = remote(
                land_b.at[row], land_b.at[row], w_send.at[nc + d], w_recv.at[nc + d],
                (lax.rem(row + d, nr), col),
            )
            move.start()
            b_moves.append(move)
        for move in act_moves:
            move.wait_recv()
    unpack_edges(act_t, 4, 1)
    gt[: 8 * wch] = jnp.zeros((8 * wch, 128), F32)

    fill(even, act_t, 4, 0, 0, False)

    def p_forward(first, last):
        @pl.loop(first, last, step=STEP)
        def _(n):
            parts = []
            for m in range(STEP):
                parts += halves(dot(wf[...], even[...]))
                fill(odd, act_t, 4, n + m, 8, False)
                parts += halves(dot(wf[...], odd[...]))
                fill(even, act_t, 4, n + m, 16, False)
            spread(parts, 4 * n, (2, 1, 0))

    p_forward(0, ti // 32)
    if comm:
        for move in b_moves:
            move.wait_recv()
    total = land_b[0]
    for m in range(1, nr):
        total = total + land_b[m]
    fin[col] = total * (1.0 / residues)
    if comm:
        for d in range(1, nc):
            move = remote(
                fin.at[col], fin.at[col], w_send.at[nc + nr + d], w_recv.at[nc + nr + d],
                (row, lax.rem(col + d, nc)),
            )
            move.start()
            c_moves.append(move)
    p_forward(ti // 32, ti // 16)
    spread(halves(dot(wf[...], even[...])), ng, (2, 1, 0))

    if comm:
        for move in l_moves:
            move.wait_recv()
        for k in range(nr):
            pltpu.make_async_copy(rg_out.at[k], land_r.at[k], g_recv.at[nc + k]).wait()
    lg = land_l[0]
    for k in range(1, nc):
        lg = lg + land_l[k]
    rg = land_r[0]
    for k in range(1, nr):
        rg = rg + land_r[k]

    def exact(x, w):
        total = jnp.zeros((own, w.shape[1]), F32)
        for _ in range(3):
            head = x.astype(BF)
            total = total + dot(head, w)
            x = x - head.astype(F32)
        return total

    fg_out[...] = (exact(lg, lw[...]) + exact(rg, rw[...])) * (1.0 / math.sqrt(residues))

    if comm:
        for move in c_moves:
            move.wait_recv()
    whole = fin[...].reshape(6 * ch, 128)
    for a in range(3):
        for b in range(3):
            base = 3 * ch * (a // 2) + b * ch
            at = ch * (a % 2)
            wg_out[3 * a + b] = whole[base : base + ch, at : at + ch]

    if comm:
        for move in left_moves + cot_moves + act_moves + a_moves + b_moves + c_moves + l_moves:
            move.wait_send()
        for me, far in right_moves + r_moves:

            @pl.when(jnp.logical_not(me))
            def _():
                far.wait_send()


def last_kernel(
    hid_n, pg_n, gt, wg_in, fg_in, bias, po_hbm, pg_hbm, wg_hbm, fg_hbm, out_n, out_sem
):
    ch, ti, _ = hid_n.shape
    wch = ch + 8
    step = ch // 4
    copies = [
        pltpu.make_async_copy(
            pg_n.at[pl.ds(k * step, step)], pg_hbm.at[pl.ds(k * step, step)], out_sem.at[k]
        )
        for k in range(4)
    ]
    copies.append(pltpu.make_async_copy(wg_in, wg_hbm, out_sem.at[4]))
    copies.append(pltpu.make_async_copy(fg_in, fg_hbm, out_sem.at[5]))
    for copy in copies:
        copy.start()
    for k in range(ti // BLOCK):

        @pl.loop(0, ch, unroll=16)
        def _(c):
            conv = gt[pl.ds((8 + BLOCK * k) * wch + c, BLOCK, stride=wch), :]
            h = hid_n[c, pl.ds(BLOCK * k, BLOCK), :].astype(F32)
            out_n[c, pl.ds(BLOCK * k, BLOCK), :] = (h + bias[c] + conv).astype(BF)

        copy = pltpu.make_async_copy(
            out_n.at[:, pl.ds(BLOCK * k, BLOCK)], po_hbm.at[:, pl.ds(BLOCK * k, BLOCK)],
            out_sem.at[6 + k],
        )
        copy.start()
        copies.append(copy)
    for copy in copies:
        copy.wait()


def call(nr, nc, residues, comm, pair_map, features, lw, rw, ow, cw, bias, cot):
    ch, ti, tj = pair_map.shape
    own, feat = features.shape
    outer = lw.shape[1]
    kg = ti // PACK
    part = 6 * ch // nc
    any_spec = pl.BlockSpec(memory_space=pl.ANY)
    vmem = pl.BlockSpec(memory_space=pltpu.VMEM)
    smem = pl.BlockSpec(memory_space=pltpu.SMEM)
    V = pltpu.VMEM
    dma = pltpu.SemaphoreType.DMA
    scratch = [
        V((ch, ti, tj), BF),
        V((ch * (ti + 8), 128), F32),
        V((ti + 8, ch, 128), BF),
        V((ti + 16, ch, 128), BF),
        V((kg + 2, ch, 128), BF),
        V((3 * ch, 1024), BF),
        V((3 * ch, 1024), BF),
        V((ti, 256), F32),
        V((ti, 256), F32),
        V((2, kg, ch, 128), BF),
        V((2, 2, 4, ch, 128), BF),
        V((2, 2, kg + 2, ch, 128), BF),
        V((own, 128), BF),
        V((nc, own, 128), BF),
        V((nr, own, 128), BF),
        V((ti, outer), BF),
        V((outer, ti), BF),
        V((outer * (ch + 8), 128), F32),
        V((ch, outer, 128), BF),
        V((3 * ch, 3 * ch), BF),
        V((3 * ch, 3 * ch), BF),
        V((outer, outer * ch), BF),
        V((outer * (ch + 8), 128), F32),
        V((3 * ch, 3 * ch), F32),
        V((6 * ch, 128), F32),
        V((nc, part, 128), F32),
        V((nr, part, 128), F32),
        V((nc, part, 128), F32),
        V((outer, ti), F32),
        V((nc, own, outer), F32),
        V((nr, own, outer), F32),
        V((nc, own, outer), F32),
        V((nr, own, outer), F32),
        dma((ch // 8 + 1,)),
        dma((nc + nr,)),
        dma((nc + nr,)),
        dma((2, 8)),
        dma((2, 8)),
        dma((2 * nc + nr,)),
        dma((2 * nc + nr,)),
        dma((nc + nr,)),
        dma((nc + nr,)),
    ]
    macs = ti * tj * (27 * ch * ch + 3 * outer * ch)
    out = pl.pallas_call(
        functools.partial(kernel, nr, nc, ch, ti, outer, comm, residues),
        out_shape=[
            V((ch, ti, tj), BF),
            V((ch, ti, tj), BF),
            V(((ti + 20) * (ch + 8), 128), F32),
            V((9, ch, ch), F32),
            V((own, feat), F32),
        ],
        in_specs=[any_spec, any_spec] + [vmem] * 5,
        out_specs=[vmem] * 5,
        scratch_shapes=scratch,
        compiler_params=pltpu.CompilerParams(
            collective_id=0 if comm else None,
            has_side_effects=True,
            vmem_limit_bytes=40 * 1024 * 1024,
        ),
        cost_estimate=pl.CostEstimate(
            flops=2 * macs, bytes_accessed=8 * ch * ti * tj, transcendentals=2 * ch * ti * tj
        ),
    )(cot, pair_map, features, lw.T, rw.T, ow, cw.reshape(9, ch, ch))
    kept = [pltpu.with_memory_space_constraint(x, pltpu.VMEM) for x in out]
    po, pg, wg, fg = pl.pallas_call(
        last_kernel,
        out_shape=[
            jax.ShapeDtypeStruct((ch, ti, tj), BF),
            jax.ShapeDtypeStruct((ch, ti, tj), BF),
            jax.ShapeDtypeStruct((9, ch, ch), F32),
            jax.ShapeDtypeStruct((own, feat), F32),
        ],
        in_specs=[vmem] * 5 + [smem],
        out_specs=[any_spec] * 4,
        scratch_shapes=[V((ch, ti, tj), BF), dma((6 + ti // BLOCK,))],
        compiler_params=pltpu.CompilerParams(vmem_limit_bytes=24 * 1024 * 1024),
        cost_estimate=pl.CostEstimate(
            flops=2 * ch * ti * tj, bytes_accessed=4 * ch * ti * tj, transcendentals=0
        ),
    )(*kept, bias)
    return po, pg, wg.reshape(3, 3, ch, ch), fg


def solution(mesh):
    nr, nc = mesh.shape["row"], mesh.shape["col"]

    def shards(pair_map, features, lw, rw, ow, cw, bias, cot):
        return call(
            nr, nc, pair_map.shape[1] * nr, True, pair_map, features, lw, rw, ow, cw, bias, cot
        )

    in_specs = (
        P(None, "row", "col"),
        P(("row", "col"), None),
        P(),
        P(),
        P(),
        P(),
        P(),
        P(None, "row", "col"),
    )
    out_specs = (P(None, "row", "col"), P(None, "row", "col"), P(), P(("row", "col"), None))
    return jax.shard_map(shards, mesh=mesh, in_specs=in_specs, out_specs=out_specs, check_vma=False)
```

```python
import functools
import math

import jax
import jax.numpy as jnp
from jax import lax
from jax.experimental import pallas as pl
from jax.experimental.pallas import tpu as pltpu
from jax.sharding import PartitionSpec as P

MESH = pl.DeviceIdType.MESH
BF = jnp.bfloat16
F32 = jnp.float32
NT = (((1,), (1,)), ((), ()))
PACK = 16
BLOCK = 32
STEP = 4


def dot(a, b, dims=None):
    if dims is None:
        return jnp.dot(a, b, preferred_element_type=F32)
    return lax.dot_general(a, b, dims, preferred_element_type=F32)


def kernel(
    nr, nc, ch, ti, outer, comm, residues,
    cot_hbm, pm_hbm, feat, lw, rw, ow, cw,
    hid_n, cot_n, gt, wg_out, fg_out,
    slope_n, wide, cot_t, act_t, hx, terms, even, odd, upd_even, upd_odd, packs, land_row, land_col,
    lr, left_in, right_in, left, left_t, mixf, mix, wf, wb, ow_q, ow_t, mgf,
    wg_acc, wgs, land_a, land_b, fin, lg_acc, lg_out, rg_out, land_l, land_r,
    in_sem, f_send, f_recv, h_send, h_recv, w_send, w_recv, g_send, g_recv,
):
    row = lax.axis_index("row")
    col = lax.axis_index("col")
    kg = ti // PACK
    ng = ti // 4
    pitch = ti + 8
    wch = ch + 8
    own = lr.shape[0]
    flat = row * nc + col
    goal = flat // nr
    slot = lax.rem(flat, nr)
    up, down = lax.rem(row + nr - 1, nr), lax.rem(row + 1, nr)
    west, east = lax.rem(col + nc - 1, nc), lax.rem(col + 1, nc)
    cstep = 8
    nchunk = ch // cstep

    cot_in = [
        pltpu.make_async_copy(
            cot_hbm.at[pl.ds(k * cstep, cstep)], cot_n.at[pl.ds(k * cstep, cstep)], in_sem.at[k]
        )
        for k in range(nchunk)
    ]
    pm_in = pltpu.make_async_copy(pm_hbm, hid_n, in_sem.at[nchunk])
    for copy in cot_in:
        copy.start()
    pm_in.start()

    def source(k):
        f = col * nr + k
        return f // nc, lax.rem(f, nc)

    if comm:
        barrier = pltpu.get_barrier_semaphore()

        def greet(r, c):
            pl.semaphore_signal(barrier, inc=1, device_id=(r, c), device_id_type=MESH)

        def greet_unless_me(r, c):
            @pl.when(jnp.logical_or(r != row, c != col))
            def _():
                greet(r, c)

        for d in range(1, nc):
            greet(row, lax.rem(col + d, nc))
        for d in range(1, nr):
            greet(lax.rem(row + d, nr), col)
        for r in (up, down):
            for c in (west, east):
                greet(r, c)
        for k in range(nr):
            greet_unless_me(k, goal)
            greet_unless_me(*source(k))
        total_greets = (nc - 1) + (nr - 1) + 4 + 2 * nr - jnp.where(goal == col, 2, 0)

    lr[...] = jnp.concatenate(
        [dot(feat[...], lw[...], NT), dot(feat[...], rw[...], NT), jnp.zeros((own, 128 - 2 * outer), F32)],
        axis=1,
    ).astype(BF)

    def remote(src, dst, ssem, rsem, dev):
        return pltpu.make_async_remote_copy(
            src_ref=src, dst_ref=dst, send_sem=ssem, recv_sem=rsem, device_id=dev, device_id_type=MESH
        )

    left_in[col] = lr[...]
    left_moves, right_moves = [], []
    if comm:
        pl.semaphore_wait(barrier, total_greets)
        for d in range(1, nc):
            move = remote(
                lr, left_in.at[col], f_send.at[d], f_recv.at[d], (row, lax.rem(col + d, nc))
            )
            move.start()
            left_moves.append(move)
        for k in range(nr):
            me = jnp.logical_and(row == k, goal == col)
            far = remote(
                lr, right_in.at[slot], f_send.at[nc + k], f_recv.at[nc + slot], (k, goal)
            )
            near = pltpu.make_async_copy(lr, right_in.at[slot], f_recv.at[nc + slot])

            @pl.when(me)
            def _():
                near.start()

            @pl.when(jnp.logical_not(me))
            def _():
                far.start()

            right_moves.append((me, far))

    for a in range(3):
        wf[a * ch : (a + 1) * ch, :] = jnp.concatenate([cw[3 * a + b] for b in range(3)], axis=1)
        wb[a * ch : (a + 1) * ch, :] = jnp.concatenate(
            [cw[3 * a + b].astype(F32).T for b in range(3)], axis=1
        ).astype(BF)
    ow_q[...] = jnp.concatenate([ow[p] for p in range(outer)], axis=1)
    step = 512
    for k in range(outer * ch // step):
        ow_t[k * step : (k + 1) * step, :] = ow_q[:, k * step : (k + 1) * step].astype(F32).T.astype(BF)

    def p_widen():
        for k in range(nchunk):
            cot_in[k].wait()

            @pl.loop(0, cstep, unroll=2)
            def _(c):
                at = pl.multiple_of((k * cstep + c) * pitch, 8)
                wide[pl.ds(at, ti), :] = cot_n[k * cstep + c].astype(F32)

    p_widen()

    lane = lax.broadcasted_iota(jnp.int32, (ch, 128), 1)
    window = lax.rem(lane + 4, 128) // 8

    def to_rows(dst, first, which, read):
        @pl.loop(0, kg, unroll=2)
        def _(k):
            packed = None
            for m in range(PACK):
                row_at = PACK * k + m
                x = read(row_at).astype(BF)
                dst[first + row_at] = x
                packed = x if m == 0 else jnp.where(window == m, pltpu.roll(x, 8 * m, 1), packed)
            packs[which, k] = packed

    def halo_moves(src, first, which):
        edges = packs.at[which]
        from_west, from_east = land_col.at[which, 0], land_col.at[which, 1]
        plan = [
            (src.at[pl.ds(first, 4)], land_row.at[which, 1], (up, col)),
            (src.at[pl.ds(first + ti - 4, 4)], land_row.at[which, 0], (down, col)),
            (edges, from_east.at[pl.ds(1, kg)], (row, west)),
            (edges, from_west.at[pl.ds(1, kg)], (row, east)),
            (edges.at[0], from_east.at[kg + 1], (up, west)),
            (edges.at[0], from_west.at[kg + 1], (up, east)),
            (edges.at[kg - 1], from_east.at[0], (down, west)),
            (edges.at[kg - 1], from_west.at[0], (down, east)),
        ]
        return [
            remote(s, d, h_send.at[which, m], h_recv.at[which, m], dev)
            for m, (s, d, dev) in enumerate(plan)
        ]

    to_rows(cot_t, 4, 0, lambda i: wide[pl.ds(i, ch, stride=pitch), :])
    cot_moves = halo_moves(cot_t, 4, 0)
    if comm:
        for move in cot_moves:
            move.start()

    if comm:
        for d in range(1, nc):
            left_moves[d - 1].wait_recv()
        for k in range(nr):
            pltpu.make_async_copy(lr, right_in.at[k], f_recv.at[nc + k]).wait()
    left[...] = left_in[...].reshape(nc * own, 128)[:, :outer]
    left_t[...] = left[...].astype(F32).T.astype(BF)
    right = right_in[...].reshape(nr * own, 128)[:, outer : 2 * outer]
    for k in range(outer * ch // step):
        rows = dot(ow_t[k * step : (k + 1) * step, :], right, NT).astype(BF).astype(F32)
        for m in range(step // ch):
            at = (k * (step // ch) + m) * wch
            mixf[at : at + ch, :] = rows[m * ch : (m + 1) * ch]

    @pl.loop(0, ch, unroll=8)
    def _(c):
        mix[c] = mixf[pl.ds(c, outer, stride=wch), :].astype(BF)

    pm_in.wait()

    def p_hidden():
        def update(c):
            return dot(left[...], jnp.concatenate([mix[c], mix[c + 1]], axis=1))

        def finish(c, change):
            for k in range(2):
                hidden = (hid_n[c + k].astype(F32) + change[:, 128 * k : 128 * (k + 1)]).astype(BF)
                hid_n[c + k] = hidden
                h = hidden.astype(F32)
                e = jnp.minimum(jnp.exp(h), 1.0)
                slope_n[c + k] = e.astype(BF)
                wide[pl.ds(c + k, ti, stride=wch), :] = jnp.maximum(h, e - 1.0)

        upd_even[...] = update(0)

        @pl.loop(0, ch, step=4)
        def _(c):
            upd_odd[...] = update(c + 2)
            finish(c, upd_even[...])
            upd_even[...] = update(jnp.minimum(c + 4, ch - 2))
            finish(c + 2, upd_odd[...])

    p_hidden()

    to_rows(act_t, 8, 1, lambda i: wide[pl.ds(pl.multiple_of(i * wch, 8), ch), :])
    for s in (0, 4, ti + 8, ti + 12):
        act_t[s : s + 4] = jnp.zeros((4, ch, 128), BF)
    act_moves = halo_moves(act_t, 8, 1)
    if comm:
        for move in act_moves:
            move.start()

    has_up, has_down, has_west, has_east = row > 0, row < nr - 1, col > 0, col < nc - 1

    def keep(ok, x):
        return jnp.where(ok, x, jnp.zeros_like(x))

    def unpack_edges(dst, first, which):
        dst[first : first + 4] = keep(has_up, land_row[which, 0])
        dst[first + ti + 4 : first + ti + 8] = keep(has_down, land_row[which, 1])

        def place(k, ok):
            from_west = keep(jnp.logical_and(ok, has_west), land_col[which, 0, k])
            from_east = keep(jnp.logical_and(ok, has_east), land_col[which, 1, k])
            hx[k] = jnp.where(
                lax.rem(lane, 8) < 4, pltpu.roll(from_west, 4, 1), pltpu.roll(from_east, 124, 1)
            )

        place(0, has_up)
        place(kg + 1, has_down)

        @pl.loop(1, kg + 1, unroll=4)
        def _(k):
            place(k, True)

    def fill(dst, src, first, n, q, turned):
        for r in range(8):
            x = src[first + 16 * n + q + r]
            at = q + r + PACK - 4
            edge = pltpu.roll(hx[n + at // PACK], (PACK - at % PACK) % PACK * 8, 1)
            before = jnp.where(lane < 4, edge, pltpu.roll(x, 4, 1))
            after = jnp.where(lane >= 124, edge, pltpu.roll(x, 124, 1))
            lanes = slice(128 * r, 128 * (r + 1))
            dst[:ch, lanes] = after if turned else before
            dst[ch : 2 * ch, lanes] = x
            dst[2 * ch :, lanes] = before if turned else after

    def halves(x):
        return [x[:, :512], x[:, 512:]]

    def spread(parts, g, order):
        for s in range(len(parts) + 2):
            terms = [
                parts[s - k][a * ch : (a + 1) * ch]
                for k, a in enumerate(order)
                if 0 <= s - k < len(parts)
            ]
            total = terms[0]
            for term in terms[1:]:
                total = total + term
            for r in range(4):
                at = pl.ds(pl.multiple_of((4 * (g + s) + r) * wch, 8), ch)
                term = total[:, 128 * r : 128 * (r + 1)]
                gt[at, :] = gt[at, :] + term if s < 2 else term

    if comm:
        for move in cot_moves:
            move.wait_recv()
    unpack_edges(cot_t, 0, 0)
    gt[: 8 * wch] = jnp.zeros((8 * wch, 128), F32)
    wg_acc[...] = jnp.zeros_like(wg_acc)

    def p_kernel():
        fill(terms.at[0], cot_t, 0, 0, 0, True)

        def acts(first):
            return jnp.concatenate(
                [
                    jnp.concatenate([act_t[first + 4 * a + r] for r in range(8)], axis=1)
                    for a in range(3)
                ],
                axis=0,
            )

        @pl.loop(0, ti // 16, step=STEP)
        def _(n):
            grad = 0
            for m in range(n_chunks):
                j = 2 * n + m
                grad = grad + dot(terms[j], acts(8 * j), NT)
                fill(terms.at[j + 1], cot_t, 0, n + (m + 1) // 2, 8 * ((m + 1) % 2), True)
            wg_acc[...] += grad

        wg_acc[...] += dot(terms[ti // 8], acts(ti), NT)

    def p_back():
        @pl.loop(0, ti // 16, step=STEP)
        def _(n):
            parts = []
            for m in range(n_chunks):
                parts += halves(dot(wb[...], terms[2 * n + m]))
            spread(parts, 4 * n, (0, 1, 2))

        spread(halves(dot(wb[...], terms[ti // 8])), ng, (0, 1, 2))

    n_chunks = 2 * STEP
    p_kernel()

    part = 2 * 3 * ch // nc
    wgs[: 3 * ch] = wg_acc[:, :128]
    wgs[3 * ch :] = jnp.concatenate([wg_acc[:, 128:], jnp.zeros((3 * ch, 256 - 3 * ch), F32)], axis=1)
    land_a[col] = wgs[pl.ds(pl.multiple_of(col * part, 8), part)]
    a_moves, b_moves, c_moves, l_moves, r_moves = [], [], [], [], []
    if comm:
        for d in range(1, nc):
            other = lax.rem(col + d, nc)
            move = remote(
                wgs.at[pl.ds(pl.multiple_of(other * part, 8), part)],
                land_a.at[col], w_send.at[d], w_recv.at[d], (row, other),
            )
            move.start()
            a_moves.append(move)

    p_back()

    if comm:
        for move in a_moves:
            move.wait_recv()
    total = land_a[0]
    for k in range(1, nc):
        total = total + land_a[k]
    land_b[row] = total
    if comm:
        for d in range(1, nr):
            move = remote(
                land_b.at[row], land_b.at[row], w_send.at[nc + d], w_recv.at[nc + d],
                (lax.rem(row + d, nr), col),
            )
            move.start()
            b_moves.append(move)

    lg_acc[...] = jnp.zeros_like(lg_acc)

    def p_grad():
        @pl.loop(0, ch, step=8)
        def _(c):
            lg = 0
            for half in (c, c + 4):
                grads = []
                for m in range(4):
                    g = gt[pl.ds(8 * wch + half + m, ti, stride=wch), :]
                    pg = (cot_n[half + m].astype(F32) + g * slope_n[half + m].astype(F32)).astype(BF)
                    cot_n[half + m] = pg
                    grads.append(pg)
                grads = jnp.concatenate(grads, axis=1)
                mixes = jnp.concatenate([mix[half + m] for m in range(4)], axis=1)
                lg = lg + dot(mixes, grads, NT)
                mg = dot(left_t[...], grads)
                for m in range(4):
                    mgf[pl.ds(half + m, outer, stride=wch), :] = mg[:, 128 * m : 128 * (m + 1)]
            lg_acc[...] += lg

    p_grad()

    mg = jnp.concatenate([mgf[p * wch : p * wch + ch, :] for p in range(outer)], axis=0)
    mg_hi = mg.astype(BF)
    mg_lo = (mg - mg_hi.astype(F32)).astype(BF)
    rg = (dot(ow_q[...], mg_hi) + dot(ow_q[...], mg_lo)).T
    rg_out[...] = rg.reshape(nr, own, outer)
    lg_out[...] = lg_acc[...].T.reshape(nc, own, outer)
    land_l[col] = lg_out[col]
    if comm:
        for d in range(1, nc):
            other = lax.rem(col + d, nc)
            move = remote(lg_out.at[other], land_l.at[col], g_send.at[d], g_recv.at[d], (row, other))
            move.start()
            l_moves.append(move)
        for k in range(nr):
            r, c = source(k)
            me = jnp.logical_and(r == row, c == col)
            far = remote(
                rg_out.at[k], land_r.at[row], g_send.at[nc + k], g_recv.at[nc + row], (r, c)
            )
            near = pltpu.make_async_copy(rg_out.at[k], land_r.at[row], g_recv.at[nc + row])

            @pl.when(me)
            def _():
                near.start()

            @pl.when(jnp.logical_not(me))
            def _():
                far.start()

            r_moves.append((me, far))
        for move in b_moves:
            move.wait_recv()
    total = land_b[0]
    for m in range(1, nr):
        total = total + land_b[m]
    fin[col] = total * (1.0 / residues)
    if comm:
        for d in range(1, nc):
            move = remote(
                fin.at[col], fin.at[col], w_send.at[nc + nr + d], w_recv.at[nc + nr + d],
                (row, lax.rem(col + d, nc)),
            )
            move.start()
            c_moves.append(move)
        for move in act_moves:
            move.wait_recv()
    unpack_edges(act_t, 4, 1)
    gt[: 8 * wch] = jnp.zeros((8 * wch, 128), F32)

    fill(even, act_t, 4, 0, 0, False)

    def p_forward(first, last):
        @pl.loop(first, last, step=STEP)
        def _(n):
            parts = []
            for m in range(STEP):
                parts += halves(dot(wf[...], even[...]))
                fill(odd, act_t, 4, n + m, 8, False)
                parts += halves(dot(wf[...], odd[...]))
                fill(even, act_t, 4, n + m, 16, False)
            spread(parts, 4 * n, (2, 1, 0))

    p_forward(0, ti // 16)
    spread(halves(dot(wf[...], even[...])), ng, (2, 1, 0))

    if comm:
        for move in l_moves:
            move.wait_recv()
        for k in range(nr):
            pltpu.make_async_copy(rg_out.at[k], land_r.at[k], g_recv.at[nc + k]).wait()
    lg = land_l[0]
    for k in range(1, nc):
        lg = lg + land_l[k]
    rg = land_r[0]
    for k in range(1, nr):
        rg = rg + land_r[k]

    def exact(x, w):
        total = jnp.zeros((own, w.shape[1]), F32)
        for _ in range(3):
            head = x.astype(BF)
            total = total + dot(head, w)
            x = x - head.astype(F32)
        return total

    fg_out[...] = (exact(lg, lw[...]) + exact(rg, rw[...])) * (1.0 / math.sqrt(residues))

    if comm:
        for move in c_moves:
            move.wait_recv()
    whole = fin[...].reshape(6 * ch, 128)
    for a in range(3):
        for b in range(3):
            base = 3 * ch * (a // 2) + b * ch
            at = ch * (a % 2)
            wg_out[3 * a + b] = whole[base : base + ch, at : at + ch]

    if comm:
        for move in left_moves + cot_moves + act_moves + a_moves + b_moves + c_moves + l_moves:
            move.wait_send()
        for me, far in right_moves + r_moves:

            @pl.when(jnp.logical_not(me))
            def _():
                far.wait_send()


def last_kernel(
    hid_n, pg_n, gt, wg_in, fg_in, bias, po_hbm, pg_hbm, wg_hbm, fg_hbm, out_n, out_sem
):
    ch, ti, _ = hid_n.shape
    wch = ch + 8
    step = ch // 4
    copies = [
        pltpu.make_async_copy(
            pg_n.at[pl.ds(k * step, step)], pg_hbm.at[pl.ds(k * step, step)], out_sem.at[k]
        )
        for k in range(4)
    ]
    copies.append(pltpu.make_async_copy(wg_in, wg_hbm, out_sem.at[4]))
    copies.append(pltpu.make_async_copy(fg_in, fg_hbm, out_sem.at[5]))
    for copy in copies:
        copy.start()
    for k in range(ti // BLOCK):

        @pl.loop(0, ch, unroll=16)
        def _(c):
            conv = gt[pl.ds((8 + BLOCK * k) * wch + c, BLOCK, stride=wch), :]
            h = hid_n[c, pl.ds(BLOCK * k, BLOCK), :].astype(F32)
            out_n[c, pl.ds(BLOCK * k, BLOCK), :] = (h + bias[c] + conv).astype(BF)

        copy = pltpu.make_async_copy(
            out_n.at[:, pl.ds(BLOCK * k, BLOCK)], po_hbm.at[:, pl.ds(BLOCK * k, BLOCK)],
            out_sem.at[6 + k],
        )
        copy.start()
        copies.append(copy)
    for copy in copies:
        copy.wait()


def call(nr, nc, residues, comm, pair_map, features, lw, rw, ow, cw, bias, cot):
    ch, ti, tj = pair_map.shape
    own, feat = features.shape
    outer = lw.shape[1]
    kg = ti // PACK
    part = 6 * ch // nc
    any_spec = pl.BlockSpec(memory_space=pl.ANY)
    vmem = pl.BlockSpec(memory_space=pltpu.VMEM)
    smem = pl.BlockSpec(memory_space=pltpu.SMEM)
    V = pltpu.VMEM
    dma = pltpu.SemaphoreType.DMA
    scratch = [
        V((ch, ti, tj), BF),
        V((max(ch * (ti + 8), ti * (ch + 8)), 128), F32),
        V((ti + 8, ch, 128), BF),
        V((ti + 16, ch, 128), BF),
        V((kg + 2, ch, 128), BF),
        V((ti // 8 + 1, 3 * ch, 1024), BF),
        V((3 * ch, 1024), BF),
        V((3 * ch, 1024), BF),
        V((ti, 256), F32),
        V((ti, 256), F32),
        V((2, kg, ch, 128), BF),
        V((2, 2, 4, ch, 128), BF),
        V((2, 2, kg + 2, ch, 128), BF),
        V((own, 128), BF),
        V((nc, own, 128), BF),
        V((nr, own, 128), BF),
        V((ti, outer), BF),
        V((outer, ti), BF),
        V((outer * (ch + 8), 128), F32),
        V((ch, outer, 128), BF),
        V((3 * ch, 3 * ch), BF),
        V((3 * ch, 3 * ch), BF),
        V((outer, outer * ch), BF),
        V((outer * ch, outer), BF),
        V((outer * (ch + 8), 128), F32),
        V((3 * ch, 3 * ch), F32),
        V((6 * ch, 128), F32),
        V((nc, part, 128), F32),
        V((nr, part, 128), F32),
        V((nc, part, 128), F32),
        V((outer, ti), F32),
        V((nc, own, outer), F32),
        V((nr, own, outer), F32),
        V((nc, own, outer), F32),
        V((nr, own, outer), F32),
        dma((ch // 8 + 1,)),
        dma((nc + nr,)),
        dma((nc + nr,)),
        dma((2, 8)),
        dma((2, 8)),
        dma((2 * nc + nr,)),
        dma((2 * nc + nr,)),
        dma((nc + nr,)),
        dma((nc + nr,)),
    ]
    macs = ti * tj * (27 * ch * ch + 3 * outer * ch)
    out = pl.pallas_call(
        functools.partial(kernel, nr, nc, ch, ti, outer, comm, residues),
        out_shape=[
            V((ch, ti, tj), BF),
            V((ch, ti, tj), BF),
            V(((ti + 20) * (ch + 8), 128), F32),
            V((9, ch, ch), F32),
            V((own, feat), F32),
        ],
        in_specs=[any_spec, any_spec] + [vmem] * 5,
        out_specs=[vmem] * 5,
        scratch_shapes=scratch,
        compiler_params=pltpu.CompilerParams(
            collective_id=0 if comm else None,
            has_side_effects=True,
            vmem_limit_bytes=44 * 1024 * 1024,
        ),
        cost_estimate=pl.CostEstimate(
            flops=2 * macs, bytes_accessed=8 * ch * ti * tj, transcendentals=2 * ch * ti * tj
        ),
    )(cot, pair_map, features, lw.T, rw.T, ow, cw.reshape(9, ch, ch))
    kept = [pltpu.with_memory_space_constraint(x, pltpu.VMEM) for x in out]
    po, pg, wg, fg = pl.pallas_call(
        last_kernel,
        out_shape=[
            jax.ShapeDtypeStruct((ch, ti, tj), BF),
            jax.ShapeDtypeStruct((ch, ti, tj), BF),
            jax.ShapeDtypeStruct((9, ch, ch), F32),
            jax.ShapeDtypeStruct((own, feat), F32),
        ],
        in_specs=[vmem] * 5 + [smem],
        out_specs=[any_spec] * 4,
        scratch_shapes=[V((ch, ti, tj), BF), dma((6 + ti // BLOCK,))],
        compiler_params=pltpu.CompilerParams(vmem_limit_bytes=24 * 1024 * 1024),
        cost_estimate=pl.CostEstimate(
            flops=2 * ch * ti * tj, bytes_accessed=4 * ch * ti * tj, transcendentals=0
        ),
    )(*kept, bias)
    return po, pg, wg.reshape(3, 3, ch, ch), fg


def solution(mesh):
    nr, nc = mesh.shape["row"], mesh.shape["col"]

    def shards(pair_map, features, lw, rw, ow, cw, bias, cot):
        return call(
            nr, nc, pair_map.shape[1] * nr, True, pair_map, features, lw, rw, ow, cw, bias, cot
        )

    in_specs = (
        P(None, "row", "col"),
        P(("row", "col"), None),
        P(),
        P(),
        P(),
        P(),
        P(),
        P(None, "row", "col"),
    )
    out_specs = (P(None, "row", "col"), P(None, "row", "col"), P(), P(("row", "col"), None))
    return jax.shard_map(shards, mesh=mesh, in_specs=in_specs, out_specs=out_specs, check_vma=False)
```

```python
import functools
import math

import jax
import jax.numpy as jnp
from jax import lax
from jax.experimental import pallas as pl
from jax.experimental.pallas import tpu as pltpu
from jax.sharding import PartitionSpec as P

MESH = pl.DeviceIdType.MESH
BF = jnp.bfloat16
F32 = jnp.float32
NT = (((1,), (1,)), ((), ()))
PACK = 16
BLOCK = 32
STEP = 4


def dot(a, b, dims=None):
    if dims is None:
        return jnp.dot(a, b, preferred_element_type=F32)
    return lax.dot_general(a, b, dims, preferred_element_type=F32)


def kernel(
    nr, nc, ch, ti, outer, comm, residues,
    cot_hbm, pm_hbm, feat, lw, rw, ow, cw,
    hid_n, cot_n, gt, wg_out, fg_out,
    slope_n, wide, cot_t, act_t, hx, terms, even, odd, upd_even, upd_odd, packs, land_row, land_col,
    lr, left_in, right_in, left, left_t, mixf, mix, wf, wb, ow_q, ow_t, mgf,
    wg_acc, wgs, land_a, land_b, fin, lg_acc, lg_out, rg_out, land_l, land_r,
    in_sem, f_send, f_recv, h_send, h_recv, w_send, w_recv, g_send, g_recv,
):
    row = lax.axis_index("row")
    col = lax.axis_index("col")
    kg = ti // PACK
    ng = ti // 4
    pitch = ti + 8
    wch = ch + 8
    own = lr.shape[0]
    flat = row * nc + col
    goal = flat // nr
    slot = lax.rem(flat, nr)
    up, down = lax.rem(row + nr - 1, nr), lax.rem(row + 1, nr)
    west, east = lax.rem(col + nc - 1, nc), lax.rem(col + 1, nc)
    cstep = 8
    nchunk = ch // cstep

    cot_in = [
        pltpu.make_async_copy(
            cot_hbm.at[pl.ds(k * cstep, cstep)], cot_n.at[pl.ds(k * cstep, cstep)], in_sem.at[k]
        )
        for k in range(nchunk)
    ]
    pm_in = pltpu.make_async_copy(pm_hbm, hid_n, in_sem.at[nchunk])
    for copy in cot_in:
        copy.start()
    pm_in.start()

    def source(k):
        f = col * nr + k
        return f // nc, lax.rem(f, nc)

    if comm:
        barrier = pltpu.get_barrier_semaphore()

        def greet(r, c):
            pl.semaphore_signal(barrier, inc=1, device_id=(r, c), device_id_type=MESH)

        def greet_unless_me(r, c):
            @pl.when(jnp.logical_or(r != row, c != col))
            def _():
                greet(r, c)

        for d in range(1, nc):
            greet(row, lax.rem(col + d, nc))
        for d in range(1, nr):
            greet(lax.rem(row + d, nr), col)
        for r in (up, down):
            for c in (west, east):
                greet(r, c)
        for k in range(nr):
            greet_unless_me(k, goal)
            greet_unless_me(*source(k))
        total_greets = (nc - 1) + (nr - 1) + 4 + 2 * nr - jnp.where(goal == col, 2, 0)

    lr[...] = jnp.concatenate(
        [dot(feat[...], lw[...], NT), dot(feat[...], rw[...], NT), jnp.zeros((own, 128 - 2 * outer), F32)],
        axis=1,
    ).astype(BF)

    def remote(src, dst, ssem, rsem, dev):
        return pltpu.make_async_remote_copy(
            src_ref=src, dst_ref=dst, send_sem=ssem, recv_sem=rsem, device_id=dev, device_id_type=MESH
        )

    left_in[col] = lr[...]
    left_moves, right_moves = [], []
    if comm:
        pl.semaphore_wait(barrier, total_greets)
        for d in range(1, nc):
            move = remote(
                lr, left_in.at[col], f_send.at[d], f_recv.at[d], (row, lax.rem(col + d, nc))
            )
            move.start()
            left_moves.append(move)
        for k in range(nr):
            me = jnp.logical_and(row == k, goal == col)
            far = remote(
                lr, right_in.at[slot], f_send.at[nc + k], f_recv.at[nc + slot], (k, goal)
            )
            near = pltpu.make_async_copy(lr, right_in.at[slot], f_recv.at[nc + slot])

            @pl.when(me)
            def _():
                near.start()

            @pl.when(jnp.logical_not(me))
            def _():
                far.start()

            right_moves.append((me, far))

    for a in range(3):
        wf[a * ch : (a + 1) * ch, :] = jnp.concatenate([cw[3 * a + b] for b in range(3)], axis=1)
        wb[a * ch : (a + 1) * ch, :] = jnp.concatenate(
            [cw[3 * a + b].astype(F32).T for b in range(3)], axis=1
        ).astype(BF)
    ow_q[...] = jnp.concatenate([ow[p] for p in range(outer)], axis=1)
    step = 512
    for k in range(outer * ch // step):
        ow_t[k * step : (k + 1) * step, :] = ow_q[:, k * step : (k + 1) * step].astype(F32).T.astype(BF)

    def p_widen():
        for k in range(nchunk):
            cot_in[k].wait()

            @pl.loop(0, cstep, unroll=2)
            def _(c):
                at = pl.multiple_of((k * cstep + c) * pitch, 8)
                wide[pl.ds(at, ti), :] = cot_n[k * cstep + c].astype(F32)

    p_widen()

    lane = lax.broadcasted_iota(jnp.int32, (ch, 128), 1)
    window = lax.rem(lane + 4, 128) // 8

    def to_rows(dst, first, which, read):
        @pl.loop(0, kg, unroll=2)
        def _(k):
            packed = None
            for m in range(PACK):
                row_at = PACK * k + m
                x = read(row_at).astype(BF)
                dst[first + row_at] = x
                packed = x if m == 0 else jnp.where(window == m, pltpu.roll(x, 8 * m, 1), packed)
            packs[which, k] = packed

    def halo_moves(src, first, which):
        edges = packs.at[which]
        from_west, from_east = land_col.at[which, 0], land_col.at[which, 1]
        plan = [
            (src.at[pl.ds(first, 4)], land_row.at[which, 1], (up, col)),
            (src.at[pl.ds(first + ti - 4, 4)], land_row.at[which, 0], (down, col)),
            (edges, from_east.at[pl.ds(1, kg)], (row, west)),
            (edges, from_west.at[pl.ds(1, kg)], (row, east)),
            (edges.at[0], from_east.at[kg + 1], (up, west)),
            (edges.at[0], from_west.at[kg + 1], (up, east)),
            (edges.at[kg - 1], from_east.at[0], (down, west)),
            (edges.at[kg - 1], from_west.at[0], (down, east)),
        ]
        return [
            remote(s, d, h_send.at[which, m], h_recv.at[which, m], dev)
            for m, (s, d, dev) in enumerate(plan)
        ]

    to_rows(cot_t, 4, 0, lambda i: wide[pl.ds(i, ch, stride=pitch), :])
    cot_moves = halo_moves(cot_t, 4, 0)
    if comm:
        for move in cot_moves:
            move.start()

    if comm:
        for d in range(1, nc):
            left_moves[d - 1].wait_recv()
        for k in range(nr):
            pltpu.make_async_copy(lr, right_in.at[k], f_recv.at[nc + k]).wait()
    left[...] = left_in[...].reshape(nc * own, 128)[:, :outer]
    left_t[...] = left[...].astype(F32).T.astype(BF)
    right = right_in[...].reshape(nr * own, 128)[:, outer : 2 * outer]
    for k in range(outer * ch // step):
        rows = dot(ow_t[k * step : (k + 1) * step, :], right, NT).astype(BF).astype(F32)
        for m in range(step // ch):
            at = (k * (step // ch) + m) * wch
            mixf[at : at + ch, :] = rows[m * ch : (m + 1) * ch]

    @pl.loop(0, ch, unroll=8)
    def _(c):
        mix[c] = mixf[pl.ds(c, outer, stride=wch), :].astype(BF)

    pm_in.wait()

    def p_hidden():
        def update(c):
            return dot(left[...], jnp.concatenate([mix[c], mix[c + 1]], axis=1))

        def finish(c, change):
            for k in range(2):
                hidden = (hid_n[c + k].astype(F32) + change[:, 128 * k : 128 * (k + 1)]).astype(BF)
                hid_n[c + k] = hidden
                h = hidden.astype(F32)
                e = jnp.minimum(jnp.exp(h), 1.0)
                slope_n[c + k] = e.astype(BF)
                wide[pl.ds(c + k, ti, stride=wch), :] = jnp.maximum(h, e - 1.0)

        upd_even[...] = update(0)

        @pl.loop(0, ch, step=4)
        def _(c):
            upd_odd[...] = update(c + 2)
            finish(c, upd_even[...])
            upd_even[...] = update(jnp.minimum(c + 4, ch - 2))
            finish(c + 2, upd_odd[...])

    p_hidden()

    to_rows(act_t, 8, 1, lambda i: wide[pl.ds(pl.multiple_of(i * wch, 8), ch), :])
    for s in (0, 4, ti + 8, ti + 12):
        act_t[s : s + 4] = jnp.zeros((4, ch, 128), BF)
    act_moves = halo_moves(act_t, 8, 1)
    if comm:
        for move in act_moves:
            move.start()

    has_up, has_down, has_west, has_east = row > 0, row < nr - 1, col > 0, col < nc - 1

    def keep(ok, x):
        return jnp.where(ok, x, jnp.zeros_like(x))

    def unpack_edges(dst, first, which):
        dst[first : first + 4] = keep(has_up, land_row[which, 0])
        dst[first + ti + 4 : first + ti + 8] = keep(has_down, land_row[which, 1])

        def place(k, ok):
            from_west = keep(jnp.logical_and(ok, has_west), land_col[which, 0, k])
            from_east = keep(jnp.logical_and(ok, has_east), land_col[which, 1, k])
            hx[k] = jnp.where(
                lax.rem(lane, 8) < 4, pltpu.roll(from_west, 4, 1), pltpu.roll(from_east, 124, 1)
            )

        place(0, has_up)
        place(kg + 1, has_down)

        @pl.loop(1, kg + 1, unroll=4)
        def _(k):
            place(k, True)

    def fill(dst, src, first, n, q, turned):
        for r in range(8):
            x = src[first + 16 * n + q + r]
            at = q + r + PACK - 4
            edge = pltpu.roll(hx[n + at // PACK], (PACK - at % PACK) % PACK * 8, 1)
            before = jnp.where(lane < 4, edge, pltpu.roll(x, 4, 1))
            after = jnp.where(lane >= 124, edge, pltpu.roll(x, 124, 1))
            lanes = slice(128 * r, 128 * (r + 1))
            dst[:ch, lanes] = after if turned else before
            dst[ch : 2 * ch, lanes] = x
            dst[2 * ch :, lanes] = before if turned else after

    def halves(x):
        return [x[:, :512], x[:, 512:]]

    def spread(parts, g, order):
        for s in range(len(parts) + 2):
            terms = [
                parts[s - k][a * ch : (a + 1) * ch]
                for k, a in enumerate(order)
                if 0 <= s - k < len(parts)
            ]
            total = terms[0]
            for term in terms[1:]:
                total = total + term
            for r in range(4):
                at = pl.ds(pl.multiple_of((4 * (g + s) + r) * wch, 8), ch)
                term = total[:, 128 * r : 128 * (r + 1)]
                gt[at, :] = gt[at, :] + term if s < 2 else term

    if comm:
        for move in cot_moves:
            move.wait_recv()
    unpack_edges(cot_t, 0, 0)
    gt[: 8 * wch] = jnp.zeros((8 * wch, 128), F32)
    wg_acc[...] = jnp.zeros_like(wg_acc)

    def p_kernel():
        fill(terms.at[0], cot_t, 0, 0, 0, True)

        def acts(first):
            return jnp.concatenate(
                [
                    jnp.concatenate([act_t[first + 4 * a + r] for r in range(8)], axis=1)
                    for a in range(3)
                ],
                axis=0,
            )

        @pl.loop(0, ti // 16, step=STEP)
        def _(n):
            grad = 0
            for m in range(n_chunks):
                j = 2 * n + m
                grad = grad + dot(terms[j], acts(8 * j), NT)
                fill(terms.at[j + 1], cot_t, 0, n + (m + 1) // 2, 8 * ((m + 1) % 2), True)
            wg_acc[...] += grad

        wg_acc[...] += dot(terms[ti // 8], acts(ti), NT)

    def p_back():
        @pl.loop(0, ti // 16, step=STEP)
        def _(n):
            parts = []
            for m in range(n_chunks):
                parts += halves(dot(wb[...], terms[2 * n + m]))
            spread(parts, 4 * n, (0, 1, 2))

        spread(halves(dot(wb[...], terms[ti // 8])), ng, (0, 1, 2))

    n_chunks = 2 * STEP
    p_kernel()

    taps = 9
    owners = [min(2 * k, nc - 1) for k in range(taps)]
    is_owner = functools.reduce(jnp.logical_or, [col == c for c in owners])
    mine = jnp.where(col == owners[-1], taps - 1, col // 2)
    half = ch // 2
    for k in range(taps):
        a, b = k // 3, k % 3
        tap = wg_acc[b * ch : (b + 1) * ch, a * ch : (a + 1) * ch]
        wgs[k] = jnp.concatenate([tap[:half], tap[half:]], axis=1).astype(BF)
    a_moves, b_moves, c_moves, l_moves, r_moves = [], [], [], [], []
    for k, c in enumerate(owners):
        move = remote(wgs.at[k], land_a.at[col], w_send.at[k], w_recv.at[col], (row, c))

        @pl.when(col == c)
        def _():
            land_a[col] = wgs[k]

        if comm:

            @pl.when(col != c)
            def _():
                move.start()

            a_moves.append((c, move))

    p_back()

    def each(refs):
        total = refs[0].astype(F32)
        for k in range(1, refs.shape[0]):
            total = total + refs[k].astype(F32)
        return total

    for d in range(1, nr):
        b_moves.append(
            remote(
                land_b.at[row], land_b.at[row], w_send.at[taps + d], w_recv.at[nc + d],
                (lax.rem(row + d, nr), col),
            )
        )
    for d in range(1, nc):
        c_moves.append(
            remote(
                fin.at[mine], fin.at[mine], w_send.at[taps + nr + d], w_recv.at[nc + nr + mine],
                (row, lax.rem(col + d, nc)),
            )
        )

    @pl.when(is_owner)
    def _():
        if comm:
            for c in range(nc):

                @pl.when(col != c)
                def _():
                    pltpu.make_async_copy(wgs.at[0], land_a.at[c], w_recv.at[c]).wait()

        land_b[row] = each(land_a)
        if comm:
            for move in b_moves:
                move.start()

    lg_acc[...] = jnp.zeros_like(lg_acc)

    def p_grad():
        @pl.loop(0, ch, step=8)
        def _(c):
            lg = 0
            for half in (c, c + 4):
                grads = []
                for m in range(4):
                    g = gt[pl.ds(8 * wch + half + m, ti, stride=wch), :]
                    pg = (cot_n[half + m].astype(F32) + g * slope_n[half + m].astype(F32)).astype(BF)
                    cot_n[half + m] = pg
                    grads.append(pg)
                grads = jnp.concatenate(grads, axis=1)
                mixes = jnp.concatenate([mix[half + m] for m in range(4)], axis=1)
                lg = lg + dot(mixes, grads, NT)
                mg = dot(left_t[...], grads)
                for m in range(4):
                    mgf[pl.ds(half + m, outer, stride=wch), :] = mg[:, 128 * m : 128 * (m + 1)]
            lg_acc[...] += lg

    p_grad()

    mg = jnp.concatenate([mgf[p * wch : p * wch + ch, :] for p in range(outer)], axis=0)
    mg_hi = mg.astype(BF)
    mg_lo = (mg - mg_hi.astype(F32)).astype(BF)
    rg = (dot(ow_q[...], mg_hi) + dot(ow_q[...], mg_lo)).T
    rg_out[...] = rg.reshape(nr, own, outer)
    lg_out[...] = lg_acc[...].T.reshape(nc, own, outer)
    land_l[col] = lg_out[col]
    if comm:
        for d in range(1, nc):
            other = lax.rem(col + d, nc)
            move = remote(lg_out.at[other], land_l.at[col], g_send.at[d], g_recv.at[d], (row, other))
            move.start()
            l_moves.append(move)
        for k in range(nr):
            r, c = source(k)
            me = jnp.logical_and(r == row, c == col)
            far = remote(
                rg_out.at[k], land_r.at[row], g_send.at[nc + k], g_recv.at[nc + row], (r, c)
            )
            near = pltpu.make_async_copy(rg_out.at[k], land_r.at[row], g_recv.at[nc + row])

            @pl.when(me)
            def _():
                near.start()

            @pl.when(jnp.logical_not(me))
            def _():
                far.start()

            r_moves.append((me, far))

    @pl.when(is_owner)
    def _():
        if comm:
            for move in b_moves:
                move.wait_recv()
        fin[mine] = (each(land_b) * (1.0 / residues)).astype(BF)
        if comm:
            for move in c_moves:
                move.start()

    if comm:
        for move in act_moves:
            move.wait_recv()
    unpack_edges(act_t, 4, 1)
    gt[: 8 * wch] = jnp.zeros((8 * wch, 128), F32)

    fill(even, act_t, 4, 0, 0, False)

    def p_forward(first, last):
        @pl.loop(first, last, step=STEP)
        def _(n):
            parts = []
            for m in range(STEP):
                parts += halves(dot(wf[...], even[...]))
                fill(odd, act_t, 4, n + m, 8, False)
                parts += halves(dot(wf[...], odd[...]))
                fill(even, act_t, 4, n + m, 16, False)
            spread(parts, 4 * n, (2, 1, 0))

    p_forward(0, ti // 16)
    spread(halves(dot(wf[...], even[...])), ng, (2, 1, 0))

    if comm:
        for move in l_moves:
            move.wait_recv()
        for k in range(nr):
            pltpu.make_async_copy(rg_out.at[k], land_r.at[k], g_recv.at[nc + k]).wait()
    lg = land_l[0]
    for k in range(1, nc):
        lg = lg + land_l[k]
    rg = land_r[0]
    for k in range(1, nr):
        rg = rg + land_r[k]

    def exact(x, w):
        total = jnp.zeros((own, w.shape[1]), F32)
        for _ in range(3):
            head = x.astype(BF)
            total = total + dot(head, w)
            x = x - head.astype(F32)
        return total

    fg_out[...] = (exact(lg, lw[...]) + exact(rg, rw[...])) * (1.0 / math.sqrt(residues))

    for k, c in enumerate(owners):
        if comm:

            @pl.when(col != c)
            def _():
                pltpu.make_async_copy(wgs.at[0], fin.at[k], w_recv.at[nc + nr + k]).wait()

        tap = fin[k].astype(F32)
        wg_out[k] = jnp.concatenate([tap[:, :ch], tap[:, ch:]], axis=0)

    if comm:
        for move in left_moves + cot_moves + act_moves + l_moves:
            move.wait_send()
        for c, move in a_moves:

            @pl.when(col != c)
            def _():
                move.wait_send()

        @pl.when(is_owner)
        def _():
            for move in b_moves + c_moves:
                move.wait_send()

        for me, far in right_moves + r_moves:

            @pl.when(jnp.logical_not(me))
            def _():
                far.wait_send()


def last_kernel(
    hid_n, pg_n, gt, wg_in, fg_in, bias, po_hbm, pg_hbm, wg_hbm, fg_hbm, out_n, out_sem
):
    ch, ti, _ = hid_n.shape
    wch = ch + 8
    step = ch // 4
    copies = [
        pltpu.make_async_copy(
            pg_n.at[pl.ds(k * step, step)], pg_hbm.at[pl.ds(k * step, step)], out_sem.at[k]
        )
        for k in range(4)
    ]
    copies.append(pltpu.make_async_copy(wg_in, wg_hbm, out_sem.at[4]))
    copies.append(pltpu.make_async_copy(fg_in, fg_hbm, out_sem.at[5]))
    for copy in copies:
        copy.start()
    for k in range(ti // BLOCK):

        @pl.loop(0, ch, unroll=16)
        def _(c):
            conv = gt[pl.ds((8 + BLOCK * k) * wch + c, BLOCK, stride=wch), :]
            h = hid_n[c, pl.ds(BLOCK * k, BLOCK), :].astype(F32)
            out_n[c, pl.ds(BLOCK * k, BLOCK), :] = (h + bias[c] + conv).astype(BF)

        copy = pltpu.make_async_copy(
            out_n.at[:, pl.ds(BLOCK * k, BLOCK)], po_hbm.at[:, pl.ds(BLOCK * k, BLOCK)],
            out_sem.at[6 + k],
        )
        copy.start()
        copies.append(copy)
    for copy in copies:
        copy.wait()


def call(nr, nc, residues, comm, pair_map, features, lw, rw, ow, cw, bias, cot):
    ch, ti, tj = pair_map.shape
    own, feat = features.shape
    outer = lw.shape[1]
    kg = ti // PACK
    any_spec = pl.BlockSpec(memory_space=pl.ANY)
    vmem = pl.BlockSpec(memory_space=pltpu.VMEM)
    smem = pl.BlockSpec(memory_space=pltpu.SMEM)
    V = pltpu.VMEM
    dma = pltpu.SemaphoreType.DMA
    scratch = [
        V((ch, ti, tj), BF),
        V((max(ch * (ti + 8), ti * (ch + 8)), 128), F32),
        V((ti + 8, ch, 128), BF),
        V((ti + 16, ch, 128), BF),
        V((kg + 2, ch, 128), BF),
        V((ti // 8 + 1, 3 * ch, 1024), BF),
        V((3 * ch, 1024), BF),
        V((3 * ch, 1024), BF),
        V((ti, 256), F32),
        V((ti, 256), F32),
        V((2, kg, ch, 128), BF),
        V((2, 2, 4, ch, 128), BF),
        V((2, 2, kg + 2, ch, 128), BF),
        V((own, 128), BF),
        V((nc, own, 128), BF),
        V((nr, own, 128), BF),
        V((ti, outer), BF),
        V((outer, ti), BF),
        V((outer * (ch + 8), 128), F32),
        V((ch, outer, 128), BF),
        V((3 * ch, 3 * ch), BF),
        V((3 * ch, 3 * ch), BF),
        V((outer, outer * ch), BF),
        V((outer * ch, outer), BF),
        V((outer * (ch + 8), 128), F32),
        V((3 * ch, 3 * ch), F32),
        V((9, ch // 2, 2 * ch), BF),
        V((nc, ch // 2, 2 * ch), BF),
        V((nr, ch // 2, 2 * ch), F32),
        V((9, ch // 2, 2 * ch), BF),
        V((outer, ti), F32),
        V((nc, own, outer), F32),
        V((nr, own, outer), F32),
        V((nc, own, outer), F32),
        V((nr, own, outer), F32),
        dma((ch // 8 + 1,)),
        dma((nc + nr,)),
        dma((nc + nr,)),
        dma((2, 8)),
        dma((2, 8)),
        dma((9 + nr + nc,)),
        dma((nc + nr + 9,)),
        dma((nc + nr,)),
        dma((nc + nr,)),
    ]
    macs = ti * tj * (27 * ch * ch + 3 * outer * ch)
    out = pl.pallas_call(
        functools.partial(kernel, nr, nc, ch, ti, outer, comm, residues),
        out_shape=[
            V((ch, ti, tj), BF),
            V((ch, ti, tj), BF),
            V(((ti + 20) * (ch + 8), 128), F32),
            V((9, ch, ch), F32),
            V((own, feat), F32),
        ],
        in_specs=[any_spec, any_spec] + [vmem] * 5,
        out_specs=[vmem] * 5,
        scratch_shapes=scratch,
        compiler_params=pltpu.CompilerParams(
            collective_id=0 if comm else None,
            has_side_effects=True,
            vmem_limit_bytes=44 * 1024 * 1024,
        ),
        cost_estimate=pl.CostEstimate(
            flops=2 * macs, bytes_accessed=8 * ch * ti * tj, transcendentals=2 * ch * ti * tj
        ),
    )(cot, pair_map, features, lw.T, rw.T, ow, cw.reshape(9, ch, ch))
    kept = [pltpu.with_memory_space_constraint(x, pltpu.VMEM) for x in out]
    po, pg, wg, fg = pl.pallas_call(
        last_kernel,
        out_shape=[
            jax.ShapeDtypeStruct((ch, ti, tj), BF),
            jax.ShapeDtypeStruct((ch, ti, tj), BF),
            jax.ShapeDtypeStruct((9, ch, ch), F32),
            jax.ShapeDtypeStruct((own, feat), F32),
        ],
        in_specs=[vmem] * 5 + [smem],
        out_specs=[any_spec] * 4,
        scratch_shapes=[V((ch, ti, tj), BF), dma((6 + ti // BLOCK,))],
        compiler_params=pltpu.CompilerParams(vmem_limit_bytes=24 * 1024 * 1024),
        cost_estimate=pl.CostEstimate(
            flops=2 * ch * ti * tj, bytes_accessed=4 * ch * ti * tj, transcendentals=0
        ),
    )(*kept, bias)
    return po, pg, wg.reshape(3, 3, ch, ch), fg


def solution(mesh):
    nr, nc = mesh.shape["row"], mesh.shape["col"]

    def shards(pair_map, features, lw, rw, ow, cw, bias, cot):
        return call(
            nr, nc, pair_map.shape[1] * nr, True, pair_map, features, lw, rw, ow, cw, bias, cot
        )

    in_specs = (
        P(None, "row", "col"),
        P(("row", "col"), None),
        P(),
        P(),
        P(),
        P(),
        P(),
        P(None, "row", "col"),
    )
    out_specs = (P(None, "row", "col"), P(None, "row", "col"), P(), P(("row", "col"), None))
    return jax.shard_map(shards, mesh=mesh, in_specs=in_specs, out_specs=out_specs, check_vma=False)
```

```python
import functools
import math

import jax
import jax.numpy as jnp
from jax import lax
from jax.experimental import pallas as pl
from jax.experimental.pallas import tpu as pltpu
from jax.sharding import PartitionSpec as P

MESH = pl.DeviceIdType.MESH
BF = jnp.bfloat16
F32 = jnp.float32
NT = (((1,), (1,)), ((), ()))
PACK = 16
BLOCK = 32
STEP = 16


def dot(a, b, dims=None):
    if dims is None:
        return jnp.dot(a, b, preferred_element_type=F32)
    return lax.dot_general(a, b, dims, preferred_element_type=F32)


def kernel(
    nr, nc, ch, ti, outer, comm, residues,
    cot_hbm, pm_hbm, feat, lw, rw, ow, cw,
    hid_n, cot_n, gt, wg_out, fg_out,
    slope_n, wide, cot_t, act_t, hx, terms, even, odd, packs, land_row, land_col,
    lr, left_in, right_in, left, left_t, mixf, mix, wf, wb, ow_q, ow_t, mgf,
    wg_acc, wgs, land_a, land_b, fin, lg_acc, lg_out, rg_out, land_l, land_r,
    in_sem, f_send, f_recv, h_send, h_recv, w_send, w_recv, g_send, g_recv,
):
    row = lax.axis_index("row")
    col = lax.axis_index("col")
    kg = ti // PACK
    ng = ti // 4
    pitch = ti + 8
    wch = ch + 8
    own = lr.shape[0]
    flat = row * nc + col
    goal = flat // nr
    slot = lax.rem(flat, nr)
    up, down = lax.rem(row + nr - 1, nr), lax.rem(row + 1, nr)
    west, east = lax.rem(col + nc - 1, nc), lax.rem(col + 1, nc)
    cstep = 8
    nchunk = ch // cstep

    def source(k):
        f = col * nr + k
        return f // nc, lax.rem(f, nc)

    if comm:
        barrier = pltpu.get_barrier_semaphore()

        def greet(r, c):
            pl.semaphore_signal(barrier, inc=1, device_id=(r, c), device_id_type=MESH)

        def greet_unless_me(r, c):
            @pl.when(jnp.logical_or(r != row, c != col))
            def _():
                greet(r, c)

        for d in range(1, nc):
            greet(row, lax.rem(col + d, nc))
        for d in range(1, nr):
            greet(lax.rem(row + d, nr), col)
        for r in (up, down):
            for c in (west, east):
                greet(r, c)
        for k in range(nr):
            greet_unless_me(k, goal)
            greet_unless_me(*source(k))
        total_greets = (nc - 1) + (nr - 1) + 4 + 2 * nr - jnp.where(goal == col, 2, 0)

    cot_in = [
        pltpu.make_async_copy(
            cot_hbm.at[pl.ds(k * cstep, cstep)], cot_n.at[pl.ds(k * cstep, cstep)], in_sem.at[k]
        )
        for k in range(nchunk)
    ]
    pm_in = pltpu.make_async_copy(pm_hbm, hid_n, in_sem.at[nchunk])
    for copy in cot_in:
        copy.start()
    pm_in.start()

    lr[...] = jnp.concatenate(
        [dot(feat[...], lw[...], NT), dot(feat[...], rw[...], NT), jnp.zeros((own, 128 - 2 * outer), F32)],
        axis=1,
    ).astype(BF)

    def remote(src, dst, ssem, rsem, dev):
        return pltpu.make_async_remote_copy(
            src_ref=src, dst_ref=dst, send_sem=ssem, recv_sem=rsem, device_id=dev, device_id_type=MESH
        )

    def drain(blocks, sem):
        pltpu.make_async_copy(blocks, blocks, sem).wait()

    def drain_some(blocks, sem, one_less):
        @pl.when(one_less)
        def _():
            drain(blocks.at[pl.ds(0, blocks.shape[0] - 1)], sem)

        @pl.when(jnp.logical_not(one_less))
        def _():
            drain(blocks, sem)

    left_in[col] = lr[...]
    if comm:
        pl.semaphore_wait(barrier, total_greets)
        for k in range(nr):
            me = jnp.logical_and(row == k, goal == col)
            far = remote(lr, right_in.at[slot], f_send.at[1], f_recv.at[1], (k, goal))
            near = pltpu.make_async_copy(lr, right_in.at[slot], f_recv.at[1])

            @pl.when(me)
            def _():
                near.start()

            @pl.when(jnp.logical_not(me))
            def _():
                far.start()

        for d in range(1, nc):
            remote(
                lr, left_in.at[col], f_send.at[0], f_recv.at[0], (row, lax.rem(col + d, nc))
            ).start()

    for a in range(3):
        wf[a * ch : (a + 1) * ch, :] = jnp.concatenate([cw[3 * a + b] for b in range(3)], axis=1)
        wb[a * ch : (a + 1) * ch, :] = jnp.concatenate(
            [cw[3 * a + b].astype(F32).T for b in range(3)], axis=1
        ).astype(BF)
    ow_q[...] = jnp.concatenate([ow[p] for p in range(outer)], axis=1)
    step = 512
    for k in range(outer * ch // step):
        ow_t[k * step : (k + 1) * step, :] = ow_q[:, k * step : (k + 1) * step].astype(F32).T.astype(BF)

    def p_widen():
        for k in range(nchunk):
            cot_in[k].wait()

            @pl.loop(0, cstep, unroll=8)
            def _(c):
                at = pl.multiple_of((k * cstep + c) * pitch, 8)
                wide[pl.ds(at, ti), :] = cot_n[k * cstep + c].astype(F32)

    p_widen()

    lane = lax.broadcasted_iota(jnp.int32, (ch, 128), 1)
    window = lax.rem(lane + 4, 128) // 8

    def to_rows(dst, first, which, read):
        @pl.loop(0, kg, unroll=4)
        def _(k):
            packed = None
            for m in range(PACK):
                row_at = PACK * k + m
                x = read(row_at).astype(BF)
                dst[first + row_at] = x
                packed = x if m == 0 else jnp.where(window == m, pltpu.roll(x, 8 * m, 1), packed)
            packs[which, k] = packed

    def halo_moves(src, first, which):
        edges = packs.at[which]
        from_west, from_east = land_col.at[which, 0], land_col.at[which, 1]
        plan = [
            (src.at[pl.ds(first, 4)], land_row.at[which, 1], (up, col)),
            (src.at[pl.ds(first + ti - 4, 4)], land_row.at[which, 0], (down, col)),
            (edges, from_east.at[pl.ds(1, kg)], (row, west)),
            (edges, from_west.at[pl.ds(1, kg)], (row, east)),
            (edges.at[0], from_east.at[kg + 1], (up, west)),
            (edges.at[0], from_west.at[kg + 1], (up, east)),
            (edges.at[kg - 1], from_east.at[0], (down, west)),
            (edges.at[kg - 1], from_west.at[0], (down, east)),
        ]
        return [
            remote(s, d, h_send.at[which, min(m // 2, 1)], h_recv.at[which, min(m // 2, 1)], dev)
            for m, (s, d, dev) in enumerate(plan)
        ]

    to_rows(cot_t, 4, 0, lambda i: wide[pl.ds(i, ch, stride=pitch), :])
    cot_moves = halo_moves(cot_t, 4, 0)
    if comm:
        for move in cot_moves:
            move.start()

    if comm:
        drain(left_in.at[pl.ds(0, nc - 1)], f_recv.at[0])
        drain(right_in, f_recv.at[1])
    left[...] = left_in[...].reshape(nc * own, 128)[:, :outer]
    left_t[...] = left[...].astype(F32).T.astype(BF)
    right = right_in[...].reshape(nr * own, 128)[:, outer : 2 * outer]
    for k in range(outer * ch // step):
        rows = dot(ow_t[k * step : (k + 1) * step, :], right, NT).astype(BF).astype(F32)
        for m in range(step // ch):
            at = (k * (step // ch) + m) * wch
            mixf[at : at + ch, :] = rows[m * ch : (m + 1) * ch]

    @pl.loop(0, ch, unroll=8)
    def _(c):
        mix[c] = mixf[pl.ds(c, outer, stride=wch), :].astype(BF)

    pm_in.wait()

    def p_hidden():
        def update(c):
            return dot(left[...], jnp.concatenate([mix[c], mix[c + 1]], axis=1))

        def finish(c, change):
            for k in range(2):
                hidden = (hid_n[c + k].astype(F32) + change[:, 128 * k : 128 * (k + 1)]).astype(BF)
                hid_n[c + k] = hidden
                h = hidden.astype(F32)
                e = jnp.minimum(jnp.exp(h), 1.0)
                slope_n[c + k] = e.astype(BF)
                wide[pl.ds(c + k, ti, stride=wch), :] = jnp.maximum(h, e - 1.0)

        @pl.loop(0, ch, step=16)
        def _(c):
            changes = [update(c + 2 * k) for k in range(8)]
            for k in range(8):
                finish(c + 2 * k, changes[k])

    p_hidden()

    to_rows(act_t, 8, 1, lambda i: wide[pl.ds(pl.multiple_of(i * wch, 8), ch), :])
    for s in (0, 4, ti + 8, ti + 12):
        act_t[s : s + 4] = jnp.zeros((4, ch, 128), BF)
    act_moves = halo_moves(act_t, 8, 1)
    if comm:
        for move in act_moves:
            move.start()

    has_up, has_down, has_west, has_east = row > 0, row < nr - 1, col > 0, col < nc - 1

    def keep(ok, x):
        return jnp.where(ok, x, jnp.zeros_like(x))

    def unpack_edges(dst, first, which):
        dst[first : first + 4] = keep(has_up, land_row[which, 0])
        dst[first + ti + 4 : first + ti + 8] = keep(has_down, land_row[which, 1])

        def place(k, ok):
            from_west = keep(jnp.logical_and(ok, has_west), land_col[which, 0, k])
            from_east = keep(jnp.logical_and(ok, has_east), land_col[which, 1, k])
            hx[k] = jnp.where(
                lax.rem(lane, 8) < 4, pltpu.roll(from_west, 4, 1), pltpu.roll(from_east, 124, 1)
            )

        place(0, has_up)
        place(kg + 1, has_down)

        @pl.loop(1, kg + 1, unroll=4)
        def _(k):
            place(k, True)

    def fill(dst, src, first, n, q, turned):
        for r in range(8):
            x = src[first + 16 * n + q + r]
            at = q + r + PACK - 4
            edge = pltpu.roll(hx[n + at // PACK], (PACK - at % PACK) % PACK * 8, 1)
            before = jnp.where(lane < 4, edge, pltpu.roll(x, 4, 1))
            after = jnp.where(lane >= 124, edge, pltpu.roll(x, 124, 1))
            lanes = slice(128 * r, 128 * (r + 1))
            dst[:ch, lanes] = after if turned else before
            dst[ch : 2 * ch, lanes] = x
            dst[2 * ch :, lanes] = before if turned else after

    def halves(x):
        return [x[:, :512], x[:, 512:]]

    def spread(parts, g, order):
        for s in range(len(parts) + 2):
            terms = [
                parts[s - k][a * ch : (a + 1) * ch]
                for k, a in enumerate(order)
                if 0 <= s - k < len(parts)
            ]
            total = terms[0]
            for term in terms[1:]:
                total = total + term
            for r in range(4):
                at = pl.ds(pl.multiple_of((4 * (g + s) + r) * wch, 8), ch)
                term = total[:, 128 * r : 128 * (r + 1)]
                gt[at, :] = gt[at, :] + term if s < 2 else term

    if comm:
        drain(land_row.at[0], h_recv.at[0, 0])
        drain(land_col.at[0], h_recv.at[0, 1])
    unpack_edges(cot_t, 0, 0)
    gt[: 8 * wch] = jnp.zeros((8 * wch, 128), F32)
    wg_acc[...] = jnp.zeros_like(wg_acc)

    def p_kernel():
        fill(terms.at[0], cot_t, 0, 0, 0, True)

        def acts(first):
            return jnp.concatenate(
                [
                    jnp.concatenate([act_t[first + 4 * a + r] for r in range(8)], axis=1)
                    for a in range(3)
                ],
                axis=0,
            )

        @pl.loop(0, ti // 16, step=STEP)
        def _(n):
            grad = 0
            for m in range(n_chunks):
                j = 2 * n + m
                grad = grad + dot(terms[j], acts(8 * j), NT)
                fill(terms.at[j + 1], cot_t, 0, n + (m + 1) // 2, 8 * ((m + 1) % 2), True)
            wg_acc[...] += grad

        wg_acc[...] += dot(terms[ti // 8], acts(ti), NT)

    def p_back():
        @pl.loop(0, ti // 16, step=STEP)
        def _(n):
            parts = []
            for m in range(n_chunks):
                parts += halves(dot(wb[...], terms[2 * n + m]))
            spread(parts, 4 * n, (0, 1, 2))

        spread(halves(dot(wb[...], terms[ti // 8])), ng, (0, 1, 2))

    n_chunks = 2 * STEP
    p_kernel()

    taps = 9
    owners = [min(2 * k, nc - 1) for k in range(taps)]
    is_owner = functools.reduce(jnp.logical_or, [col == c for c in owners])
    mine = jnp.where(col == owners[-1], taps - 1, col // 2)
    half = ch // 2
    for k in range(taps):
        a, b = k // 3, k % 3
        tap = wg_acc[b * ch : (b + 1) * ch, a * ch : (a + 1) * ch]
        wgs[k] = jnp.concatenate([tap[:half], tap[half:]], axis=1).astype(BF)
    for k, c in enumerate(owners):
        move = remote(wgs.at[k], land_a.at[col], w_send.at[0], w_recv.at[0], (row, c))

        @pl.when(col == c)
        def _():
            land_a[col] = wgs[k]

        if comm:

            @pl.when(col != c)
            def _():
                move.start()


    p_back()

    def each(refs):
        total = refs[0].astype(F32)
        for k in range(1, refs.shape[0]):
            total = total + refs[k].astype(F32)
        return total

    @pl.when(is_owner)
    def _():
        if comm:
            drain(land_a.at[pl.ds(0, nc - 1)], w_recv.at[0])
        land_b[row] = each(land_a)
        if comm:
            for d in range(1, nr):
                to = (lax.rem(row + d, nr), col)
                remote(land_b.at[row], land_b.at[row], w_send.at[1], w_recv.at[1], to).start()

    lg_acc[...] = jnp.zeros_like(lg_acc)

    def p_grad():
        @pl.loop(0, ch, step=16)
        def _(c):
            lg = 0
            for half in (c, c + 4, c + 8, c + 12):
                grads = []
                for m in range(4):
                    g = gt[pl.ds(8 * wch + half + m, ti, stride=wch), :]
                    pg = (cot_n[half + m].astype(F32) + g * slope_n[half + m].astype(F32)).astype(BF)
                    cot_n[half + m] = pg
                    grads.append(pg)
                grads = jnp.concatenate(grads, axis=1)
                mixes = jnp.concatenate([mix[half + m] for m in range(4)], axis=1)
                lg = lg + dot(mixes, grads, NT)
                mg = dot(left_t[...], grads)
                for m in range(4):
                    mgf[pl.ds(half + m, outer, stride=wch), :] = mg[:, 128 * m : 128 * (m + 1)]
            lg_acc[...] += lg

    p_grad()

    mg = jnp.concatenate([mgf[p * wch : p * wch + ch, :] for p in range(outer)], axis=0)
    mg_hi = mg.astype(BF)
    mg_lo = (mg - mg_hi.astype(F32)).astype(BF)
    rg = (dot(ow_q[...], mg_hi) + dot(ow_q[...], mg_lo)).T
    rg_out[...] = rg.reshape(nr, own, outer)
    lg_out[...] = lg_acc[...].T.reshape(nc, own, outer)
    land_l[col] = lg_out[col]
    if comm:
        for d in range(1, nc):
            other = lax.rem(col + d, nc)
            remote(
                lg_out.at[other], land_l.at[col], g_send.at[0], g_recv.at[0], (row, other)
            ).start()
        for k in range(nr):
            r, c = source(k)
            me = jnp.logical_and(r == row, c == col)
            far = remote(rg_out.at[k], land_r.at[row], g_send.at[1], g_recv.at[1], (r, c))
            near = pltpu.make_async_copy(rg_out.at[k], land_r.at[row], g_recv.at[1])

            @pl.when(me)
            def _():
                near.start()

            @pl.when(jnp.logical_not(me))
            def _():
                far.start()

    @pl.when(is_owner)
    def _():
        if comm:
            drain(land_b.at[pl.ds(0, nr - 1)], w_recv.at[1])
        fin[mine] = (each(land_b) * (1.0 / residues)).astype(BF)
        if comm:
            for d in range(1, nc):
                to = (row, lax.rem(col + d, nc))
                remote(fin.at[mine], fin.at[mine], w_send.at[2], w_recv.at[2], to).start()

    if comm:
        drain(land_row.at[1], h_recv.at[1, 0])
        drain(land_col.at[1], h_recv.at[1, 1])
    unpack_edges(act_t, 4, 1)
    gt[: 8 * wch] = jnp.zeros((8 * wch, 128), F32)

    fill(even, act_t, 4, 0, 0, False)

    def p_forward(first, last):
        @pl.loop(first, last, step=STEP)
        def _(n):
            parts = []
            for m in range(STEP):
                parts += halves(dot(wf[...], even[...]))
                fill(odd, act_t, 4, n + m, 8, False)
                parts += halves(dot(wf[...], odd[...]))
                fill(even, act_t, 4, n + m, 16, False)
            spread(parts, 4 * n, (2, 1, 0))

    p_forward(0, ti // 16)
    spread(halves(dot(wf[...], even[...])), ng, (2, 1, 0))

    if comm:
        drain(land_l.at[pl.ds(0, nc - 1)], g_recv.at[0])
        drain(land_r, g_recv.at[1])
    lg = land_l[0]
    for k in range(1, nc):
        lg = lg + land_l[k]
    rg = land_r[0]
    for k in range(1, nr):
        rg = rg + land_r[k]

    def exact(x, w):
        total = jnp.zeros((own, w.shape[1]), F32)
        for _ in range(3):
            head = x.astype(BF)
            total = total + dot(head, w)
            x = x - head.astype(F32)
        return total

    fg_out[...] = (exact(lg, lw[...]) + exact(rg, rw[...])) * (1.0 / math.sqrt(residues))

    if comm:
        drain_some(fin, w_recv.at[2], is_owner)
    for k in range(taps):
        tap = fin[k].astype(F32)
        wg_out[k] = jnp.concatenate([tap[:, :ch], tap[:, ch:]], axis=0)

    if comm:
        drain(left_in.at[pl.ds(0, nc - 1)], f_send.at[0])
        drain_some(right_in, f_send.at[1], goal == col)
        for which in range(2):
            drain(land_row.at[which], h_send.at[which, 0])
            drain(land_col.at[which], h_send.at[which, 1])
        drain_some(wgs, w_send.at[0], is_owner)
        drain(land_l.at[pl.ds(0, nc - 1)], g_send.at[0])
        drain_some(land_r, g_send.at[1], goal == col)

        @pl.when(is_owner)
        def _():
            drain(land_b.at[pl.ds(0, nr - 1)], w_send.at[1])
            drain(land_a.at[pl.ds(0, nc - 1)], w_send.at[2])


def last_kernel(
    hid_n, pg_n, gt, wg_in, fg_in, bias, po_hbm, pg_hbm, wg_hbm, fg_hbm, out_n, out_sem
):
    ch, ti, _ = hid_n.shape
    wch = ch + 8
    step = ch // 4
    copies = [
        pltpu.make_async_copy(
            pg_n.at[pl.ds(k * step, step)], pg_hbm.at[pl.ds(k * step, step)], out_sem.at[k]
        )
        for k in range(4)
    ]
    copies.append(pltpu.make_async_copy(wg_in, wg_hbm, out_sem.at[4]))
    copies.append(pltpu.make_async_copy(fg_in, fg_hbm, out_sem.at[5]))
    for copy in copies:
        copy.start()
    for k in range(ti // BLOCK):

        @pl.loop(0, ch, unroll=16)
        def _(c):
            conv = gt[pl.ds((8 + BLOCK * k) * wch + c, BLOCK, stride=wch), :]
            h = hid_n[c, pl.ds(BLOCK * k, BLOCK), :].astype(F32)
            out_n[c, pl.ds(BLOCK * k, BLOCK), :] = (h + bias[c] + conv).astype(BF)

        copy = pltpu.make_async_copy(
            out_n.at[:, pl.ds(BLOCK * k, BLOCK)], po_hbm.at[:, pl.ds(BLOCK * k, BLOCK)],
            out_sem.at[6 + k],
        )
        copy.start()
        copies.append(copy)
    for copy in copies:
        copy.wait()


def call(nr, nc, residues, comm, pair_map, features, lw, rw, ow, cw, bias, cot):
    ch, ti, tj = pair_map.shape
    own, feat = features.shape
    outer = lw.shape[1]
    kg = ti // PACK
    any_spec = pl.BlockSpec(memory_space=pl.ANY)
    vmem = pl.BlockSpec(memory_space=pltpu.VMEM)
    smem = pl.BlockSpec(memory_space=pltpu.SMEM)
    V = pltpu.VMEM
    dma = pltpu.SemaphoreType.DMA
    scratch = [
        V((ch, ti, tj), BF),
        V((max(ch * (ti + 8), ti * (ch + 8)), 128), F32),
        V((ti + 8, ch, 128), BF),
        V((ti + 16, ch, 128), BF),
        V((kg + 2, ch, 128), BF),
        V((ti // 8 + 1, 3 * ch, 1024), BF),
        V((3 * ch, 1024), BF),
        V((3 * ch, 1024), BF),
        V((2, kg, ch, 128), BF),
        V((2, 2, 4, ch, 128), BF),
        V((2, 2, kg + 2, ch, 128), BF),
        V((own, 128), BF),
        V((nc, own, 128), BF),
        V((nr, own, 128), BF),
        V((ti, outer), BF),
        V((outer, ti), BF),
        V((outer * (ch + 8), 128), F32),
        V((ch, outer, 128), BF),
        V((3 * ch, 3 * ch), BF),
        V((3 * ch, 3 * ch), BF),
        V((outer, outer * ch), BF),
        V((outer * ch, outer), BF),
        V((outer * (ch + 8), 128), F32),
        V((3 * ch, 3 * ch), F32),
        V((9, ch // 2, 2 * ch), BF),
        V((nc, ch // 2, 2 * ch), BF),
        V((nr, ch // 2, 2 * ch), F32),
        V((9, ch // 2, 2 * ch), BF),
        V((outer, ti), F32),
        V((nc, own, outer), F32),
        V((nr, own, outer), F32),
        V((nc, own, outer), F32),
        V((nr, own, outer), F32),
        dma((ch // 8 + 1,)),
        dma((2,)),
        dma((2,)),
        dma((2, 2)),
        dma((2, 2)),
        dma((3,)),
        dma((3,)),
        dma((2,)),
        dma((2,)),
    ]
    macs = ti * tj * (27 * ch * ch + 3 * outer * ch)
    out = pl.pallas_call(
        functools.partial(kernel, nr, nc, ch, ti, outer, comm, residues),
        out_shape=[
            V((ch, ti, tj), BF),
            V((ch, ti, tj), BF),
            V(((ti + 20) * (ch + 8), 128), F32),
            V((9, ch, ch), F32),
            V((own, feat), F32),
        ],
        in_specs=[any_spec, any_spec] + [vmem] * 5,
        out_specs=[vmem] * 5,
        scratch_shapes=scratch,
        compiler_params=pltpu.CompilerParams(
            collective_id=0 if comm else None,
            has_side_effects=True,
            vmem_limit_bytes=44 * 1024 * 1024,
        ),
        cost_estimate=pl.CostEstimate(
            flops=2 * macs, bytes_accessed=8 * ch * ti * tj, transcendentals=2 * ch * ti * tj
        ),
    )(cot, pair_map, features, lw.T, rw.T, ow, cw.reshape(9, ch, ch))
    kept = [pltpu.with_memory_space_constraint(x, pltpu.VMEM) for x in out]
    po, pg, wg, fg = pl.pallas_call(
        last_kernel,
        out_shape=[
            jax.ShapeDtypeStruct((ch, ti, tj), BF),
            jax.ShapeDtypeStruct((ch, ti, tj), BF),
            jax.ShapeDtypeStruct((9, ch, ch), F32),
            jax.ShapeDtypeStruct((own, feat), F32),
        ],
        in_specs=[vmem] * 5 + [smem],
        out_specs=[any_spec] * 4,
        scratch_shapes=[V((ch, ti, tj), BF), dma((6 + ti // BLOCK,))],
        compiler_params=pltpu.CompilerParams(vmem_limit_bytes=24 * 1024 * 1024),
        cost_estimate=pl.CostEstimate(
            flops=2 * ch * ti * tj, bytes_accessed=4 * ch * ti * tj, transcendentals=0
        ),
    )(*kept, bias)
    return po, pg, wg.reshape(3, 3, ch, ch), fg


def solution(mesh):
    nr, nc = mesh.shape["row"], mesh.shape["col"]

    def shards(pair_map, features, lw, rw, ow, cw, bias, cot):
        return call(
            nr, nc, pair_map.shape[1] * nr, True, pair_map, features, lw, rw, ow, cw, bias, cot
        )

    in_specs = (
        P(None, "row", "col"),
        P(("row", "col"), None),
        P(),
        P(),
        P(),
        P(),
        P(),
        P(None, "row", "col"),
    )
    out_specs = (P(None, "row", "col"), P(None, "row", "col"), P(), P(("row", "col"), None))
    return jax.shard_map(shards, mesh=mesh, in_specs=in_specs, out_specs=out_specs, check_vma=False)
```

```python
import functools
import math

import jax
import jax.numpy as jnp
from jax import lax
from jax.experimental import pallas as pl
from jax.experimental.pallas import tpu as pltpu
from jax.sharding import PartitionSpec as P

MESH = pl.DeviceIdType.MESH
BF = jnp.bfloat16
F32 = jnp.float32
NT = (((1,), (1,)), ((), ()))
PACK = 16
BLOCK = 32
STEP = 4


def dot(a, b, dims=None):
    if dims is None:
        return jnp.dot(a, b, preferred_element_type=F32)
    return lax.dot_general(a, b, dims, preferred_element_type=F32)


def kernel(
    nr, nc, ch, ti, outer, comm, residues,
    cot_hbm, pm_hbm, feat, lw, rw, ow, cw,
    hid_n, cot_n, gt, wg_out, fg_out,
    slope_n, wide, cot_t, act_t, hx, terms, even, odd, packs, land_row, land_col,
    lr, left_in, right_in, left, left_t, mixf, mix, wf, wb, ow_q, ow_t, mgf,
    wg_acc, wgs, land_a, land_b, fin, lg_acc, lg_out, rg_out, land_l, land_r,
    in_sem, f_send, f_recv, h_send, h_recv, w_send, w_recv, g_send, g_recv,
):
    row = lax.axis_index("row")
    col = lax.axis_index("col")
    kg = ti // PACK
    ng = ti // 4
    pitch = ti + 8
    wch = ch + 8
    own = lr.shape[0]
    flat = row * nc + col
    goal = flat // nr
    slot = lax.rem(flat, nr)
    up, down = lax.rem(row + nr - 1, nr), lax.rem(row + 1, nr)
    west, east = lax.rem(col + nc - 1, nc), lax.rem(col + 1, nc)
    cstep = 8
    nchunk = ch // cstep

    def source(k):
        f = col * nr + k
        return f // nc, lax.rem(f, nc)

    if comm:
        barrier = pltpu.get_barrier_semaphore()

        def greet(r, c):
            pl.semaphore_signal(barrier, inc=1, device_id=(r, c), device_id_type=MESH)

        def greet_unless_me(r, c):
            @pl.when(jnp.logical_or(r != row, c != col))
            def _():
                greet(r, c)

        for d in range(1, nc):
            greet(row, lax.rem(col + d, nc))
        for d in range(1, nr):
            greet(lax.rem(row + d, nr), col)
        for r in (up, down):
            for c in (west, east):
                greet(r, c)
        for k in range(nr):
            greet_unless_me(k, goal)
            greet_unless_me(*source(k))
        total_greets = (nc - 1) + (nr - 1) + 4 + 2 * nr - jnp.where(goal == col, 2, 0)

    cot_in = [
        pltpu.make_async_copy(
            cot_hbm.at[pl.ds(k * cstep, cstep)], cot_n.at[pl.ds(k * cstep, cstep)], in_sem.at[k]
        )
        for k in range(nchunk)
    ]
    pm_in = pltpu.make_async_copy(pm_hbm, hid_n, in_sem.at[nchunk])
    for copy in cot_in:
        copy.start()
    pm_in.start()

    lr[...] = jnp.concatenate(
        [dot(feat[...], lw[...], NT), dot(feat[...], rw[...], NT), jnp.zeros((own, 128 - 2 * outer), F32)],
        axis=1,
    ).astype(BF)

    def remote(src, dst, ssem, rsem, dev):
        return pltpu.make_async_remote_copy(
            src_ref=src, dst_ref=dst, send_sem=ssem, recv_sem=rsem, device_id=dev, device_id_type=MESH
        )

    def drain(blocks, sem):
        pltpu.make_async_copy(blocks, blocks, sem).wait()

    def drain_some(blocks, sem, one_less):
        @pl.when(one_less)
        def _():
            drain(blocks.at[pl.ds(0, blocks.shape[0] - 1)], sem)

        @pl.when(jnp.logical_not(one_less))
        def _():
            drain(blocks, sem)

    left_in[col] = lr[...]
    if comm:
        pl.semaphore_wait(barrier, total_greets)
        for k in range(nr):
            me = jnp.logical_and(row == k, goal == col)
            far = remote(lr, right_in.at[slot], f_send.at[1], f_recv.at[1], (k, goal))
            near = pltpu.make_async_copy(lr, right_in.at[slot], f_recv.at[1])

            @pl.when(me)
            def _():
                near.start()

            @pl.when(jnp.logical_not(me))
            def _():
                far.start()

        for d in range(1, nc):
            remote(
                lr, left_in.at[col], f_send.at[0], f_recv.at[0], (row, lax.rem(col + d, nc))
            ).start()

    for a in range(3):
        wf[a * ch : (a + 1) * ch, :] = jnp.concatenate([cw[3 * a + b] for b in range(3)], axis=1)
        wb[a * ch : (a + 1) * ch, :] = jnp.concatenate(
            [cw[3 * a + b].astype(F32).T for b in range(3)], axis=1
        ).astype(BF)
    ow_q[...] = jnp.concatenate([ow[p] for p in range(outer)], axis=1)
    step = 512
    for k in range(outer * ch // step):
        ow_t[k * step : (k + 1) * step, :] = ow_q[:, k * step : (k + 1) * step].astype(F32).T.astype(BF)

    def p_widen():
        for k in range(nchunk):
            cot_in[k].wait()

            @pl.loop(0, cstep, unroll=8)
            def _(c):
                at = pl.multiple_of((k * cstep + c) * pitch, 8)
                wide[pl.ds(at, ti), :] = cot_n[k * cstep + c].astype(F32)

    p_widen()

    lane = lax.broadcasted_iota(jnp.int32, (ch, 128), 1)
    window = lax.rem(lane + 4, 128) // 8

    first_four = lax.rem(lane, 8) < 4
    kt = kg // 2

    def to_rows(dst, first, which, read):
        @pl.loop(0, kt, unroll=min(4, kt))
        def _(t):
            lines = []
            for k in range(2):
                packed = None
                for m in range(PACK):
                    row_at = 2 * PACK * t + PACK * k + m
                    x = read(row_at).astype(BF)
                    dst[first + row_at] = x
                    packed = x if m == 0 else jnp.where(window == m, pltpu.roll(x, 8 * m, 1), packed)
                lines.append(packed)
            moved = pltpu.roll(lines[1], 4, 1)
            packs[which, 0, t] = jnp.where(first_four, lines[0], moved)
            packs[which, 1, t] = jnp.where(first_four, moved, lines[0])

    def halo_moves(src, first, which):
        low, high = packs.at[which, 0], packs.at[which, 1]
        from_west, from_east = land_col.at[which, 0], land_col.at[which, 1]
        plan = [
            (src.at[pl.ds(first, 4)], land_row.at[which, 1], (up, col)),
            (src.at[pl.ds(first + ti - 4, 4)], land_row.at[which, 0], (down, col)),
            (low, from_east.at[pl.ds(1, kt)], (row, west)),
            (high, from_west.at[pl.ds(1, kt)], (row, east)),
            (low.at[0], from_east.at[kt + 1], (up, west)),
            (high.at[0], from_west.at[kt + 1], (up, east)),
            (low.at[kt - 1], from_east.at[0], (down, west)),
            (high.at[kt - 1], from_west.at[0], (down, east)),
        ]
        return [
            remote(s, d, h_send.at[which, min(m // 2, 1)], h_recv.at[which, min(m // 2, 1)], dev)
            for m, (s, d, dev) in enumerate(plan)
        ]

    to_rows(cot_t, 4, 0, lambda i: wide[pl.ds(i, ch, stride=pitch), :])
    cot_moves = halo_moves(cot_t, 4, 0)
    if comm:
        for move in cot_moves:
            move.start()

    if comm:
        drain(left_in.at[pl.ds(0, nc - 1)], f_recv.at[0])
        drain(right_in, f_recv.at[1])
    left[...] = left_in[...].reshape(nc * own, 128)[:, :outer]
    left_t[...] = left[...].astype(F32).T.astype(BF)
    right = right_in[...].reshape(nr * own, 128)[:, outer : 2 * outer]
    for k in range(outer * ch // step):
        rows = dot(ow_t[k * step : (k + 1) * step, :], right, NT).astype(BF).astype(F32)
        for m in range(step // ch):
            at = (k * (step // ch) + m) * wch
            mixf[at : at + ch, :] = rows[m * ch : (m + 1) * ch]

    @pl.loop(0, ch, unroll=8)
    def _(c):
        mix[c] = mixf[pl.ds(c, outer, stride=wch), :].astype(BF)

    pm_in.wait()

    def p_hidden():
        def update(c):
            return dot(left[...], jnp.concatenate([mix[c], mix[c + 1]], axis=1))

        def finish(c, change):
            for k in range(2):
                hidden = (hid_n[c + k].astype(F32) + change[:, 128 * k : 128 * (k + 1)]).astype(BF)
                hid_n[c + k] = hidden
                h = hidden.astype(F32)
                e = jnp.minimum(jnp.exp(h), 1.0)
                slope_n[c + k] = e.astype(BF)
                wide[pl.ds(c + k, ti, stride=wch), :] = jnp.maximum(h, e - 1.0)

        @pl.loop(0, ch, step=16)
        def _(c):
            changes = [update(c + 2 * k) for k in range(8)]
            for k in range(8):
                finish(c + 2 * k, changes[k])

    p_hidden()

    to_rows(act_t, 8, 1, lambda i: wide[pl.ds(pl.multiple_of(i * wch, 8), ch), :])
    for s in (0, 4, ti + 8, ti + 12):
        act_t[s : s + 4] = jnp.zeros((4, ch, 128), BF)
    act_moves = halo_moves(act_t, 8, 1)
    if comm:
        for move in act_moves:
            move.start()

    has_up, has_down, has_west, has_east = row > 0, row < nr - 1, col > 0, col < nc - 1

    def keep(ok, x):
        return jnp.where(ok, x, jnp.zeros_like(x))

    def unpack_edges(dst, first, which):
        dst[first : first + 4] = keep(has_up, land_row[which, 0])
        dst[first + ti + 4 : first + ti + 8] = keep(has_down, land_row[which, 1])

        def place(t, ok):
            from_west = keep(jnp.logical_and(ok, has_west), land_col[which, 0, t])
            from_east = keep(jnp.logical_and(ok, has_east), land_col[which, 1, t])
            return (
                jnp.where(first_four, pltpu.roll(from_west, 4, 1), pltpu.roll(from_east, 124, 1)),
                jnp.where(first_four, from_west, pltpu.roll(from_east, 120, 1)),
            )

        hx[0] = place(0, has_up)[1]
        hx[kg + 1] = place(kt + 1, has_down)[0]

        @pl.loop(1, kt + 1, unroll=min(4, kt))
        def _(t):
            hx[2 * t - 1], hx[2 * t] = place(t, True)

    def fill(dst, src, first, n, q, turned):
        for r in range(8):
            x = src[first + 16 * n + q + r]
            at = q + r + PACK - 4
            edge = pltpu.roll(hx[n + at // PACK], (PACK - at % PACK) % PACK * 8, 1)
            before = jnp.where(lane < 4, edge, pltpu.roll(x, 4, 1))
            after = jnp.where(lane >= 124, edge, pltpu.roll(x, 124, 1))
            lanes = slice(128 * r, 128 * (r + 1))
            dst[:ch, lanes] = after if turned else before
            dst[ch : 2 * ch, lanes] = x
            dst[2 * ch :, lanes] = before if turned else after

    def halves(x):
        return [x[:, :512], x[:, 512:]]

    def spread(parts, g, order):
        for s in range(len(parts) + 2):
            terms = [
                parts[s - k][a * ch : (a + 1) * ch]
                for k, a in enumerate(order)
                if 0 <= s - k < len(parts)
            ]
            total = terms[0]
            for term in terms[1:]:
                total = total + term
            for r in range(4):
                at = pl.ds(pl.multiple_of((4 * (g + s) + r) * wch, 8), ch)
                term = total[:, 128 * r : 128 * (r + 1)]
                gt[at, :] = gt[at, :] + term if s < 2 else term

    if comm:
        drain(land_row.at[0], h_recv.at[0, 0])
        drain(land_col.at[0], h_recv.at[0, 1])
    unpack_edges(cot_t, 0, 0)
    gt[: 8 * wch] = jnp.zeros((8 * wch, 128), F32)
    wg_acc[...] = jnp.zeros_like(wg_acc)

    def p_kernel():
        fill(terms.at[0], cot_t, 0, 0, 0, True)

        def acts(first):
            return jnp.concatenate(
                [
                    jnp.concatenate([act_t[first + 4 * a + r] for r in range(8)], axis=1)
                    for a in range(3)
                ],
                axis=0,
            )

        @pl.loop(0, ti // 16, step=STEP)
        def _(n):
            grad = 0
            for m in range(n_chunks):
                j = 2 * n + m
                grad = grad + dot(terms[j], acts(8 * j), NT)
                fill(terms.at[j + 1], cot_t, 0, n + (m + 1) // 2, 8 * ((m + 1) % 2), True)
            wg_acc[...] += grad

        wg_acc[...] += dot(terms[ti // 8], acts(ti), NT)

    def p_back():
        @pl.loop(0, ti // 16, step=STEP)
        def _(n):
            parts = []
            for m in range(n_chunks):
                parts += halves(dot(wb[...], terms[2 * n + m]))
            spread(parts, 4 * n, (0, 1, 2))

        spread(halves(dot(wb[...], terms[ti // 8])), ng, (0, 1, 2))

    n_chunks = 2 * STEP
    p_kernel()

    taps = 9
    owners = [min(2 * k, nc - 1) for k in range(taps)]
    is_owner = functools.reduce(jnp.logical_or, [col == c for c in owners])
    mine = jnp.where(col == owners[-1], taps - 1, col // 2)
    half = ch // 2
    for k in range(taps):
        a, b = k // 3, k % 3
        tap = wg_acc[b * ch : (b + 1) * ch, a * ch : (a + 1) * ch]
        wgs[k] = jnp.concatenate([tap[:half], tap[half:]], axis=1).astype(BF)
    for k, c in enumerate(owners):
        move = remote(wgs.at[k], land_a.at[col], w_send.at[0], w_recv.at[0], (row, c))

        @pl.when(col == c)
        def _():
            land_a[col] = wgs[k]

        if comm:

            @pl.when(col != c)
            def _():
                move.start()


    p_back()

    def each(refs):
        total = refs[0].astype(F32)
        for k in range(1, refs.shape[0]):
            total = total + refs[k].astype(F32)
        return total

    @pl.when(is_owner)
    def _():
        if comm:
            drain(land_a.at[pl.ds(0, nc - 1)], w_recv.at[0])
        land_b[row] = each(land_a)
        if comm:
            for d in range(1, nr):
                to = (lax.rem(row + d, nr), col)
                remote(land_b.at[row], land_b.at[row], w_send.at[1], w_recv.at[1], to).start()

    lg_acc[...] = jnp.zeros_like(lg_acc)

    def p_grad():
        @pl.loop(0, ch, step=16)
        def _(c):
            lg = 0
            for half in (c, c + 4, c + 8, c + 12):
                grads = []
                for m in range(4):
                    g = gt[pl.ds(8 * wch + half + m, ti, stride=wch), :]
                    pg = (cot_n[half + m].astype(F32) + g * slope_n[half + m].astype(F32)).astype(BF)
                    cot_n[half + m] = pg
                    grads.append(pg)
                grads = jnp.concatenate(grads, axis=1)
                mixes = jnp.concatenate([mix[half + m] for m in range(4)], axis=1)
                lg = lg + dot(mixes, grads, NT)
                mg = dot(left_t[...], grads)
                for m in range(4):
                    mgf[pl.ds(half + m, outer, stride=wch), :] = mg[:, 128 * m : 128 * (m + 1)]
            lg_acc[...] += lg

    p_grad()

    mg = jnp.concatenate([mgf[p * wch : p * wch + ch, :] for p in range(outer)], axis=0)
    mg_hi = mg.astype(BF)
    mg_lo = (mg - mg_hi.astype(F32)).astype(BF)
    rg = (dot(ow_q[...], mg_hi) + dot(ow_q[...], mg_lo)).T
    rg_out[...] = rg.reshape(nr, own, outer)
    lg_out[...] = lg_acc[...].T.reshape(nc, own, outer)
    land_l[col] = lg_out[col]
    if comm:
        for d in range(1, nc):
            other = lax.rem(col + d, nc)
            remote(
                lg_out.at[other], land_l.at[col], g_send.at[0], g_recv.at[0], (row, other)
            ).start()
        for k in range(nr):
            r, c = source(k)
            me = jnp.logical_and(r == row, c == col)
            far = remote(rg_out.at[k], land_r.at[row], g_send.at[1], g_recv.at[1], (r, c))
            near = pltpu.make_async_copy(rg_out.at[k], land_r.at[row], g_recv.at[1])

            @pl.when(me)
            def _():
                near.start()

            @pl.when(jnp.logical_not(me))
            def _():
                far.start()

    @pl.when(is_owner)
    def _():
        if comm:
            drain(land_b.at[pl.ds(0, nr - 1)], w_recv.at[1])
        fin[mine] = (each(land_b) * (1.0 / residues)).astype(BF)
        if comm:
            for d in range(1, nc):
                to = (row, lax.rem(col + d, nc))
                remote(fin.at[mine], fin.at[mine], w_send.at[2], w_recv.at[2], to).start()

    if comm:
        drain(land_row.at[1], h_recv.at[1, 0])
        drain(land_col.at[1], h_recv.at[1, 1])
    unpack_edges(act_t, 4, 1)
    gt[: 8 * wch] = jnp.zeros((8 * wch, 128), F32)

    fill(even, act_t, 4, 0, 0, False)

    def p_forward(first, last):
        @pl.loop(first, last, step=STEP)
        def _(n):
            parts = []
            for m in range(STEP):
                parts += halves(dot(wf[...], even[...]))
                fill(odd, act_t, 4, n + m, 8, False)
                parts += halves(dot(wf[...], odd[...]))
                fill(even, act_t, 4, n + m, 16, False)
            spread(parts, 4 * n, (2, 1, 0))

    p_forward(0, ti // 16)
    spread(halves(dot(wf[...], even[...])), ng, (2, 1, 0))

    if comm:
        drain(land_l.at[pl.ds(0, nc - 1)], g_recv.at[0])
        drain(land_r, g_recv.at[1])
    lg = land_l[0]
    for k in range(1, nc):
        lg = lg + land_l[k]
    rg = land_r[0]
    for k in range(1, nr):
        rg = rg + land_r[k]

    def exact(x, w):
        total = jnp.zeros((own, w.shape[1]), F32)
        for _ in range(3):
            head = x.astype(BF)
            total = total + dot(head, w)
            x = x - head.astype(F32)
        return total

    fg_out[...] = (exact(lg, lw[...]) + exact(rg, rw[...])) * (1.0 / math.sqrt(residues))

    if comm:
        drain_some(fin, w_recv.at[2], is_owner)
    for k in range(taps):
        tap = fin[k].astype(F32)
        wg_out[k] = jnp.concatenate([tap[:, :ch], tap[:, ch:]], axis=0)

    if comm:
        drain(left_in.at[pl.ds(0, nc - 1)], f_send.at[0])
        drain_some(right_in, f_send.at[1], goal == col)
        for which in range(2):
            drain(land_row.at[which], h_send.at[which, 0])
            drain(land_col.at[which], h_send.at[which, 1])
        drain_some(wgs, w_send.at[0], is_owner)
        drain(land_l.at[pl.ds(0, nc - 1)], g_send.at[0])
        drain_some(land_r, g_send.at[1], goal == col)

        @pl.when(is_owner)
        def _():
            drain(land_b.at[pl.ds(0, nr - 1)], w_send.at[1])
            drain(land_a.at[pl.ds(0, nc - 1)], w_send.at[2])


def last_kernel(
    hid_n, pg_n, gt, wg_in, fg_in, bias, po_hbm, pg_hbm, wg_hbm, fg_hbm, out_n, out_sem
):
    ch, ti, _ = hid_n.shape
    wch = ch + 8
    step = ch // 4
    copies = [
        pltpu.make_async_copy(
            pg_n.at[pl.ds(k * step, step)], pg_hbm.at[pl.ds(k * step, step)], out_sem.at[k]
        )
        for k in range(4)
    ]
    copies.append(pltpu.make_async_copy(wg_in, wg_hbm, out_sem.at[4]))
    copies.append(pltpu.make_async_copy(fg_in, fg_hbm, out_sem.at[5]))
    for copy in copies:
        copy.start()
    for k in range(ti // BLOCK):

        @pl.loop(0, ch, unroll=16)
        def _(c):
            conv = gt[pl.ds((8 + BLOCK * k) * wch + c, BLOCK, stride=wch), :]
            h = hid_n[c, pl.ds(BLOCK * k, BLOCK), :].astype(F32)
            out_n[c, pl.ds(BLOCK * k, BLOCK), :] = (h + bias[c] + conv).astype(BF)

        copy = pltpu.make_async_copy(
            out_n.at[:, pl.ds(BLOCK * k, BLOCK)], po_hbm.at[:, pl.ds(BLOCK * k, BLOCK)],
            out_sem.at[6 + k],
        )
        copy.start()
        copies.append(copy)
    for copy in copies:
        copy.wait()


def call(nr, nc, residues, comm, pair_map, features, lw, rw, ow, cw, bias, cot):
    ch, ti, tj = pair_map.shape
    own, feat = features.shape
    outer = lw.shape[1]
    kg = ti // PACK
    any_spec = pl.BlockSpec(memory_space=pl.ANY)
    vmem = pl.BlockSpec(memory_space=pltpu.VMEM)
    smem = pl.BlockSpec(memory_space=pltpu.SMEM)
    V = pltpu.VMEM
    dma = pltpu.SemaphoreType.DMA
    scratch = [
        V((ch, ti, tj), BF),
        V((max(ch * (ti + 8), ti * (ch + 8)), 128), F32),
        V((ti + 8, ch, 128), BF),
        V((ti + 16, ch, 128), BF),
        V((kg + 2, ch, 128), BF),
        V((ti // 8 + 1, 3 * ch, 1024), BF),
        V((3 * ch, 1024), BF),
        V((3 * ch, 1024), BF),
        V((2, 2, kg // 2, ch, 128), BF),
        V((2, 2, 4, ch, 128), BF),
        V((2, 2, kg // 2 + 2, ch, 128), BF),
        V((own, 128), BF),
        V((nc, own, 128), BF),
        V((nr, own, 128), BF),
        V((ti, outer), BF),
        V((outer, ti), BF),
        V((outer * (ch + 8), 128), F32),
        V((ch, outer, 128), BF),
        V((3 * ch, 3 * ch), BF),
        V((3 * ch, 3 * ch), BF),
        V((outer, outer * ch), BF),
        V((outer * ch, outer), BF),
        V((outer * (ch + 8), 128), F32),
        V((3 * ch, 3 * ch), F32),
        V((9, ch // 2, 2 * ch), BF),
        V((nc, ch // 2, 2 * ch), BF),
        V((nr, ch // 2, 2 * ch), F32),
        V((9, ch // 2, 2 * ch), BF),
        V((outer, ti), F32),
        V((nc, own, outer), F32),
        V((nr, own, outer), F32),
        V((nc, own, outer), F32),
        V((nr, own, outer), F32),
        dma((ch // 8 + 1,)),
        dma((2,)),
        dma((2,)),
        dma((2, 2)),
        dma((2, 2)),
        dma((3,)),
        dma((3,)),
        dma((2,)),
        dma((2,)),
    ]
    macs = ti * tj * (27 * ch * ch + 3 * outer * ch)
    out = pl.pallas_call(
        functools.partial(kernel, nr, nc, ch, ti, outer, comm, residues),
        out_shape=[
            V((ch, ti, tj), BF),
            V((ch, ti, tj), BF),
            V(((ti + 20) * (ch + 8), 128), F32),
            V((9, ch, ch), F32),
            V((own, feat), F32),
        ],
        in_specs=[any_spec, any_spec] + [vmem] * 5,
        out_specs=[vmem] * 5,
        scratch_shapes=scratch,
        compiler_params=pltpu.CompilerParams(
            collective_id=0 if comm else None,
            has_side_effects=True,
            vmem_limit_bytes=44 * 1024 * 1024,
        ),
        cost_estimate=pl.CostEstimate(
            flops=2 * macs, bytes_accessed=8 * ch * ti * tj, transcendentals=2 * ch * ti * tj
        ),
    )(cot, pair_map, features, lw.T, rw.T, ow, cw.reshape(9, ch, ch))
    kept = [pltpu.with_memory_space_constraint(x, pltpu.VMEM) for x in out]
    po, pg, wg, fg = pl.pallas_call(
        last_kernel,
        out_shape=[
            jax.ShapeDtypeStruct((ch, ti, tj), BF),
            jax.ShapeDtypeStruct((ch, ti, tj), BF),
            jax.ShapeDtypeStruct((9, ch, ch), F32),
            jax.ShapeDtypeStruct((own, feat), F32),
        ],
        in_specs=[vmem] * 5 + [smem],
        out_specs=[any_spec] * 4,
        scratch_shapes=[V((ch, ti, tj), BF), dma((6 + ti // BLOCK,))],
        compiler_params=pltpu.CompilerParams(vmem_limit_bytes=24 * 1024 * 1024),
        cost_estimate=pl.CostEstimate(
            flops=2 * ch * ti * tj, bytes_accessed=4 * ch * ti * tj, transcendentals=0
        ),
    )(*kept, bias)
    return po, pg, wg.reshape(3, 3, ch, ch), fg


def solution(mesh):
    nr, nc = mesh.shape["row"], mesh.shape["col"]

    def shards(pair_map, features, lw, rw, ow, cw, bias, cot):
        return call(
            nr, nc, pair_map.shape[1] * nr, True, pair_map, features, lw, rw, ow, cw, bias, cot
        )

    in_specs = (
        P(None, "row", "col"),
        P(("row", "col"), None),
        P(),
        P(),
        P(),
        P(),
        P(),
        P(None, "row", "col"),
    )
    out_specs = (P(None, "row", "col"), P(None, "row", "col"), P(), P(("row", "col"), None))
    return jax.shard_map(shards, mesh=mesh, in_specs=in_specs, out_specs=out_specs, check_vma=False)
```

```python
import functools
import math

import jax
import jax.numpy as jnp
from jax import lax
from jax.experimental import pallas as pl
from jax.experimental.pallas import tpu as pltpu
from jax.sharding import PartitionSpec as P

MESH = pl.DeviceIdType.MESH
BF = jnp.bfloat16
F32 = jnp.float32
NT = (((1,), (1,)), ((), ()))
PACK = 16
BLOCK = 32
STEP = 8


def dot(a, b, dims=None):
    if dims is None:
        return jnp.dot(a, b, preferred_element_type=F32)
    return lax.dot_general(a, b, dims, preferred_element_type=F32)


def kernel(
    nr, nc, ch, ti, outer, comm, residues,
    cot_hbm, pm_hbm, feat, lw, rw, ow, cw,
    hid_n, cot_n, gt, wg_out, fg_out,
    slope_n, wide, cot_t, act_t, hx, terms, even, odd, packs, land_row, land_col,
    lr, left_in, right_in, left, left_t, mixf, mix, wf, wb, ow_q, ow_t, mgf,
    wg_acc, wgs, land_a, land_b, fin, lg_acc, lg_out, rg_out, land_l, land_r,
    in_sem, f_send, f_recv, h_send, h_recv, w_send, w_recv, g_send, g_recv,
):
    row = lax.axis_index("row")
    col = lax.axis_index("col")
    kg = ti // PACK
    ng = ti // 4
    pitch = ti + 8
    wch = ch + 8
    own = lr.shape[0]
    flat = row * nc + col
    goal = flat // nr
    slot = lax.rem(flat, nr)
    up, down = lax.rem(row + nr - 1, nr), lax.rem(row + 1, nr)
    west, east = lax.rem(col + nc - 1, nc), lax.rem(col + 1, nc)
    cstep = 8
    nchunk = ch // cstep

    def source(k):
        f = col * nr + k
        return f // nc, lax.rem(f, nc)

    if comm:
        barrier = pltpu.get_barrier_semaphore()

        def greet(r, c):
            pl.semaphore_signal(barrier, inc=1, device_id=(r, c), device_id_type=MESH)

        def greet_unless_me(r, c):
            @pl.when(jnp.logical_or(r != row, c != col))
            def _():
                greet(r, c)

        for d in range(1, nc):
            greet(row, lax.rem(col + d, nc))
        for d in range(1, nr):
            greet(lax.rem(row + d, nr), col)
        for r in (up, down):
            for c in (west, east):
                greet(r, c)
        for k in range(nr):
            greet_unless_me(k, goal)
            greet_unless_me(*source(k))
        total_greets = (nc - 1) + (nr - 1) + 4 + 2 * nr - jnp.where(goal == col, 2, 0)

    cot_in = [
        pltpu.make_async_copy(
            cot_hbm.at[pl.ds(k * cstep, cstep)], cot_n.at[pl.ds(k * cstep, cstep)], in_sem.at[k]
        )
        for k in range(nchunk)
    ]
    pm_in = pltpu.make_async_copy(pm_hbm, hid_n, in_sem.at[nchunk])
    for copy in cot_in:
        copy.start()
    pm_in.start()

    lr[...] = jnp.concatenate(
        [dot(feat[...], lw[...], NT), dot(feat[...], rw[...], NT), jnp.zeros((own, 128 - 2 * outer), F32)],
        axis=1,
    ).astype(BF)

    def remote(src, dst, ssem, rsem, dev):
        return pltpu.make_async_remote_copy(
            src_ref=src, dst_ref=dst, send_sem=ssem, recv_sem=rsem, device_id=dev, device_id_type=MESH
        )

    def drain(blocks, sem):
        pltpu.make_async_copy(blocks, blocks, sem).wait()

    def drain_some(blocks, sem, one_less):
        @pl.when(one_less)
        def _():
            drain(blocks.at[pl.ds(0, blocks.shape[0] - 1)], sem)

        @pl.when(jnp.logical_not(one_less))
        def _():
            drain(blocks, sem)

    left_in[col] = lr[...]
    if comm:
        pl.semaphore_wait(barrier, total_greets)
        for k in range(nr):
            me = jnp.logical_and(row == k, goal == col)
            far = remote(lr, right_in.at[slot], f_send.at[1], f_recv.at[1], (k, goal))
            near = pltpu.make_async_copy(lr, right_in.at[slot], f_recv.at[1])

            @pl.when(me)
            def _():
                near.start()

            @pl.when(jnp.logical_not(me))
            def _():
                far.start()

        for d in range(1, nc):
            remote(
                lr, left_in.at[col], f_send.at[0], f_recv.at[0], (row, lax.rem(col + d, nc))
            ).start()

    for a in range(3):
        wf[a * ch : (a + 1) * ch, :] = jnp.concatenate([cw[3 * a + b] for b in range(3)], axis=1)
        wb[a * ch : (a + 1) * ch, :] = jnp.concatenate(
            [cw[3 * a + b].astype(F32).T for b in range(3)], axis=1
        ).astype(BF)
    ow_q[...] = jnp.concatenate([ow[p] for p in range(outer)], axis=1)
    step = 512
    for k in range(outer * ch // step):
        ow_t[k * step : (k + 1) * step, :] = ow_q[:, k * step : (k + 1) * step].astype(F32).T.astype(BF)

    def p_widen():
        for k in range(nchunk):
            cot_in[k].wait()

            @pl.loop(0, cstep, unroll=8)
            def _(c):
                at = pl.multiple_of((k * cstep + c) * pitch, 8)
                wide[pl.ds(at, ti), :] = cot_n[k * cstep + c].astype(F32)

    p_widen()

    lane = lax.broadcasted_iota(jnp.int32, (ch, 128), 1)
    window = lax.rem(lane + 4, 128) // 8

    first_four = lax.rem(lane, 8) < 4
    kt = kg // 2

    def to_rows(dst, first, which, read):
        @pl.loop(0, kt, unroll=min(4, kt))
        def _(t):
            lines = []
            for k in range(2):
                packed = None
                for m in range(PACK):
                    row_at = 2 * PACK * t + PACK * k + m
                    x = read(row_at).astype(BF)
                    dst[first + row_at] = x
                    packed = x if m == 0 else jnp.where(window == m, pltpu.roll(x, 8 * m, 1), packed)
                lines.append(packed)
            moved = pltpu.roll(lines[1], 4, 1)
            packs[which, 0, t] = jnp.where(first_four, lines[0], moved)
            packs[which, 1, t] = jnp.where(first_four, moved, lines[0])

    def halo_moves(src, first, which):
        low, high = packs.at[which, 0], packs.at[which, 1]
        from_west, from_east = land_col.at[which, 0], land_col.at[which, 1]
        plan = [
            (src.at[pl.ds(first, 4)], land_row.at[which, 1], (up, col)),
            (src.at[pl.ds(first + ti - 4, 4)], land_row.at[which, 0], (down, col)),
            (low, from_east.at[pl.ds(1, kt)], (row, west)),
            (high, from_west.at[pl.ds(1, kt)], (row, east)),
            (low.at[0], from_east.at[kt + 1], (up, west)),
            (high.at[0], from_west.at[kt + 1], (up, east)),
            (low.at[kt - 1], from_east.at[0], (down, west)),
            (high.at[kt - 1], from_west.at[0], (down, east)),
        ]
        return [
            remote(s, d, h_send.at[which, min(m // 2, 1)], h_recv.at[which, min(m // 2, 1)], dev)
            for m, (s, d, dev) in enumerate(plan)
        ]

    to_rows(cot_t, 4, 0, lambda i: wide[pl.ds(i, ch, stride=pitch), :])
    cot_moves = halo_moves(cot_t, 4, 0)
    if comm:
        for move in cot_moves:
            move.start()

    if comm:
        drain(left_in.at[pl.ds(0, nc - 1)], f_recv.at[0])
        drain(right_in, f_recv.at[1])
    left[...] = left_in[...].reshape(nc * own, 128)[:, :outer]
    left_t[...] = left[...].astype(F32).T.astype(BF)
    right = right_in[...].reshape(nr * own, 128)[:, outer : 2 * outer]
    for k in range(outer * ch // step):
        rows = dot(ow_t[k * step : (k + 1) * step, :], right, NT).astype(BF).astype(F32)
        for m in range(step // ch):
            at = (k * (step // ch) + m) * wch
            mixf[at : at + ch, :] = rows[m * ch : (m + 1) * ch]

    @pl.loop(0, ch, unroll=8)
    def _(c):
        mix[c] = mixf[pl.ds(c, outer, stride=wch), :].astype(BF)

    pm_in.wait()

    def p_hidden():
        def update(c):
            return dot(left[...], jnp.concatenate([mix[c], mix[c + 1]], axis=1))

        def finish(c, change):
            for k in range(2):
                hidden = (hid_n[c + k].astype(F32) + change[:, 128 * k : 128 * (k + 1)]).astype(BF)
                hid_n[c + k] = hidden
                h = hidden.astype(F32)
                e = jnp.minimum(jnp.exp(h), 1.0)
                slope_n[c + k] = e.astype(BF)
                wide[pl.ds(c + k, ti, stride=wch), :] = jnp.maximum(h, e - 1.0)

        @pl.loop(0, ch, step=16)
        def _(c):
            changes = [update(c + 2 * k) for k in range(8)]
            for k in range(8):
                finish(c + 2 * k, changes[k])

    p_hidden()

    to_rows(act_t, 8, 1, lambda i: wide[pl.ds(pl.multiple_of(i * wch, 8), ch), :])
    for s in (0, 4, ti + 8, ti + 12):
        act_t[s : s + 4] = jnp.zeros((4, ch, 128), BF)
    act_moves = halo_moves(act_t, 8, 1)
    if comm:
        for move in act_moves:
            move.start()

    has_up, has_down, has_west, has_east = row > 0, row < nr - 1, col > 0, col < nc - 1

    def keep(ok, x):
        return jnp.where(ok, x, jnp.zeros_like(x))

    def unpack_edges(dst, first, which):
        dst[first : first + 4] = keep(has_up, land_row[which, 0])
        dst[first + ti + 4 : first + ti + 8] = keep(has_down, land_row[which, 1])

        def place(t, ok):
            from_west = keep(jnp.logical_and(ok, has_west), land_col[which, 0, t])
            from_east = keep(jnp.logical_and(ok, has_east), land_col[which, 1, t])
            return (
                jnp.where(first_four, pltpu.roll(from_west, 4, 1), pltpu.roll(from_east, 124, 1)),
                jnp.where(first_four, from_west, pltpu.roll(from_east, 120, 1)),
            )

        hx[0] = place(0, has_up)[1]
        hx[kg + 1] = place(kt + 1, has_down)[0]

        @pl.loop(1, kt + 1, unroll=min(4, kt))
        def _(t):
            hx[2 * t - 1], hx[2 * t] = place(t, True)

    def fill(dst, src, first, n, q, turned):
        for r in range(8):
            x = src[first + 16 * n + q + r]
            at = q + r + PACK - 4
            edge = pltpu.roll(hx[n + at // PACK], (PACK - at % PACK) % PACK * 8, 1)
            before = jnp.where(lane < 4, edge, pltpu.roll(x, 4, 1))
            after = jnp.where(lane >= 124, edge, pltpu.roll(x, 124, 1))
            lanes = slice(128 * r, 128 * (r + 1))
            dst[:ch, lanes] = after if turned else before
            dst[ch : 2 * ch, lanes] = x
            dst[2 * ch :, lanes] = before if turned else after

    def halves(x):
        return [x[:, :512], x[:, 512:]]

    def spread(parts, g, order):
        for s in range(len(parts) + 2):
            terms = [
                parts[s - k][a * ch : (a + 1) * ch]
                for k, a in enumerate(order)
                if 0 <= s - k < len(parts)
            ]
            total = terms[0]
            for term in terms[1:]:
                total = total + term
            for r in range(4):
                at = pl.ds(pl.multiple_of((4 * (g + s) + r) * wch, 8), ch)
                term = total[:, 128 * r : 128 * (r + 1)]
                gt[at, :] = gt[at, :] + term if s < 2 else term

    if comm:
        drain(land_row.at[0], h_recv.at[0, 0])
        drain(land_col.at[0], h_recv.at[0, 1])
    unpack_edges(cot_t, 0, 0)
    gt[: 8 * wch] = jnp.zeros((8 * wch, 128), F32)
    wg_acc[...] = jnp.zeros_like(wg_acc)

    def p_kernel():
        fill(terms.at[0], cot_t, 0, 0, 0, True)

        def acts(first):
            return jnp.concatenate(
                [
                    jnp.concatenate([act_t[first + 4 * a + r] for r in range(8)], axis=1)
                    for a in range(3)
                ],
                axis=0,
            )

        @pl.loop(0, ti // 16, step=STEP)
        def _(n):
            grad = 0
            for m in range(n_chunks):
                j = 2 * n + m
                grad = grad + dot(terms[j], acts(8 * j), NT)
                fill(terms.at[j + 1], cot_t, 0, n + (m + 1) // 2, 8 * ((m + 1) % 2), True)
            wg_acc[...] += grad

        wg_acc[...] += dot(terms[ti // 8], acts(ti), NT)

    def p_back():
        @pl.loop(0, ti // 16, step=STEP)
        def _(n):
            parts = []
            for m in range(n_chunks):
                parts += halves(dot(wb[...], terms[2 * n + m]))
            spread(parts, 4 * n, (0, 1, 2))

        spread(halves(dot(wb[...], terms[ti // 8])), ng, (0, 1, 2))

    n_chunks = 2 * STEP
    p_kernel()

    taps = 9
    owners = [min(2 * k, nc - 1) for k in range(taps)]
    is_owner = functools.reduce(jnp.logical_or, [col == c for c in owners])
    mine = jnp.where(col == owners[-1], taps - 1, col // 2)
    half = ch // 2
    for k in range(taps):
        a, b = k // 3, k % 3
        tap = wg_acc[b * ch : (b + 1) * ch, a * ch : (a + 1) * ch]
        wgs[k] = jnp.concatenate([tap[:half], tap[half:]], axis=1).astype(BF)
    for k, c in enumerate(owners):
        move = remote(wgs.at[k], land_a.at[col], w_send.at[0], w_recv.at[0], (row, c))

        @pl.when(col == c)
        def _():
            land_a[col] = wgs[k]

        if comm:

            @pl.when(col != c)
            def _():
                move.start()


    p_back()

    def each(refs):
        total = refs[0].astype(F32)
        for k in range(1, refs.shape[0]):
            total = total + refs[k].astype(F32)
        return total

    @pl.when(is_owner)
    def _():
        if comm:
            drain(land_a.at[pl.ds(0, nc - 1)], w_recv.at[0])
        land_b[row] = each(land_a)
        if comm:
            for d in range(1, nr):
                to = (lax.rem(row + d, nr), col)
                remote(land_b.at[row], land_b.at[row], w_send.at[1], w_recv.at[1], to).start()

    lg_acc[...] = jnp.zeros_like(lg_acc)

    def p_grad():
        @pl.loop(0, ch, step=16)
        def _(c):
            lg = 0
            for half in (c, c + 4, c + 8, c + 12):
                grads = []
                for m in range(4):
                    g = gt[pl.ds(8 * wch + half + m, ti, stride=wch), :]
                    pg = (cot_n[half + m].astype(F32) + g * slope_n[half + m].astype(F32)).astype(BF)
                    cot_n[half + m] = pg
                    grads.append(pg)
                grads = jnp.concatenate(grads, axis=1)
                mixes = jnp.concatenate([mix[half + m] for m in range(4)], axis=1)
                lg = lg + dot(mixes, grads, NT)
                mg = dot(left_t[...], grads)
                for m in range(4):
                    mgf[pl.ds(half + m, outer, stride=wch), :] = mg[:, 128 * m : 128 * (m + 1)]
            lg_acc[...] += lg

    p_grad()

    mg = jnp.concatenate([mgf[p * wch : p * wch + ch, :] for p in range(outer)], axis=0)
    mg_hi = mg.astype(BF)
    mg_lo = (mg - mg_hi.astype(F32)).astype(BF)
    rg = (dot(ow_q[...], mg_hi) + dot(ow_q[...], mg_lo)).T
    rg_out[...] = rg.reshape(nr, own, outer)
    lg_out[...] = lg_acc[...].T.reshape(nc, own, outer)
    land_l[col] = lg_out[col]
    if comm:
        for d in range(1, nc):
            other = lax.rem(col + d, nc)
            remote(
                lg_out.at[other], land_l.at[col], g_send.at[0], g_recv.at[0], (row, other)
            ).start()
        for k in range(nr):
            r, c = source(k)
            me = jnp.logical_and(r == row, c == col)
            far = remote(rg_out.at[k], land_r.at[row], g_send.at[1], g_recv.at[1], (r, c))
            near = pltpu.make_async_copy(rg_out.at[k], land_r.at[row], g_recv.at[1])

            @pl.when(me)
            def _():
                near.start()

            @pl.when(jnp.logical_not(me))
            def _():
                far.start()

    @pl.when(is_owner)
    def _():
        if comm:
            drain(land_b.at[pl.ds(0, nr - 1)], w_recv.at[1])
        fin[mine] = (each(land_b) * (1.0 / residues)).astype(BF)
        if comm:
            for d in range(1, nc):
                to = (row, lax.rem(col + d, nc))
                remote(fin.at[mine], fin.at[mine], w_send.at[2], w_recv.at[2], to).start()

    if comm:
        drain(land_row.at[1], h_recv.at[1, 0])
        drain(land_col.at[1], h_recv.at[1, 1])
    unpack_edges(act_t, 4, 1)
    gt[: 8 * wch] = jnp.zeros((8 * wch, 128), F32)

    fill(even, act_t, 4, 0, 0, False)

    def p_forward(first, last):
        @pl.loop(first, last, step=STEP)
        def _(n):
            parts = []
            for m in range(STEP):
                parts += halves(dot(wf[...], even[...]))
                fill(odd, act_t, 4, n + m, 8, False)
                parts += halves(dot(wf[...], odd[...]))
                fill(even, act_t, 4, n + m, 16, False)
            spread(parts, 4 * n, (2, 1, 0))

    p_forward(0, ti // 16)
    spread(halves(dot(wf[...], even[...])), ng, (2, 1, 0))

    if comm:
        drain(land_l.at[pl.ds(0, nc - 1)], g_recv.at[0])
        drain(land_r, g_recv.at[1])
    lg = land_l[0]
    for k in range(1, nc):
        lg = lg + land_l[k]
    rg = land_r[0]
    for k in range(1, nr):
        rg = rg + land_r[k]

    def exact(x, w):
        total = jnp.zeros((own, w.shape[1]), F32)
        for _ in range(3):
            head = x.astype(BF)
            total = total + dot(head, w)
            x = x - head.astype(F32)
        return total

    fg_out[...] = (exact(lg, lw[...]) + exact(rg, rw[...])) * (1.0 / math.sqrt(residues))

    if comm:
        drain_some(fin, w_recv.at[2], is_owner)
    for k in range(taps):
        tap = fin[k].astype(F32)
        wg_out[k] = jnp.concatenate([tap[:, :ch], tap[:, ch:]], axis=0)

    if comm:
        drain(left_in.at[pl.ds(0, nc - 1)], f_send.at[0])
        drain_some(right_in, f_send.at[1], goal == col)
        for which in range(2):
            drain(land_row.at[which], h_send.at[which, 0])
            drain(land_col.at[which], h_send.at[which, 1])
        drain_some(wgs, w_send.at[0], is_owner)
        drain(land_l.at[pl.ds(0, nc - 1)], g_send.at[0])
        drain_some(land_r, g_send.at[1], goal == col)

        @pl.when(is_owner)
        def _():
            drain(land_b.at[pl.ds(0, nr - 1)], w_send.at[1])
            drain(land_a.at[pl.ds(0, nc - 1)], w_send.at[2])


def last_kernel(
    hid_n, pg_n, gt, wg_in, fg_in, bias, po_hbm, pg_hbm, wg_hbm, fg_hbm, out_n, out_sem
):
    ch, ti, _ = hid_n.shape
    wch = ch + 8
    step = ch // 4
    copies = [
        pltpu.make_async_copy(
            pg_n.at[pl.ds(k * step, step)], pg_hbm.at[pl.ds(k * step, step)], out_sem.at[k]
        )
        for k in range(4)
    ]
    copies.append(pltpu.make_async_copy(wg_in, wg_hbm, out_sem.at[4]))
    copies.append(pltpu.make_async_copy(fg_in, fg_hbm, out_sem.at[5]))
    for copy in copies:
        copy.start()
    for k in range(ti // BLOCK):

        @pl.loop(0, ch, unroll=16)
        def _(c):
            conv = gt[pl.ds((8 + BLOCK * k) * wch + c, BLOCK, stride=wch), :]
            h = hid_n[c, pl.ds(BLOCK * k, BLOCK), :].astype(F32)
            out_n[c, pl.ds(BLOCK * k, BLOCK), :] = (h + bias[c] + conv).astype(BF)

        copy = pltpu.make_async_copy(
            out_n.at[:, pl.ds(BLOCK * k, BLOCK)], po_hbm.at[:, pl.ds(BLOCK * k, BLOCK)],
            out_sem.at[6 + k],
        )
        copy.start()
        copies.append(copy)
    for copy in copies:
        copy.wait()


def call(nr, nc, residues, comm, pair_map, features, lw, rw, ow, cw, bias, cot):
    ch, ti, tj = pair_map.shape
    own, feat = features.shape
    outer = lw.shape[1]
    kg = ti // PACK
    any_spec = pl.BlockSpec(memory_space=pl.ANY)
    vmem = pl.BlockSpec(memory_space=pltpu.VMEM)
    smem = pl.BlockSpec(memory_space=pltpu.SMEM)
    V = pltpu.VMEM
    dma = pltpu.SemaphoreType.DMA
    scratch = [
        V((ch, ti, tj), BF),
        V((max(ch * (ti + 8), ti * (ch + 8)), 128), F32),
        V((ti + 8, ch, 128), BF),
        V((ti + 16, ch, 128), BF),
        V((kg + 2, ch, 128), BF),
        V((ti // 8 + 1, 3 * ch, 1024), BF),
        V((3 * ch, 1024), BF),
        V((3 * ch, 1024), BF),
        V((2, 2, kg // 2, ch, 128), BF),
        V((2, 2, 4, ch, 128), BF),
        V((2, 2, kg // 2 + 2, ch, 128), BF),
        V((own, 128), BF),
        V((nc, own, 128), BF),
        V((nr, own, 128), BF),
        V((ti, outer), BF),
        V((outer, ti), BF),
        V((outer * (ch + 8), 128), F32),
        V((ch, outer, 128), BF),
        V((3 * ch, 3 * ch), BF),
        V((3 * ch, 3 * ch), BF),
        V((outer, outer * ch), BF),
        V((outer * ch, outer), BF),
        V((outer * (ch + 8), 128), F32),
        V((3 * ch, 3 * ch), F32),
        V((9, ch // 2, 2 * ch), BF),
        V((nc, ch // 2, 2 * ch), BF),
        V((nr, ch // 2, 2 * ch), F32),
        V((9, ch // 2, 2 * ch), BF),
        V((outer, ti), F32),
        V((nc, own, outer), F32),
        V((nr, own, outer), F32),
        V((nc, own, outer), F32),
        V((nr, own, outer), F32),
        dma((ch // 8 + 1,)),
        dma((2,)),
        dma((2,)),
        dma((2, 2)),
        dma((2, 2)),
        dma((3,)),
        dma((3,)),
        dma((2,)),
        dma((2,)),
    ]
    macs = ti * tj * (27 * ch * ch + 3 * outer * ch)
    out = pl.pallas_call(
        functools.partial(kernel, nr, nc, ch, ti, outer, comm, residues),
        out_shape=[
            V((ch, ti, tj), BF),
            V((ch, ti, tj), BF),
            V(((ti + 20) * (ch + 8), 128), F32),
            V((9, ch, ch), F32),
            V((own, feat), F32),
        ],
        in_specs=[any_spec, any_spec] + [vmem] * 5,
        out_specs=[vmem] * 5,
        scratch_shapes=scratch,
        compiler_params=pltpu.CompilerParams(
            collective_id=0 if comm else None,
            has_side_effects=True,
            vmem_limit_bytes=44 * 1024 * 1024,
        ),
        cost_estimate=pl.CostEstimate(
            flops=2 * macs, bytes_accessed=8 * ch * ti * tj, transcendentals=2 * ch * ti * tj
        ),
    )(cot, pair_map, features, lw.T, rw.T, ow, cw.reshape(9, ch, ch))
    kept = [pltpu.with_memory_space_constraint(x, pltpu.VMEM) for x in out]
    po, pg, wg, fg = pl.pallas_call(
        last_kernel,
        out_shape=[
            jax.ShapeDtypeStruct((ch, ti, tj), BF),
            jax.ShapeDtypeStruct((ch, ti, tj), BF),
            jax.ShapeDtypeStruct((9, ch, ch), F32),
            jax.ShapeDtypeStruct((own, feat), F32),
        ],
        in_specs=[vmem] * 5 + [smem],
        out_specs=[any_spec] * 4,
        scratch_shapes=[V((ch, ti, tj), BF), dma((6 + ti // BLOCK,))],
        compiler_params=pltpu.CompilerParams(vmem_limit_bytes=24 * 1024 * 1024),
        cost_estimate=pl.CostEstimate(
            flops=2 * ch * ti * tj, bytes_accessed=4 * ch * ti * tj, transcendentals=0
        ),
    )(*kept, bias)
    return po, pg, wg.reshape(3, 3, ch, ch), fg


def solution(mesh):
    nr, nc = mesh.shape["row"], mesh.shape["col"]

    def shards(pair_map, features, lw, rw, ow, cw, bias, cot):
        return call(
            nr, nc, pair_map.shape[1] * nr, True, pair_map, features, lw, rw, ow, cw, bias, cot
        )

    in_specs = (
        P(None, "row", "col"),
        P(("row", "col"), None),
        P(),
        P(),
        P(),
        P(),
        P(),
        P(None, "row", "col"),
    )
    out_specs = (P(None, "row", "col"), P(None, "row", "col"), P(), P(("row", "col"), None))
    return jax.shard_map(shards, mesh=mesh, in_specs=in_specs, out_specs=out_specs, check_vma=False)
```

```python
import functools
import math

import jax
import jax.numpy as jnp
from jax import lax
from jax.experimental import pallas as pl
from jax.experimental.pallas import tpu as pltpu
from jax.sharding import PartitionSpec as P

MESH = pl.DeviceIdType.MESH
BF = jnp.bfloat16
F32 = jnp.float32
NT = (((1,), (1,)), ((), ()))
PACK = 16
BLOCK = 32
STEP = 8


def dot(a, b, dims=None):
    if dims is None:
        return jnp.dot(a, b, preferred_element_type=F32)
    return lax.dot_general(a, b, dims, preferred_element_type=F32)


def kernel(
    nr, nc, ch, ti, outer, comm, residues,
    cot_hbm, pm_hbm, feat, lw, rw, ow, cw,
    hid_n, cot_n, gt, wg_out, fg_out,
    slope_n, wide, cot_t, act_t, hx, terms, even, odd, packs, land_row, land_col,
    lr, left_in, right_in, left, left_t, mixf, mix, wf, wb, ow_q, ow_t, mgf,
    wg_acc, wgs, land_a, land_b, fin, lg_acc, lg_out, rg_out, land_l, land_r,
    in_sem, f_send, f_recv, h_send, h_recv, w_send, w_recv, g_send, g_recv,
):
    row = lax.axis_index("row")
    col = lax.axis_index("col")
    kg = ti // PACK
    ng = ti // 4
    pitch = ti + 8
    wch = ch + 8
    own = lr.shape[0]
    flat = row * nc + col
    goal = flat // nr
    slot = lax.rem(flat, nr)
    up, down = lax.rem(row + nr - 1, nr), lax.rem(row + 1, nr)
    west, east = lax.rem(col + nc - 1, nc), lax.rem(col + 1, nc)
    cstep = 8
    nchunk = ch // cstep

    def source(k):
        f = col * nr + k
        return f // nc, lax.rem(f, nc)

    if comm:
        barrier = pltpu.get_barrier_semaphore()

        def greet(r, c):
            pl.semaphore_signal(barrier, inc=1, device_id=(r, c), device_id_type=MESH)

        def greet_unless_me(r, c):
            @pl.when(jnp.logical_or(r != row, c != col))
            def _():
                greet(r, c)

        for d in range(1, nc):
            greet(row, lax.rem(col + d, nc))
        for d in range(1, nr):
            greet(lax.rem(row + d, nr), col)
        for r in (up, down):
            for c in (west, east):
                greet(r, c)
        for k in range(nr):
            greet_unless_me(k, goal)
            greet_unless_me(*source(k))
        total_greets = (nc - 1) + (nr - 1) + 4 + 2 * nr - jnp.where(goal == col, 2, 0)

    cot_in = [
        pltpu.make_async_copy(
            cot_hbm.at[pl.ds(k * cstep, cstep)], cot_n.at[pl.ds(k * cstep, cstep)], in_sem.at[k]
        )
        for k in range(nchunk)
    ]
    pm_in = pltpu.make_async_copy(pm_hbm, hid_n, in_sem.at[nchunk])
    for copy in cot_in:
        copy.start()
    pm_in.start()

    lr[...] = jnp.concatenate(
        [dot(feat[...], lw[...], NT), dot(feat[...], rw[...], NT), jnp.zeros((own, 128 - 2 * outer), F32)],
        axis=1,
    ).astype(BF)

    def remote(src, dst, ssem, rsem, dev):
        return pltpu.make_async_remote_copy(
            src_ref=src, dst_ref=dst, send_sem=ssem, recv_sem=rsem, device_id=dev, device_id_type=MESH
        )

    def drain(blocks, sem):
        pltpu.make_async_copy(blocks, blocks, sem).wait()

    def drain_some(blocks, sem, one_less):
        @pl.when(one_less)
        def _():
            drain(blocks.at[pl.ds(0, blocks.shape[0] - 1)], sem)

        @pl.when(jnp.logical_not(one_less))
        def _():
            drain(blocks, sem)

    left_in[col] = lr[...]
    if comm:
        pl.semaphore_wait(barrier, total_greets)
        for k in range(nr):
            me = jnp.logical_and(row == k, goal == col)
            far = remote(lr, right_in.at[slot], f_send.at[1], f_recv.at[1], (k, goal))
            near = pltpu.make_async_copy(lr, right_in.at[slot], f_recv.at[1])

            @pl.when(me)
            def _():
                near.start()

            @pl.when(jnp.logical_not(me))
            def _():
                far.start()

        for d in range(1, nc):
            remote(
                lr, left_in.at[col], f_send.at[0], f_recv.at[0], (row, lax.rem(col + d, nc))
            ).start()

    for a in range(3):
        wf[a * ch : (a + 1) * ch, :] = jnp.concatenate([cw[3 * a + b] for b in range(3)], axis=1)
        wb[a * ch : (a + 1) * ch, :] = jnp.concatenate(
            [cw[3 * a + b].astype(F32).T for b in range(3)], axis=1
        ).astype(BF)
    ow_q[...] = jnp.concatenate([ow[p] for p in range(outer)], axis=1)
    step = 512
    for k in range(outer * ch // step):
        ow_t[k * step : (k + 1) * step, :] = ow_q[:, k * step : (k + 1) * step].astype(F32).T.astype(BF)

    def p_widen():
        for k in range(nchunk):
            cot_in[k].wait()

        @pl.loop(0, ch, unroll=8)
        def _(c):
            at = pl.multiple_of(c * pitch, 8)
            wide[pl.ds(at, ti), :] = cot_n[c].astype(F32)

    p_widen()

    lane = lax.broadcasted_iota(jnp.int32, (ch, 128), 1)
    window = lax.rem(lane + 4, 128) // 8

    first_four = lax.rem(lane, 8) < 4
    kt = kg // 2

    def to_rows(dst, first, which, read):
        @pl.loop(0, kt, unroll=min(4, kt))
        def _(t):
            lines = []
            for k in range(2):
                packed = None
                for m in range(PACK):
                    row_at = 2 * PACK * t + PACK * k + m
                    x = read(row_at).astype(BF)
                    dst[first + row_at] = x
                    packed = x if m == 0 else jnp.where(window == m, pltpu.roll(x, 8 * m, 1), packed)
                lines.append(packed)
            moved = pltpu.roll(lines[1], 4, 1)
            packs[which, 0, t] = jnp.where(first_four, lines[0], moved)
            packs[which, 1, t] = jnp.where(first_four, moved, lines[0])

    def halo_moves(src, first, which):
        low, high = packs.at[which, 0], packs.at[which, 1]
        from_west, from_east = land_col.at[which, 0], land_col.at[which, 1]
        plan = [
            (src.at[pl.ds(first, 4)], land_row.at[which, 1], (up, col)),
            (src.at[pl.ds(first + ti - 4, 4)], land_row.at[which, 0], (down, col)),
            (low, from_east.at[pl.ds(1, kt)], (row, west)),
            (high, from_west.at[pl.ds(1, kt)], (row, east)),
            (low.at[0], from_east.at[kt + 1], (up, west)),
            (high.at[0], from_west.at[kt + 1], (up, east)),
            (low.at[kt - 1], from_east.at[0], (down, west)),
            (high.at[kt - 1], from_west.at[0], (down, east)),
        ]
        return [
            remote(s, d, h_send.at[which, min(m // 2, 1)], h_recv.at[which, min(m // 2, 1)], dev)
            for m, (s, d, dev) in enumerate(plan)
        ]

    to_rows(cot_t, 4, 0, lambda i: wide[pl.ds(i, ch, stride=pitch), :])
    cot_moves = halo_moves(cot_t, 4, 0)
    if comm:
        for move in cot_moves:
            move.start()

    if comm:
        drain(left_in.at[pl.ds(0, nc - 1)], f_recv.at[0])
        drain(right_in, f_recv.at[1])
    left[...] = left_in[...].reshape(nc * own, 128)[:, :outer]
    left_t[...] = left[...].astype(F32).T.astype(BF)
    right = right_in[...].reshape(nr * own, 128)[:, outer : 2 * outer]
    for k in range(outer * ch // step):
        rows = dot(ow_t[k * step : (k + 1) * step, :], right, NT).astype(BF).astype(F32)
        for m in range(step // ch):
            at = (k * (step // ch) + m) * wch
            mixf[at : at + ch, :] = rows[m * ch : (m + 1) * ch]

    @pl.loop(0, ch, unroll=8)
    def _(c):
        mix[c] = mixf[pl.ds(c, outer, stride=wch), :].astype(BF)

    pm_in.wait()

    def p_hidden():
        def update(c):
            return dot(left[...], jnp.concatenate([mix[c], mix[c + 1]], axis=1))

        def finish(c, change):
            for k in range(2):
                hidden = (hid_n[c + k].astype(F32) + change[:, 128 * k : 128 * (k + 1)]).astype(BF)
                hid_n[c + k] = hidden
                h = hidden.astype(F32)
                e = jnp.minimum(jnp.exp(h), 1.0)
                slope_n[c + k] = e.astype(BF)
                wide[pl.ds(c + k, ti, stride=wch), :] = jnp.maximum(h, e - 1.0)

        @pl.loop(0, ch, step=16)
        def _(c):
            changes = [update(c + 2 * k) for k in range(8)]
            for k in range(8):
                finish(c + 2 * k, changes[k])

    p_hidden()

    to_rows(act_t, 8, 1, lambda i: wide[pl.ds(pl.multiple_of(i * wch, 8), ch), :])
    for s in (0, 4, ti + 8, ti + 12):
        act_t[s : s + 4] = jnp.zeros((4, ch, 128), BF)
    act_moves = halo_moves(act_t, 8, 1)
    if comm:
        for move in act_moves:
            move.start()

    has_up, has_down, has_west, has_east = row > 0, row < nr - 1, col > 0, col < nc - 1

    def keep(ok, x):
        return jnp.where(ok, x, jnp.zeros_like(x))

    def unpack_edges(dst, first, which):
        dst[first : first + 4] = keep(has_up, land_row[which, 0])
        dst[first + ti + 4 : first + ti + 8] = keep(has_down, land_row[which, 1])

        def place(t, ok):
            from_west = keep(jnp.logical_and(ok, has_west), land_col[which, 0, t])
            from_east = keep(jnp.logical_and(ok, has_east), land_col[which, 1, t])
            return (
                jnp.where(first_four, pltpu.roll(from_west, 4, 1), pltpu.roll(from_east, 124, 1)),
                jnp.where(first_four, from_west, pltpu.roll(from_east, 120, 1)),
            )

        hx[0] = place(0, has_up)[1]
        hx[kg + 1] = place(kt + 1, has_down)[0]

        @pl.loop(1, kt + 1, unroll=min(4, kt))
        def _(t):
            hx[2 * t - 1], hx[2 * t] = place(t, True)

    def fill(dst, src, first, n, q, turned):
        for r in range(8):
            x = src[first + 16 * n + q + r]
            at = q + r + PACK - 4
            edge = pltpu.roll(hx[n + at // PACK], (PACK - at % PACK) % PACK * 8, 1)
            before = jnp.where(lane < 4, edge, pltpu.roll(x, 4, 1))
            after = jnp.where(lane >= 124, edge, pltpu.roll(x, 124, 1))
            lanes = slice(128 * r, 128 * (r + 1))
            dst[:ch, lanes] = after if turned else before
            dst[ch : 2 * ch, lanes] = x
            dst[2 * ch :, lanes] = before if turned else after

    def halves(x):
        return [x[:, :512], x[:, 512:]]

    def spread(parts, g, order):
        for s in range(len(parts) + 2):
            terms = [
                parts[s - k][a * ch : (a + 1) * ch]
                for k, a in enumerate(order)
                if 0 <= s - k < len(parts)
            ]
            total = terms[0]
            for term in terms[1:]:
                total = total + term
            for r in range(4):
                at = pl.ds(pl.multiple_of((4 * (g + s) + r) * wch, 8), ch)
                term = total[:, 128 * r : 128 * (r + 1)]
                gt[at, :] = gt[at, :] + term if s < 2 else term

    if comm:
        drain(land_row.at[0], h_recv.at[0, 0])
        drain(land_col.at[0], h_recv.at[0, 1])
    unpack_edges(cot_t, 0, 0)
    gt[: 8 * wch] = jnp.zeros((8 * wch, 128), F32)
    wg_acc[...] = jnp.zeros_like(wg_acc)

    def p_kernel():
        fill(terms.at[0], cot_t, 0, 0, 0, True)

        def acts(first):
            return jnp.concatenate(
                [
                    jnp.concatenate([act_t[first + 4 * a + r] for r in range(8)], axis=1)
                    for a in range(3)
                ],
                axis=0,
            )

        @pl.loop(0, ti // 16, step=STEP)
        def _(n):
            grad = 0
            for m in range(n_chunks):
                j = 2 * n + m
                grad = grad + dot(terms[j], acts(8 * j), NT)
                fill(terms.at[j + 1], cot_t, 0, n + (m + 1) // 2, 8 * ((m + 1) % 2), True)
            wg_acc[...] += grad

        wg_acc[...] += dot(terms[ti // 8], acts(ti), NT)

    def p_back():
        @pl.loop(0, ti // 16, step=STEP)
        def _(n):
            parts = []
            for m in range(n_chunks):
                parts += halves(dot(wb[...], terms[2 * n + m]))
            spread(parts, 4 * n, (0, 1, 2))

        spread(halves(dot(wb[...], terms[ti // 8])), ng, (0, 1, 2))

    n_chunks = 2 * STEP
    p_kernel()

    taps = 9
    owners = [min(2 * k, nc - 1) for k in range(taps)]
    is_owner = functools.reduce(jnp.logical_or, [col == c for c in owners])
    mine = jnp.where(col == owners[-1], taps - 1, col // 2)
    half = ch // 2
    for k in range(taps):
        a, b = k // 3, k % 3
        tap = wg_acc[b * ch : (b + 1) * ch, a * ch : (a + 1) * ch]
        wgs[k] = jnp.concatenate([tap[:half], tap[half:]], axis=1).astype(BF)
    for k, c in enumerate(owners):
        move = remote(wgs.at[k], land_a.at[col], w_send.at[0], w_recv.at[0], (row, c))

        @pl.when(col == c)
        def _():
            land_a[col] = wgs[k]

        if comm:

            @pl.when(col != c)
            def _():
                move.start()


    p_back()

    def each(refs):
        total = refs[0].astype(F32)
        for k in range(1, refs.shape[0]):
            total = total + refs[k].astype(F32)
        return total

    @pl.when(is_owner)
    def _():
        if comm:
            drain(land_a.at[pl.ds(0, nc - 1)], w_recv.at[0])
        land_b[row] = each(land_a)
        if comm:
            for d in range(1, nr):
                to = (lax.rem(row + d, nr), col)
                remote(land_b.at[row], land_b.at[row], w_send.at[1], w_recv.at[1], to).start()

    lg_acc[...] = jnp.zeros_like(lg_acc)

    def p_grad():
        @pl.loop(0, ch, step=16)
        def _(c):
            lg = 0
            for half in (c, c + 4, c + 8, c + 12):
                grads = []
                for m in range(4):
                    g = gt[pl.ds(8 * wch + half + m, ti, stride=wch), :]
                    pg = (cot_n[half + m].astype(F32) + g * slope_n[half + m].astype(F32)).astype(BF)
                    cot_n[half + m] = pg
                    grads.append(pg)
                grads = jnp.concatenate(grads, axis=1)
                mixes = jnp.concatenate([mix[half + m] for m in range(4)], axis=1)
                lg = lg + dot(mixes, grads, NT)
                mg = dot(left_t[...], grads)
                for m in range(4):
                    mgf[pl.ds(half + m, outer, stride=wch), :] = mg[:, 128 * m : 128 * (m + 1)]
            lg_acc[...] += lg

    p_grad()

    mg = jnp.concatenate([mgf[p * wch : p * wch + ch, :] for p in range(outer)], axis=0)
    rg = dot(ow_q[...], mg.astype(BF)).T
    rg_out[...] = rg.reshape(nr, own, outer)
    lg_out[...] = lg_acc[...].T.reshape(nc, own, outer)
    land_l[col] = lg_out[col]
    if comm:
        for d in range(1, nc):
            other = lax.rem(col + d, nc)
            remote(
                lg_out.at[other], land_l.at[col], g_send.at[0], g_recv.at[0], (row, other)
            ).start()
        for k in range(nr):
            r, c = source(k)
            me = jnp.logical_and(r == row, c == col)
            far = remote(rg_out.at[k], land_r.at[row], g_send.at[1], g_recv.at[1], (r, c))
            near = pltpu.make_async_copy(rg_out.at[k], land_r.at[row], g_recv.at[1])

            @pl.when(me)
            def _():
                near.start()

            @pl.when(jnp.logical_not(me))
            def _():
                far.start()

    @pl.when(is_owner)
    def _():
        if comm:
            drain(land_b.at[pl.ds(0, nr - 1)], w_recv.at[1])
        fin[mine] = (each(land_b) * (1.0 / residues)).astype(BF)
        if comm:
            for d in range(1, nc):
                to = (row, lax.rem(col + d, nc))
                remote(fin.at[mine], fin.at[mine], w_send.at[2], w_recv.at[2], to).start()

    if comm:
        drain(land_row.at[1], h_recv.at[1, 0])
        drain(land_col.at[1], h_recv.at[1, 1])
    unpack_edges(act_t, 4, 1)
    gt[: 8 * wch] = jnp.zeros((8 * wch, 128), F32)

    fill(even, act_t, 4, 0, 0, False)

    def p_forward(first, last):
        @pl.loop(first, last, step=STEP)
        def _(n):
            parts = []
            for m in range(STEP):
                parts += halves(dot(wf[...], even[...]))
                fill(odd, act_t, 4, n + m, 8, False)
                parts += halves(dot(wf[...], odd[...]))
                fill(even, act_t, 4, n + m, 16, False)
            spread(parts, 4 * n, (2, 1, 0))

    p_forward(0, ti // 16)
    spread(halves(dot(wf[...], even[...])), ng, (2, 1, 0))

    if comm:
        drain(land_l.at[pl.ds(0, nc - 1)], g_recv.at[0])
        drain(land_r, g_recv.at[1])
    lg = land_l[0]
    for k in range(1, nc):
        lg = lg + land_l[k]
    rg = land_r[0]
    for k in range(1, nr):
        rg = rg + land_r[k]

    def exact(x, w):
        total = jnp.zeros((own, w.shape[1]), F32)
        for _ in range(3):
            head = x.astype(BF)
            total = total + dot(head, w)
            x = x - head.astype(F32)
        return total

    fg_out[...] = (exact(lg, lw[...]) + exact(rg, rw[...])) * (1.0 / math.sqrt(residues))

    if comm:
        drain_some(fin, w_recv.at[2], is_owner)
    for k in range(taps):
        tap = fin[k].astype(F32)
        wg_out[k] = jnp.concatenate([tap[:, :ch], tap[:, ch:]], axis=0)

    if comm:
        drain(left_in.at[pl.ds(0, nc - 1)], f_send.at[0])
        drain_some(right_in, f_send.at[1], goal == col)
        for which in range(2):
            drain(land_row.at[which], h_send.at[which, 0])
            drain(land_col.at[which], h_send.at[which, 1])
        drain_some(wgs, w_send.at[0], is_owner)
        drain(land_l.at[pl.ds(0, nc - 1)], g_send.at[0])
        drain_some(land_r, g_send.at[1], goal == col)

        @pl.when(is_owner)
        def _():
            drain(land_b.at[pl.ds(0, nr - 1)], w_send.at[1])
            drain(land_a.at[pl.ds(0, nc - 1)], w_send.at[2])


def last_kernel(
    hid_n, pg_n, gt, wg_in, fg_in, bias, po_hbm, pg_hbm, wg_hbm, fg_hbm, out_n, out_sem
):
    ch, ti, _ = hid_n.shape
    wch = ch + 8
    step = ch // 4
    copies = [
        pltpu.make_async_copy(
            pg_n.at[pl.ds(k * step, step)], pg_hbm.at[pl.ds(k * step, step)], out_sem.at[k]
        )
        for k in range(4)
    ]
    copies.append(pltpu.make_async_copy(wg_in, wg_hbm, out_sem.at[4]))
    copies.append(pltpu.make_async_copy(fg_in, fg_hbm, out_sem.at[5]))
    for copy in copies:
        copy.start()
    for k in range(ti // BLOCK):

        @pl.loop(0, ch, unroll=16)
        def _(c):
            conv = gt[pl.ds((8 + BLOCK * k) * wch + c, BLOCK, stride=wch), :]
            h = hid_n[c, pl.ds(BLOCK * k, BLOCK), :].astype(F32)
            out_n[c, pl.ds(BLOCK * k, BLOCK), :] = (h + bias[c] + conv).astype(BF)

        copy = pltpu.make_async_copy(
            out_n.at[:, pl.ds(BLOCK * k, BLOCK)], po_hbm.at[:, pl.ds(BLOCK * k, BLOCK)],
            out_sem.at[6 + k],
        )
        copy.start()
        copies.append(copy)
    for copy in copies:
        copy.wait()


def call(nr, nc, residues, comm, pair_map, features, lw, rw, ow, cw, bias, cot):
    ch, ti, tj = pair_map.shape
    own, feat = features.shape
    outer = lw.shape[1]
    kg = ti // PACK
    any_spec = pl.BlockSpec(memory_space=pl.ANY)
    vmem = pl.BlockSpec(memory_space=pltpu.VMEM)
    smem = pl.BlockSpec(memory_space=pltpu.SMEM)
    V = pltpu.VMEM
    dma = pltpu.SemaphoreType.DMA
    scratch = [
        V((ch, ti, tj), BF),
        V((max(ch * (ti + 8), ti * (ch + 8)), 128), F32),
        V((ti + 8, ch, 128), BF),
        V((ti + 16, ch, 128), BF),
        V((kg + 2, ch, 128), BF),
        V((ti // 8 + 1, 3 * ch, 1024), BF),
        V((3 * ch, 1024), BF),
        V((3 * ch, 1024), BF),
        V((2, 2, kg // 2, ch, 128), BF),
        V((2, 2, 4, ch, 128), BF),
        V((2, 2, kg // 2 + 2, ch, 128), BF),
        V((own, 128), BF),
        V((nc, own, 128), BF),
        V((nr, own, 128), BF),
        V((ti, outer), BF),
        V((outer, ti), BF),
        V((outer * (ch + 8), 128), F32),
        V((ch, outer, 128), BF),
        V((3 * ch, 3 * ch), BF),
        V((3 * ch, 3 * ch), BF),
        V((outer, outer * ch), BF),
        V((outer * ch, outer), BF),
        V((outer * (ch + 8), 128), F32),
        V((3 * ch, 3 * ch), F32),
        V((9, ch // 2, 2 * ch), BF),
        V((nc, ch // 2, 2 * ch), BF),
        V((nr, ch // 2, 2 * ch), F32),
        V((9, ch // 2, 2 * ch), BF),
        V((outer, ti), F32),
        V((nc, own, outer), F32),
        V((nr, own, outer), F32),
        V((nc, own, outer), F32),
        V((nr, own, outer), F32),
        dma((ch // 8 + 1,)),
        dma((2,)),
        dma((2,)),
        dma((2, 2)),
        dma((2, 2)),
        dma((3,)),
        dma((3,)),
        dma((2,)),
        dma((2,)),
    ]
    macs = ti * tj * (27 * ch * ch + 3 * outer * ch)
    out = pl.pallas_call(
        functools.partial(kernel, nr, nc, ch, ti, outer, comm, residues),
        out_shape=[
            V((ch, ti, tj), BF),
            V((ch, ti, tj), BF),
            V(((ti + 20) * (ch + 8), 128), F32),
            V((9, ch, ch), F32),
            V((own, feat), F32),
        ],
        in_specs=[any_spec, any_spec] + [vmem] * 5,
        out_specs=[vmem] * 5,
        scratch_shapes=scratch,
        compiler_params=pltpu.CompilerParams(
            collective_id=0 if comm else None,
            has_side_effects=True,
            vmem_limit_bytes=44 * 1024 * 1024,
        ),
        cost_estimate=pl.CostEstimate(
            flops=2 * macs, bytes_accessed=8 * ch * ti * tj, transcendentals=2 * ch * ti * tj
        ),
    )(cot, pair_map, features, lw.T, rw.T, ow, cw.reshape(9, ch, ch))
    kept = [pltpu.with_memory_space_constraint(x, pltpu.VMEM) for x in out]
    po, pg, wg, fg = pl.pallas_call(
        last_kernel,
        out_shape=[
            jax.ShapeDtypeStruct((ch, ti, tj), BF),
            jax.ShapeDtypeStruct((ch, ti, tj), BF),
            jax.ShapeDtypeStruct((9, ch, ch), F32),
            jax.ShapeDtypeStruct((own, feat), F32),
        ],
        in_specs=[vmem] * 5 + [smem],
        out_specs=[any_spec] * 4,
        scratch_shapes=[V((ch, ti, tj), BF), dma((6 + ti // BLOCK,))],
        compiler_params=pltpu.CompilerParams(vmem_limit_bytes=24 * 1024 * 1024),
        cost_estimate=pl.CostEstimate(
            flops=2 * ch * ti * tj, bytes_accessed=4 * ch * ti * tj, transcendentals=0
        ),
    )(*kept, bias)
    return po, pg, wg.reshape(3, 3, ch, ch), fg


def solution(mesh):
    nr, nc = mesh.shape["row"], mesh.shape["col"]

    def shards(pair_map, features, lw, rw, ow, cw, bias, cot):
        return call(
            nr, nc, pair_map.shape[1] * nr, True, pair_map, features, lw, rw, ow, cw, bias, cot
        )

    in_specs = (
        P(None, "row", "col"),
        P(("row", "col"), None),
        P(),
        P(),
        P(),
        P(),
        P(),
        P(None, "row", "col"),
    )
    out_specs = (P(None, "row", "col"), P(None, "row", "col"), P(), P(("row", "col"), None))
    return jax.shard_map(shards, mesh=mesh, in_specs=in_specs, out_specs=out_specs, check_vma=False)
```
